32 devices in a mesh: expert: 8 (over y, x, core), tensor: 4 (over z).
Axes of the slice: x: 2, y: 2, z: 4, core: 2. Of those that a mesh axis runs over, the one named last changes fastest.
Arguments:
- tokens: bfloat16 [8192, 2048], P('expert'), may hold values from -6 to 6
- cotangent: bfloat16 [8192, 2048], P('expert'), may hold values from -6 to 6
- seq_lengths: int32 [32], P('expert'), may hold values from 0 to 1024, as said below
- expert_ids: int32 [8192, 8], P('expert'), may hold values from 0 to 15, as said below
- slot_index: int32 [8192, 8], P('expert'), may hold values from -1 to 383, as said below
- w_query: bfloat16 [2048, 2048], P(None, 'tensor'), may hold values from -0.125 to 0.125
- w_key: bfloat16 [2048, 2048], P(None, 'tensor'), may hold values from -0.125 to 0.125
- w_value: bfloat16 [2048, 2048], P(None, 'tensor'), may hold values from -0.125 to 0.125
- w_output: bfloat16 [2048, 2048], P('tensor'), may hold values from -0.75 to 0.75
- query_gain: float32 [2048], P('tensor'), may hold values from 0.5 to 1.5
- key_gain: float32 [2048], P('tensor'), may hold values from 0.5 to 1.5
- attn_gain: float32 [2048], replicated, may hold values from 0.5 to 1.5
- moe_gain: float32 [2048], replicated, may hold values from 0.5 to 1.5
- router: bfloat16 [2048, 16], replicated, may hold values from -0.06591797 to 0.06591797
- w_gate: bfloat16 [16, 2048, 1024], P('expert', None, 'tensor'), may hold values from -0.125 to 0.125
- w_up: bfloat16 [16, 2048, 1024], P('expert', None, 'tensor'), may hold values from -0.125 to 0.125
- w_down: bfloat16 [16, 1024, 2048], P('expert', 'tensor'), may hold values from -12 to 12
Outputs:
- out: bfloat16 [8192, 2048], P('expert')
- grad_input: bfloat16 [8192, 2048], P('expert')
- grad_w_query: bfloat16 [2048, 2048], P('expert', 'tensor')
- grad_w_key: bfloat16 [2048, 2048], P('expert', 'tensor')
- grad_w_value: bfloat16 [2048, 2048], P('expert', 'tensor')
- grad_w_output: bfloat16 [2048, 2048], P('tensor', 'expert')
- grad_query_gain: bfloat16 [2048], P(('tensor', 'expert'))
- grad_key_gain: bfloat16 [2048], P(('tensor', 'expert'))
- grad_attn_gain: bfloat16 [2048], P('expert')
- grad_moe_gain: bfloat16 [2048], P('expert')
- grad_router: bfloat16 [2048, 16], P('expert')
- grad_w_gate: bfloat16 [16, 2048, 1024], P('expert', None, 'tensor')
- grad_w_up: bfloat16 [16, 2048, 1024], P('expert', None, 'tensor')
- grad_w_down: bfloat16 [16, 1024, 2048], P('expert', 'tensor')
The draws below stay inside these ranges and needn't reach their ends.
Inputs may be any that keep to these rules, and one draw needn't show every extreme that they name: `seq_lengths`: each group's 4 lengths fill its first rows in order and sum to 512 or more; some group holds a single sequence of 1024 rows. `expert_ids`: the 8 experts of a token differ. `slot_index`: -1 marks a choice that is not carried (every choice of a padding row, and some others). The carried choices of one group that name one expert hold distinct slots. One expert receives 384 rows from every group.
All inputs are finite; a program needn't handle non-finite values.
Results may differ from the reference program's by a relative error of at most 0.03.
Values may be sent and summed in bfloat16 or wider, within the bound.
No kernel may reach another device: no remote copies, remote signals or barrier semaphores. Data moves between devices by JAX's collectives and lax.ppermute only.
A program may use at most 384 MiB of HBM per device.

```python
import jax
import jax.numpy as jnp
from jax import lax

D = 2048
HEADS = 16
HEAD_DIM = 128
EXP_HID = 1024
TOP = 8
TOK_DEV = 1024
SEQ_DEV = 4
EXPERTS = 16
TOKENS = 8192
CAP = 384
N_TENSOR = 4


def routing_tables(key):
    groups = TOKENS // TOK_DEV
    count = TOK_DEV * TOP
    keys = jax.random.split(key, 7)
    totals = jax.random.randint(keys[0], (groups,), TOK_DEV // 2, TOK_DEV + 1)
    cuts = jax.random.randint(keys[1], (groups, SEQ_DEV - 1), 0, 2 ** 20)
    cuts = jnp.sort(cuts * totals[:, None] // 2 ** 20, axis=1)
    edges = jnp.concatenate([jnp.zeros((groups, 1), jnp.int32), cuts, totals[:, None]], axis=1)
    lengths = edges[:, 1:] - edges[:, :-1]
    full_group = jax.random.randint(keys[2], (), 0, groups)
    single = (jnp.arange(SEQ_DEV) == 0).astype(jnp.int32) * TOK_DEV
    lengths = jnp.where((jnp.arange(groups) == full_group)[:, None], single[None, :], lengths)
    totals = jnp.sum(lengths, axis=1)
    noise = jax.random.randint(keys[3], (TOKENS, EXPERTS), 0, 2 ** 20)
    favour = jax.random.randint(keys[4], (EXPERTS,), 0, 2 ** 20)
    favoured = jax.random.randint(keys[5], (), 0, EXPERTS)
    favour = jnp.where(jnp.arange(EXPERTS) == favoured, 2 ** 21, favour)
    scores = (noise + favour[None, :]) * EXPERTS + jnp.arange(EXPERTS)[None, :]
    expert_ids = lax.top_k(scores, TOP)[1].astype(jnp.int32)
    flat_ids = expert_ids.reshape(groups, count)
    alive = jnp.repeat(jnp.arange(TOK_DEV)[None, :] < totals[:, None], TOP, axis=1)
    target = jnp.where(alive, flat_ids, EXPERTS)
    priority = jax.vmap(lambda part_key: jax.random.permutation(part_key, count))(jax.random.split(keys[6], groups))
    order = jnp.argsort(target * count + priority, axis=1, stable=True)
    sorted_target = jnp.take_along_axis(target, order, axis=1)
    counts = jnp.sum((target[:, :, None] == jnp.arange(EXPERTS + 1)[None, None, :]).astype(jnp.int32), axis=1)
    starts = jnp.cumsum(counts, axis=1) - counts
    ranks_sorted = jnp.arange(count)[None, :] - jnp.take_along_axis(starts, sorted_target, axis=1)
    ranks = jax.vmap(lambda place, value: jnp.zeros((count,), jnp.int32).at[place].set(value))(order, ranks_sorted)
    slots = jnp.where(alive & (ranks < CAP), ranks, -1).reshape(TOKENS, TOP)
    return (lengths.reshape(-1).astype(jnp.int32), expert_ids, slots.astype(jnp.int32))


def draw_seq_lengths(key, part):
    tables = routing_tables(key)
    return tables[0]


def draw_expert_ids(key, part):
    tables = routing_tables(key)
    return tables[1]


def draw_slot_index(key, part):
    tables = routing_tables(key)
    return tables[2]


def level_of(own_key, extent, cuts, smallest, top_value):
    factor_of, own = 1.0, jax.random.fold_in(own_key, 6)
    for dim, shards_of in cuts:
        steps = jnp.exp(jax.random.uniform(jax.random.fold_in(own, dim), (shards_of,), jnp.float32, smallest / len(cuts), top_value / len(cuts)))
        factor_of = factor_of * jnp.repeat(steps, extent[dim] // shards_of).reshape([-1 if axis == dim else 1 for axis in range(len(extent))])
    return factor_of


def scatter_about(stream_key, extent, width, limit, pieces=(), kind=jnp.bfloat16):
    entries = width * jax.random.normal(stream_key, extent, jnp.float32)
    if pieces:
        entries = entries * level_of(stream_key, extent, pieces, -0.22, 0.18)
    return jnp.clip(entries, -limit, limit).astype(kind)


def setup_inputs(seed: int = 0) -> dict:
    streams_of = jax.random.split(jax.random.key(seed), 18)
    tokens = scatter_about(streams_of[0], (TOKENS, D), 1.0, 6.0, ((0, 8),))
    cotangent = scatter_about(streams_of[1], (TOKENS, D), 1.0, 6.0, ((0, 8),))
    seq_lengths = draw_seq_lengths(jax.random.fold_in(streams_of[17], 71), 0)
    expert_ids = draw_expert_ids(jax.random.fold_in(streams_of[17], 71), 0)
    slot_index = draw_slot_index(jax.random.fold_in(streams_of[17], 71), 0)
    w_query = scatter_about(streams_of[5], (D, D), D ** -0.5, 0.125, ((1, 4),))
    w_key = scatter_about(streams_of[6], (D, D), D ** -0.5, 0.125, ((1, 4),))
    w_value = scatter_about(streams_of[7], (D, D), D ** -0.5, 0.125, ((1, 4),))
    w_output = scatter_about(streams_of[8], (D, D), (D // 32) ** -0.5, 0.75, ((0, 4),))
    query_gain = jnp.clip(1.0 + 0.1 * jax.random.normal(streams_of[9], (D,), jnp.float32), 0.5, 1.5)
    key_gain = jnp.clip(1.0 + 0.1 * jax.random.normal(streams_of[10], (D,), jnp.float32), 0.5, 1.5)
    attn_gain = jnp.clip(1.0 + 0.1 * jax.random.normal(streams_of[11], (D,), jnp.float32), 0.5, 1.5)
    moe_gain = jnp.clip(1.0 + 0.1 * jax.random.normal(streams_of[12], (D,), jnp.float32), 0.5, 1.5)
    router = scatter_about(streams_of[13], (D, EXPERTS), 0.011, 0.06591797)
    w_gate = scatter_about(streams_of[14], (EXPERTS, D, EXP_HID), D ** -0.5, 0.125, ((0, 8), (2, 4)))
    w_up = scatter_about(streams_of[15], (EXPERTS, D, EXP_HID), D ** -0.5, 0.125, ((0, 8), (2, 4)))
    w_down = scatter_about(streams_of[16], (EXPERTS, EXP_HID, D), (EXPERTS // TOP), 12.0, ((0, 8), (1, 4)))
    return {"tokens": tokens, "cotangent": cotangent, "seq_lengths": seq_lengths, "expert_ids": expert_ids, "slot_index": slot_index, "w_query": w_query, "w_key": w_key, "w_value": w_value, "w_output": w_output, "query_gain": query_gain, "key_gain": key_gain, "attn_gain": attn_gain, "moe_gain": moe_gain, "router": router, "w_gate": w_gate, "w_up": w_up, "w_down": w_down}


EPS = 1e-05
THETA = 10000.0
NEG = -1e+30

@jax.custom_vjp
def low(v):
    return lax.optimization_barrier(v.astype(jnp.bfloat16)).astype(jnp.float32)

@jax.custom_vjp
def low_back(v):
    return v

def low_keep(v):
    return (low(v), None)

def low_pass(kept, grad):
    return (grad,)

def back_keep(v):
    return (v, None)

def back_low(kept, grad):
    return (low(grad),)
low.defvjp(low_keep, low_pass)
low_back.defvjp(back_keep, back_low)

def wide_dot(left, right):
    return jnp.dot(left, right, precision=lax.Precision.HIGHEST, preferred_element_type=jnp.float32)

def norm_rows(values, gain):
    return values * lax.rsqrt(lax.optimization_barrier(jnp.mean(values * values, axis=-1, keepdims=True)) + EPS) * gain

def layout(lengths, rows):
    ends = jnp.cumsum(lengths, axis=-1)
    starts = ends - lengths
    places = jnp.arange(rows, dtype=jnp.int32)
    inside = ((places[..., :, None] >= starts[..., None, :]) & (places[..., :, None] < ends[..., None, :])).astype(jnp.int32)
    number = jnp.arange(lengths.shape[-1], dtype=jnp.int32)
    alive = lax.optimization_barrier(jnp.sum(inside, axis=-1))
    segment = lax.optimization_barrier(jnp.sum(inside * number, axis=-1)) + (1 - alive) * (lengths.shape[-1] + places)
    position = lax.optimization_barrier(jnp.sum(inside * (places[..., :, None] - starts[..., None, :]), axis=-1))
    return (segment.astype(jnp.int32), position.astype(jnp.int32))

def rope_angles(position, head_size):
    half = head_size // 2
    freq = THETA ** (-2.0 * jnp.arange(half, dtype=jnp.float32) / head_size)
    angle = position.astype(jnp.float32)[..., None] * freq
    return (jnp.cos(angle), jnp.sin(angle))

def rotate(values, cosine, sine):
    half = values.shape[-1] // 2
    first, second = (values[..., :half], values[..., half:])
    cos_here = cosine[..., None, :]
    sin_here = sine[..., None, :]
    return jnp.concatenate([first * cos_here - second * sin_here, second * cos_here + first * sin_here], axis=-1)

def attend_group(queries, keys, values, segment):
    rows = queries.shape[0]
    scores = jnp.einsum('qhd,khd->hqk', queries, keys, precision=lax.Precision.HIGHEST) * HEAD_DIM ** (-0.5)
    scores = low_back(scores)
    places = jnp.arange(rows, dtype=jnp.int32)
    allowed = (segment[:, None] == segment[None, :]) & (places[None, :] <= places[:, None])
    scores = jnp.where(allowed[None], scores, NEG)
    weights = low(jax.nn.softmax(scores, axis=-1))
    return low_back(jnp.einsum('hqk,khd->qhd', weights, values, precision=lax.Precision.HIGHEST))

def reference(tokens, cotangent, seq_lengths, expert_ids, slot_index, w_query, w_key, w_value, w_output, query_gain, key_gain, attn_gain, moe_gain, router, w_gate, w_up, w_down):
    groups = TOKENS // TOK_DEV
    segment, position = layout(seq_lengths.reshape(groups, SEQ_DEV), TOK_DEV)
    cosine, sine = rope_angles(position, HEAD_DIM)
    kept = slot_index >= 0
    source = (jnp.arange(TOKENS, dtype=jnp.int32) // TOK_DEV)[:, None]
    block_rows = groups * CAP
    target_slot = jnp.where(kept, expert_ids * block_rows + source * CAP + slot_index, EXPERTS * block_rows).reshape(-1)
    token_of = jnp.full((EXPERTS * block_rows,), -1, jnp.int32).at[target_slot].set(jnp.repeat(jnp.arange(TOKENS, dtype=jnp.int32), TOP), mode='drop')
    filled = (token_of >= 0).reshape(EXPERTS, block_rows)
    picks = jnp.maximum(token_of, 0).reshape(EXPERTS, block_rows)
    hid_width = EXP_HID // N_TENSOR
    shape_heads = (groups, TOK_DEV, HEADS, HEAD_DIM)

    def forward(params):
        inputs, wq, wk, wv, wo, gq, gk, g_attn, g_moe, w_router, wg, wu, wd = params
        attn_in = low(norm_rows(inputs, g_attn))
        query_raw = low_back(wide_dot(attn_in, wq))
        key_raw = low_back(wide_dot(attn_in, wk))
        value_raw = low_back(wide_dot(attn_in, wv))
        queries = low(rotate(norm_rows(query_raw, gq).reshape(shape_heads), cosine, sine))
        keys = low(rotate(norm_rows(key_raw, gk).reshape(shape_heads), cosine, sine))
        values = low(value_raw.reshape(shape_heads))
        context = lax.map(jax.checkpoint(lambda item: attend_group(*item)), (queries, keys, values, segment))
        context_low = low(context.reshape(TOKENS, D))
        hidden_in = inputs + low_back(wide_dot(context_low, wo))
        moe_in = norm_rows(hidden_in, g_moe)
        shares = jax.nn.softmax(wide_dot(moe_in, w_router), axis=-1)
        gates = jnp.take_along_axis(shares, expert_ids, axis=1)
        moe_low = low(moe_in)

        def expert_block(item):
            chosen_rows, alive, wg_e, wu_e, wd_e = item
            rows_in = jnp.where(alive[:, None], moe_low[chosen_rows], 0.0)
            total = jnp.zeros((rows_in.shape[0], D), jnp.float32)
            for part in range(N_TENSOR):
                columns = slice(part * hid_width, (part + 1) * hid_width)
                piece = low_back(rows_in)
                gate_pre = low_back(wide_dot(piece, wg_e[:, columns]))
                up_pre = low_back(wide_dot(piece, wu_e[:, columns]))
                hidden = low(jax.nn.silu(gate_pre) * up_pre)
                total = total + low(low_back(wide_dot(hidden, wd_e[columns, :])))
            return total
        expert_out = lax.map(jax.checkpoint(expert_block), (picks, filled, wg, wu, wd))
        flat_out = expert_out.reshape(EXPERTS * block_rows, D)
        gate_of = jnp.zeros((EXPERTS * block_rows,), jnp.float32).at[target_slot].set(gates.reshape(-1), mode='drop')
        moe = jax.ops.segment_sum(flat_out * gate_of[:, None], jnp.maximum(token_of, 0), num_segments=TOKENS)
        return hidden_in + moe
    params = tuple((item.astype(jnp.float32) for item in (tokens, w_query, w_key, w_value, w_output, query_gain, key_gain, attn_gain, moe_gain, router, w_gate, w_up, w_down)))
    result, pullback = jax.vjp(forward, params)
    grads, = pullback(cotangent.astype(jnp.float32))
    lows = tuple((item.astype(jnp.bfloat16) for item in grads[1:]))
    return (result.astype(jnp.bfloat16), grads[0].astype(jnp.bfloat16), lows[0], lows[1], lows[2], lows[3], lows[4], lows[5], lows[6], lows[7], lows[8], lows[9], lows[10], lows[11])
```

```python
import functools

import jax
import jax.numpy as jnp
from jax import lax
from jax.experimental import pallas as pl
from jax.experimental.pallas import tpu as pltpu
from jax.sharding import PartitionSpec as P

HEAD_DIM = 128
TOP = 8


EPS = 1e-05
THETA = 10000.0
NEG = -1e30


def norm_rows(values, gain):
    inverse = lax.rsqrt(jnp.mean(values * values, axis=-1, keepdims=True) + EPS)
    return (values * inverse * gain, inverse)


def norm_back(values, inverse, gain, upstream):
    scaled = upstream * gain
    inner = jnp.mean(values * scaled, axis=-1, keepdims=True)
    grad_values = inverse * scaled - values * inverse * inverse * inverse * inner
    grad_gain = jnp.sum(upstream * values * inverse, axis=0)
    return (grad_values, grad_gain)


def layout(lengths, rows):
    ends = jnp.cumsum(lengths, axis=-1)
    starts = ends - lengths
    places = jnp.arange(rows, dtype=jnp.int32)
    inside = (
        (places[..., :, None] >= starts[..., None, :]) & (places[..., :, None] < ends[..., None, :])
    ).astype(jnp.int32)
    number = jnp.arange(lengths.shape[-1], dtype=jnp.int32)
    alive = jnp.sum(inside, axis=-1)
    segment = jnp.sum(inside * number, axis=-1) + (1 - alive) * (lengths.shape[-1] + places)
    position = jnp.sum(inside * (places[..., :, None] - starts[..., None, :]), axis=-1)
    return (segment, position)


def rope_angles(position, head_size):
    half = head_size // 2
    freq = THETA ** (-2.0 * jnp.arange(half, dtype=jnp.float32) / head_size)
    angle = position.astype(jnp.float32)[..., None] * freq
    return (jnp.cos(angle), jnp.sin(angle))


def rotate(values, cosine, sine):
    half = values.shape[-1] // 2
    first, second = (values[..., :half], values[..., half:])
    cos_here = cosine[..., None, :]
    sin_here = sine[..., None, :]
    return jnp.concatenate(
        [first * cos_here - second * sin_here, second * cos_here + first * sin_here], axis=-1
    )


def unrotate(grads, cosine, sine):
    half = grads.shape[-1] // 2
    first, second = (grads[..., :half], grads[..., half:])
    cos_here = cosine[..., None, :]
    sin_here = sine[..., None, :]
    return jnp.concatenate(
        [first * cos_here + second * sin_here, second * cos_here - first * sin_here], axis=-1
    )


def block_scores(query_block, keys, seg_block, segment, start):
    scores = jnp.einsum(
        "qhd,khd->hqk", query_block, keys, preferred_element_type=jnp.float32
    ) * HEAD_DIM ** (-0.5)
    rows_query = start + jnp.arange(query_block.shape[0], dtype=jnp.int32)
    rows_key = jnp.arange(keys.shape[0], dtype=jnp.int32)
    allowed = (seg_block[:, None] == segment[None, :]) & (rows_key[None, :] <= rows_query[:, None])
    return jnp.where(allowed[None], scores, NEG)


def attention_forward(queries, keys, values, segment, block):
    rows = queries.shape[0]

    def one_block(index):
        start = index * block
        query_block = lax.dynamic_slice_in_dim(queries, start, block, 0)
        seg_block = lax.dynamic_slice_in_dim(segment, start, block, 0)
        scores = block_scores(query_block, keys, seg_block, segment, start)
        top = jnp.max(scores, axis=-1, keepdims=True)
        raised = jnp.exp(scores - top)
        total = jnp.sum(raised, axis=-1, keepdims=True)
        weights = (raised / total).astype(jnp.bfloat16)
        context = jnp.einsum("hqk,khd->qhd", weights, values, preferred_element_type=jnp.float32)
        return (context, top, total)

    context, top, total = lax.map(one_block, jnp.arange(rows // block, dtype=jnp.int32))
    return (context.reshape(queries.shape), top, total)


def attention_backward(queries, keys, values, segment, block, top, total, grad_context):
    rows = queries.shape[0]
    scale = HEAD_DIM ** (-0.5)

    def one_block(carry, index):
        grad_keys, grad_values = carry
        start = index * block
        query_block = lax.dynamic_slice_in_dim(queries, start, block, 0)
        seg_block = lax.dynamic_slice_in_dim(segment, start, block, 0)
        grad_block = lax.dynamic_slice_in_dim(grad_context, start, block, 0)
        scores = block_scores(query_block, keys, seg_block, segment, start)
        weights_f = jnp.exp(scores - top[index]) / total[index]
        weights = weights_f.astype(jnp.bfloat16)
        grad_weights = jnp.einsum(
            "qhd,khd->hqk", grad_block, values, preferred_element_type=jnp.float32
        )
        inner = jnp.sum(weights_f * grad_weights, axis=-1, keepdims=True)
        grad_scores = (weights_f * (grad_weights - inner)).astype(jnp.bfloat16)
        grad_query = (
            jnp.einsum("hqk,khd->qhd", grad_scores, keys, preferred_element_type=jnp.float32)
            * scale
        )
        grad_keys = (
            grad_keys
            + jnp.einsum(
                "hqk,qhd->khd", grad_scores, query_block, preferred_element_type=jnp.float32
            )
            * scale
        )
        grad_values = grad_values + jnp.einsum(
            "hqk,qhd->khd", weights, grad_block, preferred_element_type=jnp.float32
        )
        return ((grad_keys, grad_values), grad_query)

    empty = jnp.zeros(keys.shape, jnp.float32)
    (grad_keys, grad_values), grad_query = lax.scan(
        one_block, (empty, empty), jnp.arange(rows // block, dtype=jnp.int32)
    )
    return (grad_query.reshape(queries.shape), grad_keys, grad_values)


def shards(
    tokens,
    cotangent,
    seq_lengths,
    expert_ids,
    slot_index,
    w_query,
    w_key,
    w_value,
    w_output,
    query_gain,
    key_gain,
    attn_gain,
    moe_gain,
    router,
    w_gate,
    w_up,
    w_down,
):
    rows, width = tokens.shape
    local = w_query.shape[1]
    heads_here = local // HEAD_DIM
    groups = lax.axis_size("expert")
    experts_here = w_gate.shape[0]
    experts_all = experts_here * groups
    capacity = max(2, 3 * rows * TOP // (4 * experts_all))
    block = min(512, rows)
    shape_heads = (rows, heads_here, HEAD_DIM)
    segment, position = layout(seq_lengths, rows)
    cosine, sine = rope_angles(position, HEAD_DIM)
    inputs = tokens.astype(jnp.float32)
    normed, inverse_in = norm_rows(inputs, attn_gain)
    attn_in = normed.astype(jnp.bfloat16)
    query_raw = jnp.dot(attn_in, w_query, preferred_element_type=jnp.float32)
    key_raw = jnp.dot(attn_in, w_key, preferred_element_type=jnp.float32)
    value_raw = jnp.dot(attn_in, w_value, preferred_element_type=jnp.float32)
    query_total, key_total = lax.psum(
        (jnp.sum(query_raw * query_raw, axis=-1), jnp.sum(key_raw * key_raw, axis=-1)), "tensor"
    )
    query_inverse = lax.rsqrt(query_total / width + EPS)[:, None]
    key_inverse = lax.rsqrt(key_total / width + EPS)[:, None]
    queries = rotate(
        (query_raw * query_inverse * query_gain).reshape(shape_heads), cosine, sine
    ).astype(jnp.bfloat16)
    keys = rotate((key_raw * key_inverse * key_gain).reshape(shape_heads), cosine, sine).astype(
        jnp.bfloat16
    )
    values = value_raw.reshape(shape_heads).astype(jnp.bfloat16)
    context, top, total = attention_forward(queries, keys, values, segment, block)
    context_low = context.reshape(rows, local).astype(jnp.bfloat16)
    attn = lax.psum(
        jnp.dot(context_low, w_output, preferred_element_type=jnp.float32).astype(jnp.bfloat16),
        "tensor",
    ).astype(jnp.float32)
    hidden_in = inputs + attn
    moe_in, inverse_moe = norm_rows(hidden_in, moe_gain)
    router_wide = router.astype(jnp.float32)
    shares = jax.nn.softmax(jnp.dot(moe_in, router_wide, precision=lax.Precision.HIGHEST), axis=-1)
    chosen = expert_ids[:, :, None] == jnp.arange(experts_all, dtype=jnp.int32)[None, None, :]
    gates = jnp.sum(jnp.where(chosen, shares[:, None, :], 0.0), axis=-1)
    kept = slot_index >= 0
    target_slot = jnp.where(
        kept, expert_ids * capacity + slot_index, experts_all * capacity
    ).reshape(-1)
    token_of = (
        jnp.full((experts_all * capacity,), -1, jnp.int32)
        .at[target_slot]
        .set(jnp.repeat(jnp.arange(rows, dtype=jnp.int32), TOP), mode="drop")
    )
    gate_of = (
        jnp.zeros((experts_all * capacity,), jnp.float32)
        .at[target_slot]
        .set(gates.reshape(-1), mode="drop")
    )
    filled = (token_of >= 0)[:, None]
    source_row = jnp.maximum(token_of, 0)
    moe_low = moe_in.astype(jnp.bfloat16)
    send_rows = jnp.where(filled, moe_low[source_row], jnp.zeros((), jnp.bfloat16)).reshape(
        groups, experts_here * capacity, width
    )
    arrived = lax.all_to_all(send_rows, "expert", split_axis=0, concat_axis=0, tiled=True)
    arrived = arrived.reshape(groups, experts_here, capacity, width)
    gate_pre = jnp.einsum("secd,edf->secf", arrived, w_gate, preferred_element_type=jnp.float32)
    up_pre = jnp.einsum("secd,edf->secf", arrived, w_up, preferred_element_type=jnp.float32)
    activated = jax.nn.silu(gate_pre)
    hidden = (activated * up_pre).astype(jnp.bfloat16)
    partial_value = jnp.einsum(
        "secf,efd->secd", hidden, w_down, preferred_element_type=jnp.float32
    ).astype(jnp.bfloat16)
    dy_rows = jnp.where(filled, cotangent[source_row], jnp.zeros((), jnp.bfloat16))
    returned = lax.all_to_all(partial_value, "expert", split_axis=0, concat_axis=0, tiled=True)
    returned = returned.reshape(experts_all * capacity, width).astype(jnp.float32)
    moe_part = jax.ops.segment_sum(returned * gate_of[:, None], source_row, num_segments=rows)
    moe = lax.psum(moe_part.astype(jnp.bfloat16), "tensor").astype(jnp.float32)
    row_dots = jnp.sum(dy_rows.astype(jnp.float32) * returned, axis=-1)
    out = (hidden_in + moe).astype(jnp.bfloat16)
    grad_gate = jnp.take(row_dots, target_slot, mode="fill", fill_value=0.0).reshape(rows, TOP)
    grad_shares = jnp.sum(jnp.where(chosen, grad_gate[:, :, None], 0.0), axis=1)
    grad_logits = shares * (grad_shares - jnp.sum(shares * grad_shares, axis=-1, keepdims=True))
    router_back = jnp.einsum("te,de->td", grad_logits, router_wide, precision=lax.Precision.HIGHEST)
    router_part = jnp.einsum("td,te->de", moe_in, grad_logits, precision=lax.Precision.HIGHEST)
    grad_rows = (
        (dy_rows.astype(jnp.float32) * gate_of[:, None])
        .astype(jnp.bfloat16)
        .reshape(groups, experts_here * capacity, width)
    )
    grad_arrived = lax.all_to_all(grad_rows, "expert", split_axis=0, concat_axis=0, tiled=True)
    grad_arrived = grad_arrived.reshape(groups, experts_here, capacity, width)
    grad_hidden = jnp.einsum(
        "secd,efd->secf", grad_arrived, w_down, preferred_element_type=jnp.float32
    )
    grad_w_down = jnp.einsum(
        "secf,secd->efd", hidden, grad_arrived, preferred_element_type=jnp.float32
    )
    sigma = jax.nn.sigmoid(gate_pre)
    grad_gate_pre = (grad_hidden * up_pre * sigma * (1.0 + gate_pre * (1.0 - sigma))).astype(
        jnp.bfloat16
    )
    grad_up_pre = (grad_hidden * activated).astype(jnp.bfloat16)
    grad_w_gate = jnp.einsum(
        "secd,secf->edf", arrived, grad_gate_pre, preferred_element_type=jnp.float32
    )
    grad_w_up = jnp.einsum(
        "secd,secf->edf", arrived, grad_up_pre, preferred_element_type=jnp.float32
    )
    grad_in_rows = jnp.einsum(
        "secf,edf->secd", grad_gate_pre, w_gate, preferred_element_type=jnp.float32
    )
    grad_in_rows = (
        grad_in_rows
        + jnp.einsum("secf,edf->secd", grad_up_pre, w_up, preferred_element_type=jnp.float32)
    ).astype(jnp.bfloat16)
    back_rows = lax.all_to_all(
        grad_in_rows.reshape(groups, experts_here * capacity, width),
        "expert",
        split_axis=0,
        concat_axis=0,
        tiled=True,
    )
    back_rows = back_rows.reshape(experts_all * capacity, width).astype(jnp.float32)
    moe_back = jax.ops.segment_sum(back_rows, source_row, num_segments=rows)
    grad_moe_in, grad_router_rows = (
        lax.psum((moe_back + router_back).astype(jnp.bfloat16), "tensor").astype(jnp.float32),
        lax.psum(router_part.astype(jnp.bfloat16), "tensor").astype(jnp.float32),
    )
    grad_norm_moe, grad_moe_gain = norm_back(hidden_in, inverse_moe, moe_gain, grad_moe_in)
    grad_hidden_in = cotangent.astype(jnp.float32) + grad_norm_moe
    grad_low = grad_hidden_in.astype(jnp.bfloat16)
    grad_w_output = jnp.einsum(
        "tf,td->fd", context_low, grad_low, preferred_element_type=jnp.float32
    )
    grad_context = (
        jnp.einsum("td,fd->tf", grad_low, w_output, preferred_element_type=jnp.float32)
        .astype(jnp.bfloat16)
        .reshape(shape_heads)
    )
    grad_queries, grad_keys, grad_values = attention_backward(
        queries, keys, values, segment, block, top, total, grad_context
    )
    grad_query_normed = unrotate(grad_queries, cosine, sine).reshape(rows, local)
    grad_key_normed = unrotate(grad_keys, cosine, sine).reshape(rows, local)
    query_scaled = grad_query_normed * query_gain
    key_scaled = grad_key_normed * key_gain
    query_inner, key_inner = lax.psum(
        (jnp.sum(query_raw * query_scaled, axis=-1), jnp.sum(key_raw * key_scaled, axis=-1)),
        "tensor",
    )
    grad_query_raw = (
        query_inverse * query_scaled
        - query_raw * query_inverse * query_inverse * query_inverse * (query_inner / width)[:, None]
    )
    grad_key_raw = (
        key_inverse * key_scaled
        - key_raw * key_inverse * key_inverse * key_inverse * (key_inner / width)[:, None]
    )
    grad_query_gain = jnp.sum(grad_query_normed * query_raw * query_inverse, axis=0)
    grad_key_gain = jnp.sum(grad_key_normed * key_raw * key_inverse, axis=0)
    query_low = grad_query_raw.astype(jnp.bfloat16)
    key_low = grad_key_raw.astype(jnp.bfloat16)
    value_low = grad_values.reshape(rows, local).astype(jnp.bfloat16)
    grad_w_query = jnp.einsum("td,tf->df", attn_in, query_low, preferred_element_type=jnp.float32)
    grad_w_key = jnp.einsum("td,tf->df", attn_in, key_low, preferred_element_type=jnp.float32)
    grad_w_value = jnp.einsum("td,tf->df", attn_in, value_low, preferred_element_type=jnp.float32)
    terms_in = jnp.einsum("tf,df->td", query_low, w_query, preferred_element_type=jnp.float32)
    terms_in = terms_in + jnp.einsum(
        "tf,df->td", key_low, w_key, preferred_element_type=jnp.float32
    )
    terms_in = terms_in + jnp.einsum(
        "tf,df->td", value_low, w_value, preferred_element_type=jnp.float32
    )
    grad_normed = lax.psum(terms_in.astype(jnp.bfloat16), "tensor").astype(jnp.float32)
    grad_norm_in, grad_attn_gain = norm_back(inputs, inverse_in, attn_gain, grad_normed)
    grad_input = (grad_hidden_in + grad_norm_in).astype(jnp.bfloat16)
    sums = (
        lax.psum_scatter(
            grad_w_query.astype(jnp.bfloat16), "expert", scatter_dimension=0, tiled=True
        ).astype(jnp.float32),
        lax.psum_scatter(
            grad_w_key.astype(jnp.bfloat16), "expert", scatter_dimension=0, tiled=True
        ).astype(jnp.float32),
        lax.psum_scatter(
            grad_w_value.astype(jnp.bfloat16), "expert", scatter_dimension=0, tiled=True
        ).astype(jnp.float32),
        lax.psum_scatter(
            grad_w_output.astype(jnp.bfloat16), "expert", scatter_dimension=1, tiled=True
        ).astype(jnp.float32),
        lax.psum_scatter(
            grad_query_gain.astype(jnp.bfloat16), "expert", scatter_dimension=0, tiled=True
        ).astype(jnp.float32),
        lax.psum_scatter(
            grad_key_gain.astype(jnp.bfloat16), "expert", scatter_dimension=0, tiled=True
        ).astype(jnp.float32),
        lax.psum_scatter(
            grad_attn_gain.astype(jnp.bfloat16), "expert", scatter_dimension=0, tiled=True
        ).astype(jnp.float32),
        lax.psum_scatter(
            grad_moe_gain.astype(jnp.bfloat16), "expert", scatter_dimension=0, tiled=True
        ).astype(jnp.float32),
        lax.psum_scatter(
            grad_router_rows.astype(jnp.bfloat16), "expert", scatter_dimension=0, tiled=True
        ).astype(jnp.float32),
    )
    lows = tuple((item.astype(jnp.bfloat16) for item in sums))
    return (
        out,
        grad_input,
        lows[0],
        lows[1],
        lows[2],
        lows[3],
        lows[4],
        lows[5],
        lows[6],
        lows[7],
        lows[8],
        grad_w_gate.astype(jnp.bfloat16),
        grad_w_up.astype(jnp.bfloat16),
        grad_w_down.astype(jnp.bfloat16),
    )


F32 = jnp.float32
BF = jnp.bfloat16
NN = (((1,), (0,)), ((), ()))
NT = (((1,), (1,)), ((), ()))
TN = (((0,), (0,)), ((), ()))
VMEM_BYTES = 62 * 2**20
COLUMN_TILE = 512
ROW_TILE = 512
QUERY_TILE = 256


def mul(left, right, dims=NN):
    return lax.dot_general(left, right, dims, preferred_element_type=F32)


def kernel_params():
    return pltpu.CompilerParams(vmem_limit_bytes=VMEM_BYTES)


def whole(shape):
    return pl.BlockSpec(shape, lambda i: (0,) * len(shape), pipeline_mode=pl.Buffered(1))


def softmax_block(queries, keys, seg_rows, seg_columns, start, scale):
    scores = mul(queries, keys, NT) * scale
    rows = start + lax.broadcasted_iota(jnp.int32, scores.shape, 0)
    columns = lax.broadcasted_iota(jnp.int32, scores.shape, 1)
    allowed = (seg_rows == seg_columns) & (columns <= rows)
    scores = jnp.where(allowed, scores, NEG)
    raised = jnp.exp(scores - jnp.max(scores, axis=-1, keepdims=True))
    return raised * (1.0 / jnp.sum(raised, axis=-1, keepdims=True))


def attention_kernel(
    q_ref, k_ref, v_ref, qi_ref, ki_ref, qg_ref, kg_ref, cos_ref, sin_ref, row_ref, col_ref,
    qh_ref, kh_ref, ctx_ref,
):
    rows, size = q_ref.shape
    tile = min(QUERY_TILE, rows)
    for raw, inverse, gain, low in ((q_ref, qi_ref, qg_ref, qh_ref), (k_ref, ki_ref, kg_ref, kh_ref)):
        normed = raw[...] * inverse[...] * gain[...]
        turned = normed * cos_ref[...] + pltpu.roll(normed, size // 2, 1) * sin_ref[...]
        low[...] = turned.astype(BF)
    for start in range(0, rows, tile):
        end = start + tile
        weights = softmax_block(
            qh_ref[start:end], kh_ref[:end], row_ref[start:end], col_ref[:, :end], start, size**-0.5
        )
        ctx_ref[start:end] = mul(weights.astype(BF), v_ref[:end]).astype(BF)


def attention_back_kernel(
    q_ref, k_ref, v_ref, qi_ref, ki_ref, qg_ref, kg_ref, cos_ref, sin_ref, row_ref, col_ref,
    qh_ref, kh_ref, dctx_ref,
    dq_ref, dk_ref, dv_ref, inner_ref, dqg_ref, dkg_ref, dq_total, dk_total, dv_total,
):
    rows, size = q_ref.shape
    scale = size**-0.5
    tile = min(QUERY_TILE, rows)
    dk_total[...] = jnp.zeros_like(dk_total)
    dv_total[...] = jnp.zeros_like(dv_total)
    for start in range(0, rows, tile):
        end = start + tile
        keys = kh_ref[:end]
        weights = softmax_block(
            qh_ref[start:end], keys, row_ref[start:end], col_ref[:, :end], start, scale
        )
        grad_weights = mul(dctx_ref[start:end], v_ref[:end], NT)
        inner = jnp.sum(weights * grad_weights, axis=-1, keepdims=True)
        grad_scores = (weights * (grad_weights - inner)).astype(BF)
        dq_total[start:end] = mul(grad_scores, keys) * scale
        dk_total[:end] += mul(grad_scores, qh_ref[start:end], TN) * scale
        dv_total[:end] += mul(weights.astype(BF), dctx_ref[start:end], TN)
    dv_ref[...] = dv_total[...].astype(BF)
    inners = []
    for total, raw, inverse, gain, out, dgain in (
        (dq_total, q_ref, qi_ref, qg_ref, dq_ref, dqg_ref),
        (dk_total, k_ref, ki_ref, kg_ref, dk_ref, dkg_ref),
    ):
        grad = total[...]
        grad = grad * cos_ref[...] - pltpu.roll(grad, size // 2, 1) * sin_ref[...]
        values = raw[...]
        dgain[...] = jnp.sum(grad * values * inverse[...], axis=0, keepdims=True)
        scaled = grad * gain[...]
        inners.append(jnp.sum(values * scaled, axis=1, keepdims=True))
        out[...] = scaled
    inner_ref[0] = jnp.concatenate(inners, axis=1)


def head_specs(rows):
    head = pl.BlockSpec((rows, HEAD_DIM), lambda h: (0, h))
    gain = pl.BlockSpec((1, HEAD_DIM), lambda h: (0, h))
    column = whole((rows, 1))
    table = whole((rows, HEAD_DIM))
    return head, gain, [head, head, head, column, column, gain, gain, table, table, column, whole((1, rows))]


def attention_call(operands, rows, local):
    head, gain, specs = head_specs(rows)
    heads = local // HEAD_DIM
    return pl.pallas_call(
        attention_kernel,
        grid=(heads,),
        in_specs=specs,
        out_specs=[head] * 3,
        out_shape=[jax.ShapeDtypeStruct((rows, local), BF)] * 3,
        compiler_params=kernel_params(),
        cost_estimate=pl.CostEstimate(
            flops=2 * rows * rows * local, bytes_accessed=12 * rows * local, transcendentals=rows * rows * heads // 2
        ),
        name="attention_rows",
    )(*operands)


def attention_back_call(operands, rows, local):
    head, gain, specs = head_specs(rows)
    heads = local // HEAD_DIM
    return pl.pallas_call(
        attention_back_kernel,
        grid=(heads,),
        in_specs=specs + [head] * 3,
        out_specs=[head] * 3 + [pl.BlockSpec((1, rows, 2), lambda h: (h, 0, 0)), gain, gain],
        out_shape=[jax.ShapeDtypeStruct((rows, local), F32)] * 2
        + [jax.ShapeDtypeStruct((rows, local), BF), jax.ShapeDtypeStruct((heads, rows, 2), F32)]
        + [jax.ShapeDtypeStruct((1, local), F32)] * 2,
        scratch_shapes=[pltpu.VMEM((rows, HEAD_DIM), F32)] * 3,
        compiler_params=kernel_params(),
        cost_estimate=pl.CostEstimate(
            flops=8 * rows * rows * local, bytes_accessed=24 * rows * local, transcendentals=rows * rows * heads // 2
        ),
        name="attention_rows_back",
    )(*operands)


def rows_kernel(sets, experts, x_ref, dy_ref, gate_ref, *rest):
    w_refs = rest[:sets]
    moe_ref, dx_ref, kept_ref, dot_ref, held, moe, dx, sems = rest[sets:]
    step = pl.program_id(0)
    slot = lax.rem(step, 2)
    rows, width = x_ref.shape
    hid = held.shape[2] // 3

    def fetch(index, place):
        for number in range(sets):

            @pl.when(index == number)
            def _():
                pltpu.make_async_copy(w_refs[number], held.at[place], sems.at[place]).start()

    @pl.when(step == 0)
    def _():
        fetch(0, 0)
        moe[...] = jnp.zeros_like(moe)
        dx[...] = jnp.zeros_like(dx)

    @pl.when(step + 1 < sets)
    def _():
        fetch(step + 1, 1 - slot)

    pltpu.make_async_copy(w_refs[0], held.at[slot], sems.at[slot]).wait()
    for one in range(experts):
        base = one * 3 * hid
        for first in range(0, rows, ROW_TILE):
            here = slice(first, first + ROW_TILE)
            both = mul(x_ref[here], held[slot, one, hid:], NT)
            back = mul(dy_ref[here], held[slot, one, :hid], NT)
            pre, up = both[:, :hid], both[:, hid:]
            sigma = 1.0 / (1.0 + jnp.exp(-pre))
            active = pre * sigma
            gate = gate_ref[0, here, one : one + 1]
            hidden = active * up
            dot_ref[0, here, one : one + 1] = jnp.sum(hidden * back, axis=1, keepdims=True)
            back = back * gate
            kept_ref[here, base : base + hid] = (hidden * gate).astype(BF)
            kept_ref[here, base + hid : base + 2 * hid] = (
                back * up * sigma * (1.0 + pre * (1.0 - sigma))
            ).astype(BF)
            kept_ref[here, base + 2 * hid : base + 3 * hid] = (back * active).astype(BF)
    for first in range(0, width, COLUMN_TILE):
        here = slice(first, first + COLUMN_TILE)
        total = moe[:, here]
        for one in range(experts):
            base = one * 3 * hid
            total = total + mul(kept_ref[:, base : base + hid], held[slot, one, :hid, here])
        moe[:, here] = total
        total = dx[:, here]
        for one in range(experts):
            base = one * 3 * hid
            total = total + mul(kept_ref[:, base + hid : base + 3 * hid], held[slot, one, hid:, here])
        dx[:, here] = total

    @pl.when(step == sets - 1)
    def _():
        moe_ref[...] = moe[...].astype(BF)
        dx_ref[...] = dx[...].astype(BF)


def rows_call(moe_in, cotangent, gates, weights):
    rows, width = moe_in.shape
    sets = len(weights)
    experts, depth, _ = weights[0].shape
    full = whole((rows, width))
    narrow = pl.BlockSpec((1, rows, experts), lambda i: (i, 0, 0))
    wide = experts * depth
    return pl.pallas_call(
        functools.partial(rows_kernel, sets, experts),
        grid=(sets,),
        in_specs=[full, full, narrow] + [pl.BlockSpec(memory_space=pl.ANY)] * sets,
        out_specs=[full, full, pl.BlockSpec((rows, wide), lambda i: (0, i)), narrow],
        out_shape=[jax.ShapeDtypeStruct((rows, width), BF)] * 2
        + [jax.ShapeDtypeStruct((rows, sets * wide), BF), jax.ShapeDtypeStruct((sets, rows, experts), F32)],
        scratch_shapes=[
            pltpu.VMEM((2, experts, depth, width), BF),
            pltpu.VMEM((rows, width), F32),
            pltpu.VMEM((rows, width), F32),
            pltpu.SemaphoreType.DMA((2,)),
        ],
        compiler_params=kernel_params(),
        cost_estimate=pl.CostEstimate(
            flops=4 * rows * width * wide * sets,
            bytes_accessed=8 * rows * width + 2 * sets * wide * (rows + width),
            transcendentals=rows * wide * sets // 3,
        ),
        name="expert_rows",
    )(moe_in, cotangent, gates, *weights)


def weight_grads_kernel(experts, added, x_ref, dy_ref, kept_ref, *rest):
    out_ref, turned = rest[-2:]
    hid = turned.shape[0] // (3 * experts)

    @pl.when(pl.program_id(0) == 0)
    def _():
        for one in range(experts):
            base = one * 3 * hid
            turned[one * hid : (one + 1) * hid] = kept_ref[:, base : base + hid].T
            place = experts * hid + one * 2 * hid
            turned[place : place + 2 * hid] = kept_ref[:, base + hid : base + 3 * hid].T

    down = mul(turned[: experts * hid], dy_ref[...])
    both = mul(turned[experts * hid :], x_ref[...])
    for one in range(experts):
        first, second = down[one * hid : (one + 1) * hid], both[one * 2 * hid : (one + 1) * 2 * hid]
        if added:
            first = first + rest[0][one, :hid].astype(F32)
            second = second + rest[0][one, hid:].astype(F32)
        out_ref[one, :hid] = first.astype(BF)
        out_ref[one, hid:] = second.astype(BF)


def weight_grads_call(moe_in, cotangent, kept, number, experts, depth, addend=None):
    rows, width = moe_in.shape
    tile = COLUMN_TILE
    column = pl.BlockSpec((rows, tile), lambda i: (0, i))
    out = pl.BlockSpec((experts, depth, tile), lambda i: (0, 0, i))
    operands = [moe_in, cotangent, kept]
    specs = [column, column, pl.BlockSpec((rows, experts * depth), lambda i: (0, number), pipeline_mode=pl.Buffered(1))]
    if addend is not None:
        operands.append(addend)
        specs.append(out)
    return pl.pallas_call(
        functools.partial(weight_grads_kernel, experts, addend is not None),
        grid=(width // tile,),
        in_specs=specs,
        out_specs=out,
        out_shape=jax.ShapeDtypeStruct((experts, depth, width), BF),
        scratch_shapes=[pltpu.VMEM((experts * depth, rows), BF)],
        compiler_params=kernel_params(),
        cost_estimate=pl.CostEstimate(
            flops=2 * rows * width * experts * depth,
            bytes_accessed=4 * rows * width + 4 * experts * depth * width,
            transcendentals=0,
        ),
        name="expert_weight_grads",
    )(*operands)


def swap(values, bit):
    size = lax.axis_size("expert")
    return lax.ppermute(values, "expert", [(i, i ^ bit) for i in range(size)])


def spread_weights(own):
    held = {0: own}
    held[1] = swap(own, 1)
    held[2] = swap(own, 2)
    held[4] = swap(own, 4)
    half = own.shape[0] // 2
    far = (swap(held[2][:half], 4), swap(held[4][half:], 2))
    held[6] = jnp.concatenate(far, axis=0)
    for r in (3, 5, 7):
        held[r] = swap(held[r - 1], 1)
    return held


def collect_weight_grads(part):
    chip = {}
    for r in (6, 4, 2, 0):
        chip[r] = part(r, swap(part(r + 1, None), 1))
    half = chip[6].shape[0] // 2
    via_first = swap(chip[6][:half], 2)
    via_second = swap(chip[6][half:], 4)
    plus = lambda left, right: (left.astype(F32) + right.astype(F32)).astype(BF)
    from_four = (swap(plus(chip[4][:half], via_first), 4), swap(chip[4][half:], 4))
    from_two = (swap(chip[2][:half], 2), swap(plus(chip[2][half:], via_second), 2))
    total = chip[0].astype(F32) + jnp.concatenate(from_four, axis=0).astype(F32)
    return total + jnp.concatenate(from_two, axis=0).astype(F32)


def shards_near(
    tokens, cotangent, seq_lengths, expert_ids, slot_index, w_query, w_key, w_value, w_output,
    query_gain, key_gain, attn_gain, moe_gain, router, w_gate, w_up, w_down,
):
    rows, width = tokens.shape
    local = w_query.shape[1]
    groups = lax.axis_size("expert")
    n_tensor = lax.axis_size("tensor")
    here = lax.axis_index("expert")
    layer = lax.axis_index("tensor")
    experts_here, hid = w_gate.shape[0], w_gate.shape[2]
    experts_all = experts_here * groups
    own_rows = rows // n_tensor

    packed = jnp.concatenate([w_down, jnp.swapaxes(w_gate, 1, 2), jnp.swapaxes(w_up, 1, 2)], axis=1)
    weights = spread_weights(packed)

    segment, position = layout(seq_lengths, rows)
    cosine, sine = rope_angles(position, HEAD_DIM)
    cos_table = jnp.concatenate([cosine, cosine], axis=1)
    sin_table = jnp.concatenate([-sine, sine], axis=1)
    inputs = tokens.astype(F32)
    normed, inverse_in = norm_rows(inputs, attn_gain)
    attn_in = normed.astype(BF)
    query_raw = mul(attn_in, w_query)
    key_raw = mul(attn_in, w_key)
    totals = jnp.stack([jnp.sum(query_raw * query_raw, axis=-1), jnp.sum(key_raw * key_raw, axis=-1)])
    totals = sum_small(totals)
    values = mul(attn_in, w_value).astype(BF)
    query_inverse = lax.rsqrt(totals[0] / width + EPS)[:, None]
    key_inverse = lax.rsqrt(totals[1] / width + EPS)[:, None]
    operands = [
        query_raw, key_raw, values, query_inverse, key_inverse, query_gain[None], key_gain[None],
        cos_table, sin_table, segment[:, None], segment[None],
    ]
    queries, keys, context = attention_call(operands, rows, local)
    attn = lax.psum_scatter(mul(context, w_output).astype(BF), "tensor", scatter_dimension=0, tiled=True)

    own = lambda array: lax.dynamic_slice_in_dim(array, layer * own_rows, own_rows, 0)
    tokens_own = own(tokens).astype(F32)
    cotangent_own = own(cotangent).astype(F32)
    hidden_in = tokens_own + attn.astype(F32)
    moe_in, inverse_moe = norm_rows(hidden_in, moe_gain)
    router_wide = router.astype(F32)
    shares = jax.nn.softmax(jnp.dot(moe_in, router_wide, precision=lax.Precision.HIGHEST), axis=-1)
    moe_low = lax.all_gather(moe_in.astype(BF), "tensor", tiled=True)
    shares_all = gather_small(shares)

    number = jnp.arange(experts_all, dtype=jnp.int32)
    carried = (expert_ids[:, :, None] == number) & (slot_index >= 0)[:, :, None]
    carried = jnp.sum(carried.astype(F32), axis=1)
    gates = shares_all * carried
    order = [0, 1, 2, 3, 4, 5, 6, 7]
    of_set = lambda array, r: lax.dynamic_slice_in_dim(array, (here ^ r) * experts_here, experts_here, 1)
    gate_sets = jnp.stack([of_set(gates, r) for r in order])
    moe_part, dx_part, kept, dots = rows_call(moe_low, cotangent, gate_sets, [weights[r] for r in order])

    dots_all = jnp.zeros((rows, experts_all), F32)
    for place, r in enumerate(order):
        dots_all = lax.dynamic_update_slice(dots_all, dots[place], (0, (here ^ r) * experts_here))
    dshares = scatter_small(dots_all * carried)
    dlogits = shares * (dshares - jnp.sum(shares * dshares, axis=-1, keepdims=True))
    router_back = jnp.einsum("te,de->td", dlogits, router_wide, precision=lax.Precision.HIGHEST)
    router_part = jnp.einsum("td,te->de", moe_in, dlogits, precision=lax.Precision.HIGHEST)

    dx = lax.psum_scatter(dx_part, "tensor", scatter_dimension=0, tiled=True)
    grad_moe_in = dx.astype(F32) + router_back
    grad_norm_moe, grad_moe_gain = norm_back(hidden_in, inverse_moe, moe_gain, grad_moe_in)
    grad_hidden_in = cotangent_own + grad_norm_moe
    grad_low = lax.all_gather(grad_hidden_in.astype(BF), "tensor", tiled=True)
    grad_context = mul(grad_low, w_output, NT).astype(BF)
    dq, dk, value_low, inner, grad_query_gain, grad_key_gain = attention_back_call(
        operands + [queries, keys, grad_context], rows, local
    )
    inner = sum_small(jnp.sum(inner, axis=0).T)
    moe = lax.psum_scatter(moe_part, "tensor", scatter_dimension=0, tiled=True)
    out = lax.all_gather((hidden_in + moe.astype(F32)).astype(BF), "tensor", tiled=True)

    def raw_grad(scaled, raw, inverse, total):
        return (inverse * scaled - raw * inverse * inverse * inverse * (total / width)[:, None]).astype(BF)

    query_low = raw_grad(dq, query_raw, query_inverse, inner[0])
    key_low = raw_grad(dk, key_raw, key_inverse, inner[1])
    terms_in = mul(query_low, w_query, NT) + mul(key_low, w_key, NT) + mul(value_low, w_value, NT)
    grad_normed = lax.psum_scatter(terms_in.astype(BF), "tensor", scatter_dimension=0, tiled=True).astype(F32)
    inverse_own = lax.dynamic_slice_in_dim(inverse_in, layer * own_rows, own_rows, 0)
    grad_norm_in, grad_attn_gain = norm_back(tokens_own, inverse_own, attn_gain, grad_normed)
    grad_input = lax.all_gather((grad_hidden_in + grad_norm_in).astype(BF), "tensor", tiled=True)

    depth = packed.shape[1]
    part = lambda r, addend: weight_grads_call(moe_low, cotangent, kept, order.index(r), experts_here, depth, addend)
    expert_grads = collect_weight_grads(part).astype(BF)
    grad_w_down = expert_grads[:, :hid]
    grad_w_gate = jnp.swapaxes(expert_grads[:, hid : 2 * hid], 1, 2)
    grad_w_up = jnp.swapaxes(expert_grads[:, 2 * hid :], 1, 2)

    scatter = lambda array, dim: lax.psum_scatter(array, "expert", scatter_dimension=dim, tiled=True)
    grad_w_query = scatter(mul(attn_in, query_low, TN).astype(BF), 0)
    grad_w_key = scatter(mul(attn_in, key_low, TN).astype(BF), 0)
    grad_w_value = scatter(mul(attn_in, value_low, TN).astype(BF), 0)
    grad_w_output = scatter(mul(context, grad_low, TN).astype(BF), 1)
    gains = scatter(jnp.concatenate([
        grad_query_gain.reshape(groups, -1), grad_key_gain.reshape(groups, -1)], axis=1), 0)[0]
    span = local // groups
    both = jnp.concatenate(
        [router_part, grad_moe_gain[:, None], grad_attn_gain[:, None]], axis=1
    )
    both = scatter(lax.psum(both, "tensor"), 0)
    return (
        out, grad_input, grad_w_query, grad_w_key, grad_w_value, grad_w_output,
        gains[:span].astype(BF), gains[span:].astype(BF),
        both[:, experts_all + 1].astype(BF), both[:, experts_all].astype(BF), both[:, :experts_all].astype(BF),
        grad_w_gate, grad_w_up, grad_w_down,
    )


def rotations():
    size = lax.axis_size("tensor")
    return [[(i, (i + d) % size) for i in range(size)] for d in range(1, size)]


def sum_small(values):
    total = values
    for pairs in rotations():
        total = total + lax.ppermute(values, "tensor", pairs)
    return total


def gather_small(values):
    rows = values.shape[0]
    size = lax.axis_size("tensor")
    place = lax.axis_index("tensor")
    whole_rows = jnp.zeros((rows * size,) + values.shape[1:], values.dtype)
    whole_rows = lax.dynamic_update_slice_in_dim(whole_rows, values, place * rows, 0)
    for d, pairs in enumerate(rotations(), 1):
        came = lax.ppermute(values, "tensor", pairs)
        whole_rows = lax.dynamic_update_slice_in_dim(whole_rows, came, lax.rem(place + size - d, size) * rows, 0)
    return whole_rows


def scatter_small(values):
    size = lax.axis_size("tensor")
    place = lax.axis_index("tensor")
    rows = values.shape[0] // size
    cut = lambda index: lax.dynamic_slice_in_dim(values, index * rows, rows, 0)
    total = cut(place)
    for d, pairs in enumerate(rotations(), 1):
        total = total + lax.ppermute(cut(lax.rem(place + d, size)), "tensor", pairs)
    return total


NEAR_GROUPS = 8


def solution(mesh):
    placed = (
        P("expert", None),
        P("expert", None),
        P("expert"),
        P("expert", None),
        P("expert", None),
        P(None, "tensor"),
        P(None, "tensor"),
        P(None, "tensor"),
        P("tensor", None),
        P("tensor"),
        P("tensor"),
        P(),
        P(),
        P(),
        P("expert", None, "tensor"),
        P("expert", None, "tensor"),
        P("expert", "tensor", None),
    )
    return jax.shard_map(
        shards_near if mesh.shape["expert"] == NEAR_GROUPS else shards,
        mesh=mesh,
        in_specs=placed,
        out_specs=(
            P("expert", None),
            P("expert", None),
            P("expert", "tensor"),
            P("expert", "tensor"),
            P("expert", "tensor"),
            P("tensor", "expert"),
            P(("tensor", "expert")),
            P(("tensor", "expert")),
            P("expert"),
            P("expert"),
            P("expert", None),
            P("expert", None, "tensor"),
            P("expert", None, "tensor"),
            P("expert", "tensor", None),
        ),
        check_vma=False,
    )
```

```python
import functools

import jax
import jax.numpy as jnp
from jax import lax
from jax.experimental import pallas as pl
from jax.experimental.pallas import tpu as pltpu
from jax.sharding import PartitionSpec as P

HEAD_DIM = 128
EXPERT = "expert"
TENSOR = "tensor"
TOP = 8


EPS = 1e-05
THETA = 10000.0
NEG = -1e30


def norm_rows(values, gain):
    inverse = lax.rsqrt(jnp.mean(values * values, axis=-1, keepdims=True) + EPS)
    return (values * inverse * gain, inverse)


def norm_back(values, inverse, gain, upstream):
    scaled = upstream * gain
    inner = jnp.mean(values * scaled, axis=-1, keepdims=True)
    grad_values = inverse * scaled - values * inverse * inverse * inverse * inner
    grad_gain = jnp.sum(upstream * values * inverse, axis=0)
    return (grad_values, grad_gain)


def layout(lengths, rows):
    ends = jnp.cumsum(lengths, axis=-1)
    starts = ends - lengths
    places = jnp.arange(rows, dtype=jnp.int32)
    inside = (
        (places[..., :, None] >= starts[..., None, :]) & (places[..., :, None] < ends[..., None, :])
    ).astype(jnp.int32)
    number = jnp.arange(lengths.shape[-1], dtype=jnp.int32)
    alive = jnp.sum(inside, axis=-1)
    segment = jnp.sum(inside * number, axis=-1) + (1 - alive) * (lengths.shape[-1] + places)
    position = jnp.sum(inside * (places[..., :, None] - starts[..., None, :]), axis=-1)
    return (segment, position)


def rope_angles(position, head_size):
    half = head_size // 2
    freq = THETA ** (-2.0 * jnp.arange(half, dtype=jnp.float32) / head_size)
    angle = position.astype(jnp.float32)[..., None] * freq
    return (jnp.cos(angle), jnp.sin(angle))


def rotate(values, cosine, sine):
    half = values.shape[-1] // 2
    first, second = (values[..., :half], values[..., half:])
    cos_here = cosine[..., None, :]
    sin_here = sine[..., None, :]
    return jnp.concatenate(
        [first * cos_here - second * sin_here, second * cos_here + first * sin_here], axis=-1
    )


def unrotate(grads, cosine, sine):
    half = grads.shape[-1] // 2
    first, second = (grads[..., :half], grads[..., half:])
    cos_here = cosine[..., None, :]
    sin_here = sine[..., None, :]
    return jnp.concatenate(
        [first * cos_here + second * sin_here, second * cos_here - first * sin_here], axis=-1
    )


def block_scores(query_block, keys, seg_block, segment, start):
    scores = jnp.einsum(
        "qhd,khd->hqk", query_block, keys, preferred_element_type=jnp.float32
    ) * HEAD_DIM ** (-0.5)
    rows_query = start + jnp.arange(query_block.shape[0], dtype=jnp.int32)
    rows_key = jnp.arange(keys.shape[0], dtype=jnp.int32)
    allowed = (seg_block[:, None] == segment[None, :]) & (rows_key[None, :] <= rows_query[:, None])
    return jnp.where(allowed[None], scores, NEG)


def attention_forward(queries, keys, values, segment, block):
    rows = queries.shape[0]

    def one_block(index):
        start = index * block
        query_block = lax.dynamic_slice_in_dim(queries, start, block, 0)
        seg_block = lax.dynamic_slice_in_dim(segment, start, block, 0)
        scores = block_scores(query_block, keys, seg_block, segment, start)
        top = jnp.max(scores, axis=-1, keepdims=True)
        raised = jnp.exp(scores - top)
        total = jnp.sum(raised, axis=-1, keepdims=True)
        weights = (raised / total).astype(jnp.bfloat16)
        context = jnp.einsum("hqk,khd->qhd", weights, values, preferred_element_type=jnp.float32)
        return (context, top, total)

    context, top, total = lax.map(one_block, jnp.arange(rows // block, dtype=jnp.int32))
    return (context.reshape(queries.shape), top, total)


def attention_backward(queries, keys, values, segment, block, top, total, grad_context):
    rows = queries.shape[0]
    scale = HEAD_DIM ** (-0.5)

    def one_block(carry, index):
        grad_keys, grad_values = carry
        start = index * block
        query_block = lax.dynamic_slice_in_dim(queries, start, block, 0)
        seg_block = lax.dynamic_slice_in_dim(segment, start, block, 0)
        grad_block = lax.dynamic_slice_in_dim(grad_context, start, block, 0)
        scores = block_scores(query_block, keys, seg_block, segment, start)
        weights_f = jnp.exp(scores - top[index]) / total[index]
        weights = weights_f.astype(jnp.bfloat16)
        grad_weights = jnp.einsum(
            "qhd,khd->hqk", grad_block, values, preferred_element_type=jnp.float32
        )
        inner = jnp.sum(weights_f * grad_weights, axis=-1, keepdims=True)
        grad_scores = (weights_f * (grad_weights - inner)).astype(jnp.bfloat16)
        grad_query = (
            jnp.einsum("hqk,khd->qhd", grad_scores, keys, preferred_element_type=jnp.float32)
            * scale
        )
        grad_keys = (
            grad_keys
            + jnp.einsum(
                "hqk,qhd->khd", grad_scores, query_block, preferred_element_type=jnp.float32
            )
            * scale
        )
        grad_values = grad_values + jnp.einsum(
            "hqk,qhd->khd", weights, grad_block, preferred_element_type=jnp.float32
        )
        return ((grad_keys, grad_values), grad_query)

    empty = jnp.zeros(keys.shape, jnp.float32)
    (grad_keys, grad_values), grad_query = lax.scan(
        one_block, (empty, empty), jnp.arange(rows // block, dtype=jnp.int32)
    )
    return (grad_query.reshape(queries.shape), grad_keys, grad_values)


def shards(
    tokens,
    cotangent,
    seq_lengths,
    expert_ids,
    slot_index,
    w_query,
    w_key,
    w_value,
    w_output,
    query_gain,
    key_gain,
    attn_gain,
    moe_gain,
    router,
    w_gate,
    w_up,
    w_down,
):
    rows, width = tokens.shape
    local = w_query.shape[1]
    heads_here = local // HEAD_DIM
    groups = lax.axis_size(EXPERT)
    experts_here = w_gate.shape[0]
    experts_all = experts_here * groups
    capacity = max(2, 3 * rows * TOP // (4 * experts_all))
    block = min(512, rows)
    shape_heads = (rows, heads_here, HEAD_DIM)
    segment, position = layout(seq_lengths, rows)
    cosine, sine = rope_angles(position, HEAD_DIM)
    inputs = tokens.astype(jnp.float32)
    normed, inverse_in = norm_rows(inputs, attn_gain)
    attn_in = normed.astype(jnp.bfloat16)
    query_raw = jnp.dot(attn_in, w_query, preferred_element_type=jnp.float32)
    key_raw = jnp.dot(attn_in, w_key, preferred_element_type=jnp.float32)
    value_raw = jnp.dot(attn_in, w_value, preferred_element_type=jnp.float32)
    query_total, key_total = lax.psum(
        (jnp.sum(query_raw * query_raw, axis=-1), jnp.sum(key_raw * key_raw, axis=-1)), TENSOR
    )
    query_inverse = lax.rsqrt(query_total / width + EPS)[:, None]
    key_inverse = lax.rsqrt(key_total / width + EPS)[:, None]
    queries = rotate(
        (query_raw * query_inverse * query_gain).reshape(shape_heads), cosine, sine
    ).astype(jnp.bfloat16)
    keys = rotate((key_raw * key_inverse * key_gain).reshape(shape_heads), cosine, sine).astype(
        jnp.bfloat16
    )
    values = value_raw.reshape(shape_heads).astype(jnp.bfloat16)
    context, top, total = attention_forward(queries, keys, values, segment, block)
    context_low = context.reshape(rows, local).astype(jnp.bfloat16)
    attn = lax.psum(
        jnp.dot(context_low, w_output, preferred_element_type=jnp.float32).astype(jnp.bfloat16),
        TENSOR,
    ).astype(jnp.float32)
    hidden_in = inputs + attn
    moe_in, inverse_moe = norm_rows(hidden_in, moe_gain)
    router_wide = router.astype(jnp.float32)
    shares = jax.nn.softmax(jnp.dot(moe_in, router_wide, precision=lax.Precision.HIGHEST), axis=-1)
    chosen = expert_ids[:, :, None] == jnp.arange(experts_all, dtype=jnp.int32)[None, None, :]
    gates = jnp.sum(jnp.where(chosen, shares[:, None, :], 0.0), axis=-1)
    kept = slot_index >= 0
    target_slot = jnp.where(
        kept, expert_ids * capacity + slot_index, experts_all * capacity
    ).reshape(-1)
    token_of = (
        jnp.full((experts_all * capacity,), -1, jnp.int32)
        .at[target_slot]
        .set(jnp.repeat(jnp.arange(rows, dtype=jnp.int32), TOP), mode="drop")
    )
    gate_of = (
        jnp.zeros((experts_all * capacity,), jnp.float32)
        .at[target_slot]
        .set(gates.reshape(-1), mode="drop")
    )
    filled = (token_of >= 0)[:, None]
    source_row = jnp.maximum(token_of, 0)
    moe_low = moe_in.astype(jnp.bfloat16)
    send_rows = jnp.where(filled, moe_low[source_row], jnp.zeros((), jnp.bfloat16)).reshape(
        groups, experts_here * capacity, width
    )
    arrived = lax.all_to_all(send_rows, EXPERT, split_axis=0, concat_axis=0, tiled=True)
    arrived = arrived.reshape(groups, experts_here, capacity, width)
    gate_pre = jnp.einsum("secd,edf->secf", arrived, w_gate, preferred_element_type=jnp.float32)
    up_pre = jnp.einsum("secd,edf->secf", arrived, w_up, preferred_element_type=jnp.float32)
    activated = jax.nn.silu(gate_pre)
    hidden = (activated * up_pre).astype(jnp.bfloat16)
    partial_value = jnp.einsum(
        "secf,efd->secd", hidden, w_down, preferred_element_type=jnp.float32
    ).astype(jnp.bfloat16)
    dy_rows = jnp.where(filled, cotangent[source_row], jnp.zeros((), jnp.bfloat16))
    returned = lax.all_to_all(partial_value, EXPERT, split_axis=0, concat_axis=0, tiled=True)
    returned = returned.reshape(experts_all * capacity, width).astype(jnp.float32)
    moe_part = jax.ops.segment_sum(returned * gate_of[:, None], source_row, num_segments=rows)
    moe = lax.psum(moe_part.astype(jnp.bfloat16), TENSOR).astype(jnp.float32)
    row_dots = jnp.sum(dy_rows.astype(jnp.float32) * returned, axis=-1)
    out = (hidden_in + moe).astype(jnp.bfloat16)
    grad_gate = jnp.take(row_dots, target_slot, mode="fill", fill_value=0.0).reshape(rows, TOP)
    grad_shares = jnp.sum(jnp.where(chosen, grad_gate[:, :, None], 0.0), axis=1)
    grad_logits = shares * (grad_shares - jnp.sum(shares * grad_shares, axis=-1, keepdims=True))
    router_back = jnp.einsum("te,de->td", grad_logits, router_wide, precision=lax.Precision.HIGHEST)
    router_part = jnp.einsum("td,te->de", moe_in, grad_logits, precision=lax.Precision.HIGHEST)
    grad_rows = (
        (dy_rows.astype(jnp.float32) * gate_of[:, None])
        .astype(jnp.bfloat16)
        .reshape(groups, experts_here * capacity, width)
    )
    grad_arrived = lax.all_to_all(grad_rows, EXPERT, split_axis=0, concat_axis=0, tiled=True)
    grad_arrived = grad_arrived.reshape(groups, experts_here, capacity, width)
    grad_hidden = jnp.einsum(
        "secd,efd->secf", grad_arrived, w_down, preferred_element_type=jnp.float32
    )
    grad_w_down = jnp.einsum(
        "secf,secd->efd", hidden, grad_arrived, preferred_element_type=jnp.float32
    )
    sigma = jax.nn.sigmoid(gate_pre)
    grad_gate_pre = (grad_hidden * up_pre * sigma * (1.0 + gate_pre * (1.0 - sigma))).astype(
        jnp.bfloat16
    )
    grad_up_pre = (grad_hidden * activated).astype(jnp.bfloat16)
    grad_w_gate = jnp.einsum(
        "secd,secf->edf", arrived, grad_gate_pre, preferred_element_type=jnp.float32
    )
    grad_w_up = jnp.einsum(
        "secd,secf->edf", arrived, grad_up_pre, preferred_element_type=jnp.float32
    )
    grad_in_rows = jnp.einsum(
        "secf,edf->secd", grad_gate_pre, w_gate, preferred_element_type=jnp.float32
    )
    grad_in_rows = (
        grad_in_rows
        + jnp.einsum("secf,edf->secd", grad_up_pre, w_up, preferred_element_type=jnp.float32)
    ).astype(jnp.bfloat16)
    back_rows = lax.all_to_all(
        grad_in_rows.reshape(groups, experts_here * capacity, width),
        EXPERT,
        split_axis=0,
        concat_axis=0,
        tiled=True,
    )
    back_rows = back_rows.reshape(experts_all * capacity, width).astype(jnp.float32)
    moe_back = jax.ops.segment_sum(back_rows, source_row, num_segments=rows)
    grad_moe_in, grad_router_rows = (
        lax.psum((moe_back + router_back).astype(jnp.bfloat16), TENSOR).astype(jnp.float32),
        lax.psum(router_part.astype(jnp.bfloat16), TENSOR).astype(jnp.float32),
    )
    grad_norm_moe, grad_moe_gain = norm_back(hidden_in, inverse_moe, moe_gain, grad_moe_in)
    grad_hidden_in = cotangent.astype(jnp.float32) + grad_norm_moe
    grad_low = grad_hidden_in.astype(jnp.bfloat16)
    grad_w_output = jnp.einsum(
        "tf,td->fd", context_low, grad_low, preferred_element_type=jnp.float32
    )
    grad_context = (
        jnp.einsum("td,fd->tf", grad_low, w_output, preferred_element_type=jnp.float32)
        .astype(jnp.bfloat16)
        .reshape(shape_heads)
    )
    grad_queries, grad_keys, grad_values = attention_backward(
        queries, keys, values, segment, block, top, total, grad_context
    )
    grad_query_normed = unrotate(grad_queries, cosine, sine).reshape(rows, local)
    grad_key_normed = unrotate(grad_keys, cosine, sine).reshape(rows, local)
    query_scaled = grad_query_normed * query_gain
    key_scaled = grad_key_normed * key_gain
    query_inner, key_inner = lax.psum(
        (jnp.sum(query_raw * query_scaled, axis=-1), jnp.sum(key_raw * key_scaled, axis=-1)),
        TENSOR,
    )
    grad_query_raw = (
        query_inverse * query_scaled
        - query_raw * query_inverse * query_inverse * query_inverse * (query_inner / width)[:, None]
    )
    grad_key_raw = (
        key_inverse * key_scaled
        - key_raw * key_inverse * key_inverse * key_inverse * (key_inner / width)[:, None]
    )
    grad_query_gain = jnp.sum(grad_query_normed * query_raw * query_inverse, axis=0)
    grad_key_gain = jnp.sum(grad_key_normed * key_raw * key_inverse, axis=0)
    query_low = grad_query_raw.astype(jnp.bfloat16)
    key_low = grad_key_raw.astype(jnp.bfloat16)
    value_low = grad_values.reshape(rows, local).astype(jnp.bfloat16)
    grad_w_query = jnp.einsum("td,tf->df", attn_in, query_low, preferred_element_type=jnp.float32)
    grad_w_key = jnp.einsum("td,tf->df", attn_in, key_low, preferred_element_type=jnp.float32)
    grad_w_value = jnp.einsum("td,tf->df", attn_in, value_low, preferred_element_type=jnp.float32)
    terms_in = jnp.einsum("tf,df->td", query_low, w_query, preferred_element_type=jnp.float32)
    terms_in = terms_in + jnp.einsum(
        "tf,df->td", key_low, w_key, preferred_element_type=jnp.float32
    )
    terms_in = terms_in + jnp.einsum(
        "tf,df->td", value_low, w_value, preferred_element_type=jnp.float32
    )
    grad_normed = lax.psum(terms_in.astype(jnp.bfloat16), TENSOR).astype(jnp.float32)
    grad_norm_in, grad_attn_gain = norm_back(inputs, inverse_in, attn_gain, grad_normed)
    grad_input = (grad_hidden_in + grad_norm_in).astype(jnp.bfloat16)
    sums = (
        lax.psum_scatter(
            grad_w_query.astype(jnp.bfloat16), EXPERT, scatter_dimension=0, tiled=True
        ).astype(jnp.float32),
        lax.psum_scatter(
            grad_w_key.astype(jnp.bfloat16), EXPERT, scatter_dimension=0, tiled=True
        ).astype(jnp.float32),
        lax.psum_scatter(
            grad_w_value.astype(jnp.bfloat16), EXPERT, scatter_dimension=0, tiled=True
        ).astype(jnp.float32),
        lax.psum_scatter(
            grad_w_output.astype(jnp.bfloat16), EXPERT, scatter_dimension=1, tiled=True
        ).astype(jnp.float32),
        lax.psum_scatter(
            grad_query_gain.astype(jnp.bfloat16), EXPERT, scatter_dimension=0, tiled=True
        ).astype(jnp.float32),
        lax.psum_scatter(
            grad_key_gain.astype(jnp.bfloat16), EXPERT, scatter_dimension=0, tiled=True
        ).astype(jnp.float32),
        lax.psum_scatter(
            grad_attn_gain.astype(jnp.bfloat16), EXPERT, scatter_dimension=0, tiled=True
        ).astype(jnp.float32),
        lax.psum_scatter(
            grad_moe_gain.astype(jnp.bfloat16), EXPERT, scatter_dimension=0, tiled=True
        ).astype(jnp.float32),
        lax.psum_scatter(
            grad_router_rows.astype(jnp.bfloat16), EXPERT, scatter_dimension=0, tiled=True
        ).astype(jnp.float32),
    )
    lows = tuple((item.astype(jnp.bfloat16) for item in sums))
    return (
        out,
        grad_input,
        lows[0],
        lows[1],
        lows[2],
        lows[3],
        lows[4],
        lows[5],
        lows[6],
        lows[7],
        lows[8],
        grad_w_gate.astype(jnp.bfloat16),
        grad_w_up.astype(jnp.bfloat16),
        grad_w_down.astype(jnp.bfloat16),
    )


F32 = jnp.float32
BF = jnp.bfloat16
NN = (((1,), (0,)), ((), ()))
NT = (((1,), (1,)), ((), ()))
TN = (((0,), (0,)), ((), ()))
VMEM_BYTES = 62 * 2**20
COLUMN_TILE = 512
ROW_TILE = 512
QUERY_TILE = 256
EXPERT_STEP = 2
HIDDEN_TILE = 256
LANES = 128


def mul(left, right, dims=NN):
    return lax.dot_general(left, right, dims, preferred_element_type=F32)


def kernel_params():
    return pltpu.CompilerParams(vmem_limit_bytes=VMEM_BYTES)


def whole(shape):
    return pl.BlockSpec(shape, lambda i: (0,) * len(shape), pipeline_mode=pl.Buffered(1))


def softmax_block(queries, keys, seg_rows, seg_columns, start, scale):
    scores = mul(queries, keys, NT) * scale
    rows = start + lax.broadcasted_iota(jnp.int32, scores.shape, 0)
    columns = lax.broadcasted_iota(jnp.int32, scores.shape, 1)
    allowed = (seg_rows == seg_columns) & (columns <= rows)
    scores = jnp.where(allowed, scores, NEG)
    raised = jnp.exp(scores - jnp.max(scores, axis=-1, keepdims=True))
    return raised * (1.0 / jnp.sum(raised, axis=-1, keepdims=True))


ANYWHERE = pl.BlockSpec(memory_space=pl.ANY)


def front_kernel(tokens_ref, gain_ref, wq_ref, wk_ref, wv_ref, *refs):
    low_ref, inverse_ref, q_ref, k_ref, v_ref, sums_ref = refs[-6:]
    rows = tokens_ref[...].astype(F32)
    inverse = lax.rsqrt(jnp.mean(rows * rows, axis=1, keepdims=True) + EPS)
    low = (rows * inverse * gain_ref[...]).astype(BF)
    low_ref[...] = low
    inverse_ref[...] = inverse
    sums = []
    for w_ref, out_ref in ((wq_ref, q_ref), (wk_ref, k_ref)):
        raw = mul(low, w_ref[...])
        out_ref[...] = raw
        sums.append(jnp.sum(raw * raw, axis=1, keepdims=True))
    v_ref[...] = mul(low, wv_ref[...]).astype(BF)
    sums_ref[...] = jnp.concatenate(sums, axis=1)


def front_call(tokens, gain, w_query, w_key, w_value, waits):
    rows, width = tokens.shape
    local = w_query.shape[1]
    tile = min(HIDDEN_TILE, rows)
    row = lambda c: pl.BlockSpec((tile, c), lambda i: (i, 0))
    shape = jax.ShapeDtypeStruct
    return pl.pallas_call(
        front_kernel,
        grid=(rows // tile,),
        in_specs=[row(width), whole((1, width))] + [whole(w_query.shape)] * 3 + [ANYWHERE] * len(waits),
        out_specs=[row(width), row(1)] + [row(local)] * 3 + [row(2)],
        out_shape=[shape((rows, width), BF), shape((rows, 1), F32)]
        + [shape((rows, local), F32)] * 2
        + [shape((rows, local), BF), shape((rows, 2), F32)],
        compiler_params=kernel_params(),
        cost_estimate=pl.CostEstimate(
            flops=6 * rows * width * local, bytes_accessed=4 * rows * width + 6 * width * local, transcendentals=0
        ),
        name="front_rows",
    )(tokens, gain, w_query, w_key, w_value, *waits)


def attention_kernel(
    q_ref, k_ref, v_ref, qi_ref, ki_ref, qg_ref, kg_ref, cos_ref, sin_ref, row_ref, col_ref,
    qh_ref, kh_ref, ctx_ref,
):
    rows, size = q_ref.shape
    tile = min(QUERY_TILE, rows)
    for raw, inverse, gain, low in ((q_ref, qi_ref, qg_ref, qh_ref), (k_ref, ki_ref, kg_ref, kh_ref)):
        normed = raw[...] * inverse[...] * gain[...]
        turned = normed * cos_ref[...] + pltpu.roll(normed, size // 2, 1) * sin_ref[...]
        low[...] = turned.astype(BF)
    for start in range(0, rows, tile):
        end = start + tile
        weights = softmax_block(
            qh_ref[start:end], kh_ref[:end], row_ref[start:end], col_ref[:, :end], start, size**-0.5
        )
        ctx_ref[start:end] = mul(weights.astype(BF), v_ref[:end]).astype(BF)


def attention_back_kernel(
    q_ref, k_ref, v_ref, qi_ref, ki_ref, qg_ref, kg_ref, cos_ref, sin_ref, row_ref, col_ref,
    qh_ref, kh_ref, dctx_ref, *rest,
):
    dq_ref, dk_ref, dv_ref, inner_ref, dqg_ref, dkg_ref, dq_total, dk_total, dv_total = rest[-9:]
    rows, size = q_ref.shape
    scale = size**-0.5
    tile = min(QUERY_TILE, rows)
    dk_total[...] = jnp.zeros_like(dk_total)
    dv_total[...] = jnp.zeros_like(dv_total)
    for start in range(0, rows, tile):
        end = start + tile
        keys = kh_ref[:end]
        weights = softmax_block(
            qh_ref[start:end], keys, row_ref[start:end], col_ref[:, :end], start, scale
        )
        grad_weights = mul(dctx_ref[start:end], v_ref[:end], NT)
        inner = jnp.sum(weights * grad_weights, axis=-1, keepdims=True)
        grad_scores = (weights * (grad_weights - inner)).astype(BF)
        dq_total[start:end] = mul(grad_scores, keys) * scale
        dk_total[:end] += mul(grad_scores, qh_ref[start:end], TN) * scale
        dv_total[:end] += mul(weights.astype(BF), dctx_ref[start:end], TN)
    dv_ref[...] = dv_total[...].astype(BF)
    inners = []
    for total, raw, inverse, gain, out, dgain in (
        (dq_total, q_ref, qi_ref, qg_ref, dq_ref, dqg_ref),
        (dk_total, k_ref, ki_ref, kg_ref, dk_ref, dkg_ref),
    ):
        grad = total[...]
        grad = grad * cos_ref[...] - pltpu.roll(grad, size // 2, 1) * sin_ref[...]
        values = raw[...]
        dgain[...] = jnp.sum(grad * values * inverse[...], axis=0, keepdims=True)
        scaled = grad * gain[...]
        inners.append(jnp.sum(values * scaled, axis=1, keepdims=True))
        out[...] = scaled
    inner_ref[0] = jnp.concatenate(inners, axis=1)


def head_specs(rows):
    head = pl.BlockSpec((rows, HEAD_DIM), lambda h: (0, h))
    gain = pl.BlockSpec((1, HEAD_DIM), lambda h: (0, h))
    column = whole((rows, 1))
    table = whole((rows, HEAD_DIM))
    return head, gain, [head, head, head, column, column, gain, gain, table, table, column, whole((1, rows))]


def attention_call(operands, rows, local):
    head, gain, specs = head_specs(rows)
    heads = local // HEAD_DIM
    return pl.pallas_call(
        attention_kernel,
        grid=(heads,),
        in_specs=specs,
        out_specs=[head] * 3,
        out_shape=[jax.ShapeDtypeStruct((rows, local), BF)] * 3,
        compiler_params=kernel_params(),
        cost_estimate=pl.CostEstimate(
            flops=2 * rows * rows * local, bytes_accessed=12 * rows * local, transcendentals=rows * rows * heads // 2
        ),
        name="attention_rows",
    )(*operands)


def attention_back_call(operands, rows, local, waits=()):
    head, gain, specs = head_specs(rows)
    heads = local // HEAD_DIM
    return pl.pallas_call(
        attention_back_kernel,
        grid=(heads,),
        in_specs=specs + [head] * 3 + [ANYWHERE] * len(waits),
        out_specs=[head] * 3 + [pl.BlockSpec((1, rows, 2), lambda h: (h, 0, 0)), gain, gain],
        out_shape=[jax.ShapeDtypeStruct((rows, local), F32)] * 2
        + [jax.ShapeDtypeStruct((rows, local), BF), jax.ShapeDtypeStruct((heads, rows, 2), F32)]
        + [jax.ShapeDtypeStruct((1, local), F32)] * 2,
        scratch_shapes=[pltpu.VMEM((rows, HEAD_DIM), F32)] * 3,
        compiler_params=kernel_params(),
        cost_estimate=pl.CostEstimate(
            flops=8 * rows * rows * local, bytes_accessed=24 * rows * local, transcendentals=rows * rows * heads // 2
        ),
        name="attention_rows_back",
    )(*operands, *waits)


def hidden_kernel(pieces, core_ref, tokens_ref, gain_ref, *refs):
    ctx_refs, w_ref = refs[:pieces], refs[pieces]
    hidden_ref, low_ref, inverse_ref = refs[pieces + 1 :]
    local = ctx_refs[0].shape[1]
    half = local // 2
    near = pl.ds(pl.multiple_of(core_ref[0] * half, half), half)
    far = pl.ds(pl.multiple_of((1 - core_ref[0]) * half, half), half)
    total = tokens_ref[...].astype(F32) + mul(ctx_refs[0][...], w_ref[:local])
    for number in range(1, pieces):
        mine = local + (number - 1) * half
        other = mine + (pieces - 1) * half
        total = total + mul(ctx_refs[number][:, near], w_ref[mine : mine + half])
        total = total + mul(ctx_refs[number][:, far], w_ref[other : other + half])
    inverse = lax.rsqrt(jnp.mean(total * total, axis=1, keepdims=True) + EPS)
    hidden_ref[...] = total
    low_ref[...] = (total * inverse * gain_ref[...]).astype(BF)
    inverse_ref[...] = inverse


def hidden_call(core, tokens, gain, context, weights):
    rows, width = tokens.shape
    tile = min(HIDDEN_TILE, rows)
    row = lambda c: pl.BlockSpec((tile, c), lambda i: (i, 0))
    return pl.pallas_call(
        functools.partial(hidden_kernel, len(context)),
        grid=(rows // tile,),
        in_specs=[pl.BlockSpec(memory_space=pltpu.SMEM), row(width), whole((1, width))]
        + [row(context[0].shape[1])] * len(context)
        + [whole(weights.shape)],
        out_specs=[row(width), row(width), row(1)],
        out_shape=[
            jax.ShapeDtypeStruct((rows, width), F32),
            jax.ShapeDtypeStruct((rows, width), BF),
            jax.ShapeDtypeStruct((rows, 1), F32),
        ],
        compiler_params=kernel_params(),
        cost_estimate=pl.CostEstimate(
            flops=2 * rows * width * width, bytes_accessed=10 * rows * width + 2 * width * width, transcendentals=0
        ),
        name="hidden_rows",
    )(core, tokens, gain, *context, weights)


def rows_kernel(arrays, first_number, each_device, added, waits, *refs):
    parts = 2
    core_ref, router_ref = refs[:2]
    x_refs, dy_refs, carried_refs = refs[2:4], refs[4:6], refs[6:8]
    w_refs = refs[8 : 8 + arrays]
    rest = refs[8 + arrays :]
    if added:
        before, rest = rest[:4], rest[4:]
    rest = rest[waits:]
    moe_refs, dx_refs = rest[:2], rest[2:4]
    kept_ref, share_ref, held, moe, dx, gates, dots, sems, before_sems = rest[4:]
    step = pl.program_id(0)
    slot = lax.rem(step, 2)
    blocks, _, own, width = x_refs[0].shape
    rows = blocks * own
    experts = held.shape[1]

    def take(ref, first, count):
        part = ref[first // own : (first + count) // own, 0]
        return part.reshape(count, part.shape[-1])

    hid = held.shape[2] // 3
    tile = min(ROW_TILE, rows)
    each = w_refs[0].shape[0] // experts
    sets = each * arrays

    def source(number):
        return w_refs[number // each].at[pl.ds(number % each * experts, experts)]

    def fetch(index, place):
        for number in range(sets):

            @pl.when(index == number)
            def _():
                pltpu.make_async_copy(source(number), held.at[place], sems.at[place]).start()

    @pl.when(step == 0)
    def _():
        fetch(0, 0)
        earlier = []
        if added:
            for number, place in enumerate((*moe_refs, *dx_refs)):
                earlier.append(pltpu.make_async_copy(before[number], place, before_sems.at[number]))
                earlier[-1].start()
        for number in range(parts):
            here = slice(number * rows, (number + 1) * rows)
            logits = mul(take(x_refs[number], 0, rows), router_ref[...])
            raised = jnp.exp(logits - jnp.max(logits, axis=1, keepdims=True))
            shares = raised / jnp.sum(raised, axis=1, keepdims=True)
            if number == 0:
                share_ref[...] = shares
            gates[here] = shares * take(carried_refs[number], 0, rows).astype(F32)
        for copy in earlier:
            copy.wait()
        if added:
            for number in range(parts):
                here = slice(number * rows, (number + 1) * rows)
                moe[here] = moe_refs[number][...].astype(F32)
                dx[here] = dx_refs[number][:, :width].astype(F32)
                dots[here] = dx_refs[number][:, width:].astype(F32)
        else:
            moe[...] = jnp.zeros_like(moe)
            dx[...] = jnp.zeros_like(dx)
            dots[...] = jnp.zeros_like(dots)

    @pl.when(step + 1 < sets)
    def _():
        fetch(step + 1, 1 - slot)

    pltpu.make_async_copy(source(0), held.at[slot], sems.at[slot]).wait()
    for one in range(experts):
        base = one * 3 * hid
        chip = lax.rem(step, each) * experts + one
        index = (chip * 2 + core_ref[0]) * each_device + first_number + step // each
        for first in range(0, parts * rows, tile):
            here = slice(first, first + tile)
            both = mul(take(x_refs[first // rows], first % rows, tile), held[slot, one, hid:], NT)
            back = mul(take(dy_refs[first // rows], first % rows, tile), held[slot, one, :hid], NT)
            pre, up = both[:, :hid], both[:, hid:]
            sigma = 0.5 * jnp.tanh(0.5 * pre) + 0.5
            active = pre * sigma
            chosen = lax.broadcasted_iota(jnp.int32, (tile, gates.shape[1]), 1) == index
            gate = jnp.sum(jnp.where(chosen, gates[here], 0.0), axis=1, keepdims=True)
            column = lax.broadcasted_iota(jnp.int32, (tile, LANES), 1) == index
            hidden = active * up
            dot = jnp.sum(hidden * back, axis=1, keepdims=True)
            dots[here] += jnp.where(column, dot, 0.0)
            back = back * gate
            kept_ref[here, base : base + hid] = (hidden * gate).astype(BF)
            kept_ref[here, base + hid : base + 2 * hid] = (
                back * up * sigma * (1.0 + pre * (1.0 - sigma))
            ).astype(BF)
            kept_ref[here, base + 2 * hid : base + 3 * hid] = (back * active).astype(BF)
    for first in range(0, width, COLUMN_TILE):
        here = slice(first, first + COLUMN_TILE)
        total = moe[:, here]
        for one in range(experts):
            base = one * 3 * hid
            total = total + mul(kept_ref[:, base : base + hid], held[slot, one, :hid, here])
        moe[:, here] = total
        total = dx[:, here]
        for one in range(experts):
            base = one * 3 * hid
            total = total + mul(kept_ref[:, base + hid : base + 3 * hid], held[slot, one, hid:, here])
        dx[:, here] = total

    @pl.when(step == sets - 1)
    def _():
        for number in range(parts):
            here = slice(number * rows, (number + 1) * rows)
            moe_refs[number][...] = moe[here].astype(BF)
            dx_refs[number][:, :width] = dx[here].astype(BF)
            dx_refs[number][:, width:] = dots[here].astype(BF)


def rows_call(core, router, moe_in, cotangent, carried, place, weights, first_number, each_device, before=None, waits=()):
    blocks, _, own, width = moe_in[0].shape
    rows = blocks * own
    parts = 2
    chips, depth, _ = weights[0].shape
    experts = EXPERT_STEP
    sets = len(weights) * chips // experts
    number = router.shape[1]
    full = whole((rows, width))
    wide = experts * depth
    wider = whole((rows, width + LANES))
    operands = [core, router, *moe_in, *cotangent, *carried, *weights]

    def half(columns):
        return pl.BlockSpec((blocks, 1, own, columns), lambda i: (0, place, 0, 0), pipeline_mode=pl.Buffered(1))

    specs = [pl.BlockSpec(memory_space=pltpu.SMEM), whole(router.shape)] + [half(width)] * 4 + [half(number)] * 2
    specs += [pl.BlockSpec(memory_space=pl.ANY)] * len(weights)
    if before is not None:
        operands += before
        specs += [ANYWHERE] * 4
    operands += waits
    specs += [ANYWHERE] * len(waits)
    return pl.pallas_call(
        functools.partial(rows_kernel, len(weights), first_number, each_device, before is not None, len(waits)),
        grid=(sets,),
        in_specs=specs,
        out_specs=[full] * 2
        + [wider] * 2
        + [pl.BlockSpec((parts * rows, wide), lambda i: (0, i)), whole((rows, number))],
        out_shape=[jax.ShapeDtypeStruct((rows, width), BF)] * 2
        + [jax.ShapeDtypeStruct((rows, width + LANES), BF)] * 2
        + [
            jax.ShapeDtypeStruct((parts * rows, sets * wide), BF),
            jax.ShapeDtypeStruct((rows, number), F32),
        ],
        scratch_shapes=[
            pltpu.VMEM((2, experts, depth, width), BF),
            pltpu.VMEM((parts * rows, width), F32),
            pltpu.VMEM((parts * rows, width), F32),
            pltpu.VMEM((parts * rows, number), F32),
            pltpu.VMEM((parts * rows, LANES), F32),
            pltpu.SemaphoreType.DMA((2,)),
            pltpu.SemaphoreType.DMA((4,)),
        ],
        compiler_params=kernel_params(),
        cost_estimate=pl.CostEstimate(
            flops=4 * parts * rows * width * wide * sets,
            bytes_accessed=8 * parts * rows * width + 2 * sets * wide * (parts * rows + width),
            transcendentals=parts * rows * wide * sets // 3,
        ),
        name="expert_rows",
    )(*operands)


def weight_grads_kernel(sides, halves, outs, added, skipped, order_ref, *refs):
    parts = sides * halves
    x_refs, dy_refs = refs[:parts], refs[parts : 2 * parts]
    kept_refs = refs[2 * parts : 2 * parts + 2 * halves]
    add_refs = refs[2 * parts + 2 * halves : 2 * parts + 2 * halves + added]
    out_refs, turned = refs[2 * parts + 2 * halves + added + skipped : -1], refs[-1]
    hid = turned.shape[0] // 6
    span = kept_refs[0].shape[0]
    rows = span // sides

    @pl.when(pl.program_id(0) == 0)
    def _():
        for h in range(halves):
            there = slice(h * span, (h + 1) * span)
            for one in range(2):
                kept_ref = kept_refs[2 * h + one]
                turned[one * hid : (one + 1) * hid, there] = kept_ref[:, :hid].T
                place = 2 * hid + one * 2 * hid
                turned[place : place + 2 * hid, there] = kept_ref[:, hid:].T

    def total(first, last, refs):
        return sum(
            mul(turned[first:last, p * rows : (p + 1) * rows], ref[:, 0].reshape(rows, ref.shape[-1]))
            for p, ref in enumerate(refs)
        )

    down = total(0, 2 * hid, dy_refs)
    both = total(2 * hid, 6 * hid, x_refs)
    for one in range(2):
        value = jnp.concatenate(
            [down[one * hid : (one + 1) * hid], both[one * 2 * hid : (one + 1) * 2 * hid]], axis=0
        )
        if outs == 1:
            out_refs[0][one] = value.astype(BF)
            continue
        middle = value.shape[0] // 2
        for number, part in enumerate((value[:middle], value[middle:])):
            if added and number == one:
                part = part + add_refs[one][...].astype(F32)
            out_refs[2 * one + number][...] = part.astype(BF)


def weight_grads_call(moe_in, cotangent, kept, order, depth, addends=(), waits=(), pair=None, into=None):
    blocks, halves, own, width = moe_in[0].shape
    sides = len(moe_in)
    tile = COLUMN_TILE
    span = kept[0].shape[0]
    parts = [(h, side) for h in range(halves) for side in range(sides)]

    def column(h):
        return pl.BlockSpec((blocks, 1, own, tile), lambda i, order: (0, h, 0, i))

    def expert(one):
        return pl.BlockSpec((span, depth), lambda i, order: (0, order[one]), pipeline_mode=pl.Buffered(1))

    operands = [moe_in[side] for _, side in parts] + [cotangent[side] for _, side in parts]
    operands += [kept[h] for h in range(halves) for _ in range(2)]
    specs = [column(h) for h, _ in parts] * 2 + [expert(one) for _ in range(halves) for one in range(2)]
    operands += addends
    specs += [pl.BlockSpec((addend.shape[0], tile), lambda i, order: (0, i)) for addend in addends]
    aliases = {}
    if into is not None:
        waits = [into, *waits]
        aliases = {1 + len(operands): 0}
    if pair is None:
        outs = 4
        out_specs = [pl.BlockSpec((depth // 2, tile), lambda i, order: (0, i))] * 4
        out_shape = [jax.ShapeDtypeStruct((depth // 2, width), BF)] * 4
    else:
        outs = 1
        out_specs = pl.BlockSpec((2, depth, tile), lambda i, order: (pair, 0, i))
        out_shape = jax.ShapeDtypeStruct((kept[0].shape[1] // depth, depth, width), BF)
    return pl.pallas_call(
        functools.partial(weight_grads_kernel, sides, halves, outs, len(addends), len(waits)),
        grid_spec=pltpu.PrefetchScalarGridSpec(
            num_scalar_prefetch=1,
            grid=(width // tile,),
            in_specs=specs + [ANYWHERE] * len(waits),
            out_specs=out_specs,
            scratch_shapes=[pltpu.VMEM((2 * depth, halves * span), BF)],
        ),
        out_shape=out_shape,
        input_output_aliases=aliases,
        compiler_params=kernel_params(),
        cost_estimate=pl.CostEstimate(
            flops=4 * halves * span * width * depth,
            bytes_accessed=4 * halves * span * width + 8 * depth * width,
            transcendentals=0,
        ),
        name="expert_weight_grads",
    )(order, *operands, *waits)


def swap(values, bit):
    size = lax.axis_size(EXPERT)
    return lax.ppermute(values, EXPERT, [(i, i ^ bit) for i in range(size)])


def plus(left, right):
    return (left.astype(F32) + right.astype(F32)).astype(BF)


def relative_columns(values):
    here = lax.axis_index(EXPERT)
    size = lax.axis_size(EXPERT)
    span = values.shape[1] // size
    order = [*range(0, size, 2), *range(1, size, 2)]
    return jnp.concatenate(
        [lax.dynamic_slice_in_dim(values, (here ^ r) * span, span, 1) for r in order], axis=1
    )


def block_terms(values):
    rows = values.shape[0] // 4
    mine, to_two, to_four, across = (values[n * rows : (n + 1) * rows] for n in range(4))
    return (across[: rows // 2], across[rows // 2 :]), to_four, to_two, mine


def beside(terms, via):
    _, to_four, to_two, _ = terms
    middle = to_four.shape[0] // 2
    return (
        jnp.concatenate([plus(to_four[:middle], via[0]), to_four[middle:]], axis=0),
        jnp.concatenate([to_two[:middle], plus(to_two[middle:], via[1])], axis=0),
    )


def join(*values):
    return lax.optimization_barrier(values)


def scatter_tensor(values):
    return lax.psum_scatter(values, TENSOR, scatter_dimension=0, tiled=True)


HALVES = 2


def shards_near(
    tokens, cotangent, seq_lengths, expert_ids, slot_index, w_query, w_key, w_value, w_output,
    query_gain, key_gain, attn_gain, moe_gain, router, w_gate, w_up, w_down,
):
    rows, width = tokens.shape
    local = w_query.shape[1]
    groups = lax.axis_size(EXPERT)
    n_tensor = lax.axis_size(TENSOR)
    here = lax.axis_index(EXPERT)
    layer = lax.axis_index(TENSOR)
    experts_here, hid = w_gate.shape[0], w_gate.shape[2]
    experts_all = experts_here * groups
    own_rows = rows // n_tensor
    own = lambda array: lax.dynamic_slice_in_dim(array, layer * own_rows, own_rows, 0)
    view = lambda array: array.reshape(n_tensor, HALVES, own_rows // HALVES, array.shape[-1])
    half = range(HALVES)

    chips = groups // 2
    sides_of = [[2 * chip + core for chip in range(chips)] for core in (0, 1)]
    core = lax.rem(here, 2)

    core_rows = local // 2
    w_half = lax.dynamic_slice_in_dim(w_output, core * core_rows, core_rows, 0)
    w_mine = [swap_tensor(w_half, bits) for bits in (1, 2)]

    def pack(gate, up, down):
        return jnp.concatenate([down, gate.T, up.T], axis=0)

    def spread(value):
        return lax.all_gather(value, EXPERT, axis_index_groups=sides_of)

    depth = 3 * hid
    packed = [pack(w_gate[j], w_up[j], w_down[j]) for j in range(experts_here)]
    weights = [spread(packed[0])]
    number = jnp.arange(experts_all, dtype=jnp.int32)
    carried = (expert_ids[:, :, None] == number) & (slot_index >= 0)[:, :, None]
    carried = jnp.sum(carried.astype(BF), axis=1)
    segment, position = layout(seq_lengths, rows)
    cosine, sine = rope_angles(position, HEAD_DIM)
    cos_table = jnp.concatenate([cosine, cosine], axis=1)
    sin_table = jnp.concatenate([-sine, sine], axis=1)
    attn_in, inverse_in, query_raw, key_raw, values, totals = front_call(
        tokens, attn_gain[None], w_query, w_key, w_value, [*packed, cos_table, sin_table]
    )
    total = sum_small(totals.T.reshape(-1, LANES)).reshape(2, rows)
    total, w_mine[0], w_mine[1] = join(total, *w_mine)
    w_mine.append(swap_tensor(w_mine[1], 1))
    query_inverse = lax.rsqrt(total[0] / width + EPS)[:, None]
    key_inverse = lax.rsqrt(total[1] / width + EPS)[:, None]
    operands = [
        query_raw, key_raw, values, query_inverse, key_inverse, query_gain[None], key_gain[None],
        cos_table, sin_table, segment[:, None], segment[None],
    ]
    queries, keys, context = attention_call(operands, rows, local)
    far_context = swap_tensor(context, 2)
    near_context = swap_tensor(context, 1)
    packed[1], w_mine[2], context = join(packed[1], w_mine[2], context)
    weights.append(spread(packed[1]))
    near_context, far_context, *w_mine = join(near_context, far_context, *w_mine)
    contexts = [context, near_context, far_context, swap_tensor(far_context, 1)]
    w_mine = jnp.concatenate(w_mine, axis=0)
    w_all = jnp.concatenate([w_output, w_mine, swap(w_mine, 1)], axis=0)
    carried_later, cotangent_later, contexts[0] = lax.optimization_barrier((carried, cotangent, contexts[0]))
    carried_sides = [view(carried), view(swap(carried_later, 1))]
    cotangent_sides = [view(cotangent), view(swap(cotangent_later, 1))]
    hidden, moe_low, inverse_moe = hidden_call(core[None], tokens, moe_gain[None], contexts, w_all)
    sides = [view(moe_low), view(swap(moe_low, 1))]
    router_wide = router.astype(F32)
    calls, kept, shares = [None, None], [{}, {}], [None, None]

    def run(h, j, *waits):
        before = None if calls[h] is None else calls[h][:4]
        calls[h] = rows_call(
            core[None], router, sides, cotangent_sides, carried_sides, h, [weights[j]], j, experts_here, before, waits
        )
        kept[h][j] = calls[h][4]
        shares[h] = calls[h][5]

    def send_back(h):
        terms = plus(calls[h][2], swap(calls[h][3], 1))
        return terms, scatter_tensor(terms)

    chip = here // 2

    def part(j, first, second, *rest, **more):
        order = jnp.stack([first, second]).astype(jnp.int32)
        return weight_grads_call(
            sides, cotangent_sides, [kept[h][j] for h in half], order, depth, *rest, **more
        )

    def send(terms, bits):
        return [swap(term, bit) for term, bit in zip(terms, bits)]

    run(0, 0)
    run(1, 0, calls[0][4])
    *far, mine_low, mine_high = part(0, chip ^ 3, chip)
    via = send(far, (2, 4))
    run(0, 1, *far)
    *calls[0], via[0], via[1] = join(*calls[0], *via)
    kept[0][1] = calls[0][4]
    terms, sums_first = send_back(0)
    run(1, 1, terms)
    *calls[1], sums_first = join(*calls[1], sums_first)
    kept[1][1] = calls[1][4]
    terms, sums_second = send_back(1)
    near = part(0, chip ^ 2, chip ^ 1, via, [terms])
    near_low = send(near[::2], (4, 2))
    second = part(1, 0 * chip, 0 * chip + 1, (), [near[0]], pair=0)
    sums_second, second, attn_in, *moe_terms = join(sums_second, second, attn_in, *calls[0][:2], *calls[1][:2])
    moe_terms = [plus(moe_terms[2 * h], swap(moe_terms[2 * h + 1], 1)) for h in half]
    moe_terms = jnp.stack([term.reshape(n_tensor, -1, width) for term in moe_terms], axis=1).reshape(rows, width)
    sums = jnp.concatenate([sums_first, sums_second], axis=0)
    dshares = sums[:, width : width + experts_all].astype(F32) * own(carried).astype(F32)
    share = jnp.concatenate(
        [lax.dynamic_slice_in_dim(item, layer * (own_rows // HALVES), own_rows // HALVES, 0) for item in shares], axis=0
    )
    hidden_own, inverse_own = own(hidden), own(inverse_moe)
    moe_in = hidden_own * inverse_own * moe_gain
    dlogits = share * (dshares - jnp.sum(share * dshares, axis=-1, keepdims=True))
    router_back = jnp.einsum("te,de->td", dlogits, router_wide, precision=lax.Precision.HIGHEST)
    grad_norm_moe, grad_moe_gain = norm_back(
        hidden_own, inverse_own, moe_gain, sums[:, :width].astype(F32) + router_back
    )
    grad_hidden = own(cotangent).astype(F32) + grad_norm_moe
    grad_low = grad_hidden.astype(BF)

    by_head = mul(grad_low, w_all, NT).astype(BF)
    core_columns = local // 2
    grad_context = jnp.zeros((rows, local), BF)
    for bits in range(n_tensor):
        if bits == 0:
            came = by_head[:, :local]
        else:
            begin = local + (bits - 1) * core_columns
            mine = by_head[:, begin : begin + core_columns]
            begin += (n_tensor - 1) * core_columns
            other = by_head[:, begin : begin + core_columns]
            lower = jnp.where(core == 0, mine, other)
            upper = jnp.where(core == 0, other, mine)
            came = swap_tensor(jnp.concatenate([lower, upper], axis=1), bits)
        grad_context = lax.dynamic_update_slice_in_dim(grad_context, came, (layer ^ bits) * own_rows, 0)
    heads_own = jnp.concatenate([own(item) for item in contexts], axis=1)
    output_grads = mul(relative_columns(grad_low), heads_own, TN).astype(BF)
    output_grads = [output_grads[: width // 2], output_grads[width // 2 :]]
    attn_relative = relative_columns(attn_in)
    grad_context, moe_terms, attn_relative, *output_grads = join(
        grad_context, moe_terms, attn_relative, *output_grads
    )
    moe = scatter_tensor(moe_terms)
    came = swap(output_grads[1], 1)
    back = attention_back_call(
        operands + [queries, keys, grad_context], rows, local, [output_grads[1]]
    )
    *back, came, near_low[0], near_low[1] = join(*back, came, *near_low)
    near_high = send(near[1::2], (4, 2))
    dq, dk, value_low, inner, grad_query_gain, grad_key_gain = back
    inner = jnp.sum(inner, axis=0).T
    inner = sum_small(inner.reshape(-1, LANES)).reshape(inner.shape)
    output_grads = block_terms(plus(output_grads[0], came))
    output_via = send(output_grads[0], (2, 4))
    second = part(1, 0 * chip + 2, 0 * chip + 3, (), [inner], pair=1, into=second)
    inner, moe, second, *output_via, near_high[0], near_high[1] = join(inner, moe, second, *output_via, *near_high)
    grads_one = lax.psum_scatter(
        second.reshape(-1, width), EXPERT, scatter_dimension=0, axis_index_groups=sides_of, tiled=True
    )
    out_own = (hidden_own + moe.astype(F32)).astype(BF)
    came = exchange(out_own, out_own)

    def raw_grad(scaled, raw, inverse, total):
        return (inverse * scaled - raw * inverse * inverse * inverse * (total / width)[:, None]).astype(BF)

    query_low = raw_grad(dq, query_raw, query_inverse, inner[0])
    key_low = raw_grad(dk, key_raw, key_inverse, inner[1])
    lows = jnp.concatenate([query_low, key_low, value_low], axis=1)
    wide = jnp.concatenate([w_query, w_key, w_value], axis=1)
    terms_in = mul(lows, wide, NT).astype(BF)
    def expert_outputs(grads):
        return grads[hid : 2 * hid].T, grads[2 * hid :].T, grads[:hid]

    outputs_zero = jnp.concatenate([
        (mine.astype(F32) + near[0].astype(F32) + near[1].astype(F32)).astype(BF)
        for mine, near in ((mine_low, near_low), (mine_high, near_high))], axis=0)
    outputs_zero = list(expert_outputs(outputs_zero))
    output_near = send(beside(output_grads, output_via), (4, 2))
    *came, terms_in, lows = join(*came, terms_in, lows)
    out_above, out_below = [from_above(came)], [from_below(came)]
    chunk = lambda place: lax.dynamic_slice_in_dim(terms_in, jnp.clip(place, 0, n_tensor - 1) * own_rows, own_rows, 0)
    sum_above = sum_below = jnp.zeros((), BF)
    for step in range(1, n_tensor):
        came = exchange(
            jnp.where(
                layer >= n_tensor - step, plus(chunk(layer - n_tensor + step), sum_above), out_above[-1]
            ),
            jnp.where(layer < step, plus(chunk(layer + n_tensor - step), sum_below), out_below[-1]),
        )
        if step == 1:
            grad_attn_gain = jnp.sum(terms_in.astype(F32) * tokens.astype(F32) * inverse_in, axis=0)
            router_part = jnp.einsum("td,te->de", moe_in, dlogits, precision=lax.Precision.HIGHEST)
            own_width, span = width // groups, local // groups
            spread_gain = lambda gain: jnp.pad(
                gain.reshape(groups, span), ((0, 0), (0, own_width - span))
            ).reshape(width, 1)
            small = jnp.concatenate([
                router_part, grad_moe_gain[:, None], grad_attn_gain[:, None],
                spread_gain(grad_query_gain), spread_gain(grad_key_gain)], axis=1).astype(BF)
            small = jnp.pad(small, ((0, 0), (0, LANES - small.shape[1])))
            blocks = jnp.concatenate([
                mul(attn_relative, lows, TN).astype(BF), relative_columns(small.T).T], axis=1)
            blocks = [blocks[: width // 2], blocks[width // 2 :]]
            *came, blocks[0], blocks[1] = join(*came, *blocks)
            blocks_came = swap(blocks[1], 1)
        elif step == 2:
            came[0], came[1], blocks_came, *outputs_zero = join(*came, blocks_came, *outputs_zero)
            blocks = block_terms(plus(blocks[0], blocks_came))
            via = send(blocks[0], (2, 4))
        else:
            *came, via[0], via[1] = join(*came, *via)
        above, below = from_above(came), from_below(came)
        sum_above = jnp.where(layer == n_tensor - 1, 0, above)
        sum_below = jnp.where(layer == 0, 0, below)
        if step < n_tensor - 1:
            out_above.append(above)
            out_below.append(below)
    grad_normed = own(terms_in).astype(F32) + sum_above.astype(F32) + sum_below.astype(F32)
    out = end_line(out_own, out_above, out_below)

    grad_norm_in, _ = norm_back(own(tokens).astype(F32), own(inverse_in), attn_gain, grad_normed)
    grad_input = (grad_hidden + grad_norm_in).astype(BF)
    input_above, input_below = [grad_input], [grad_input]
    for step in range(1, n_tensor):
        came = exchange(input_above[-1], input_below[-1])
        if step == 1:
            near = send(beside(blocks, via), (4, 2))
            *came, output_near[0], output_near[1] = join(*came, *output_near)
        if step == 2:
            *came, near[0], near[1], grads_one = join(*came, *near, grads_one)
        input_above.append(from_above(came))
        input_below.append(from_below(came))
    projections = sum((item.astype(F32) for item in near), blocks[3].astype(F32))
    small = projections[:, 3 * local :]
    projections = projections[:, : 3 * local].astype(BF)
    by_index = sum((item.astype(F32) for item in output_near), output_grads[3].astype(F32))
    grad_w_output, shared = by_index[:, :local], small
    for bits in range(1, n_tensor):
        terms = jnp.concatenate([by_index[:, bits * local : (bits + 1) * local], small], axis=1)
        came = swap_tensor(terms.astype(BF), bits).astype(F32)
        grad_w_output, shared = grad_w_output + came[:, :local], shared + came[:, local:]
    grad_w_output = grad_w_output.T
    grad_input = end_line(grad_input, input_above[1:], input_below[1:])

    gains = small[:span, experts_all + 2 : experts_all + 4].astype(BF)
    return (
        out, grad_input,
        projections[:, :local], projections[:, local : 2 * local], projections[:, 2 * local : 3 * local],
        grad_w_output.astype(BF),
        gains[:, 0], gains[:, 1], shared[:, experts_all + 1].astype(BF), shared[:, experts_all].astype(BF),
        shared[:, :experts_all].astype(BF),
        *(jnp.stack(pair) for pair in zip(outputs_zero, expert_outputs(grads_one))),
    )


def swap_tensor(values, bit):
    size = lax.axis_size(TENSOR)
    return lax.ppermute(values, TENSOR, [(i, i ^ bit) for i in range(size)])


def scatter_halving(values):
    place = lax.axis_index(TENSOR)
    rows = values.shape[0] // lax.axis_size(TENSOR)
    cut = lambda bits: lax.dynamic_slice_in_dim(values, (place ^ bits) * rows, rows, 0)
    passed = swap_tensor(plus(cut(2), swap_tensor(cut(3), 1)), 2)
    return cut(0).astype(F32) + swap_tensor(cut(1), 1).astype(F32) + passed.astype(F32), passed


def scatter_direct(values):
    place = lax.axis_index(TENSOR)
    size = lax.axis_size(TENSOR)
    rows = values.shape[0] // size
    cut = lambda bits: lax.dynamic_slice_in_dim(values, (place ^ bits) * rows, rows, 0)
    return sum((swap_tensor(cut(bits), bits).astype(F32) for bits in range(1, size)), cut(0).astype(F32))


def exchange(to_below, to_above):
    place = lax.axis_index(TENSOR)
    even = lax.rem(place, 2) == 0
    outer = lax.ppermute(jnp.where(even, to_above, to_below), TENSOR, [(0, 1), (1, 0), (2, 3), (3, 2)])
    inner = lax.ppermute(jnp.where(even, to_below, to_above), TENSOR, [(1, 2), (2, 1), (0, 0), (3, 3)])
    return [outer, inner]


def from_above(came):
    return jnp.where(lax.rem(lax.axis_index(TENSOR), 2) == 0, came[0], came[1])


def from_below(came):
    return jnp.where(lax.rem(lax.axis_index(TENSOR), 2) == 0, came[1], came[0])


def end_line(values, above, below):
    place = lax.axis_index(TENSOR)
    size = lax.axis_size(TENSOR)
    rows = values.shape[0]
    everything = jnp.zeros((rows * size,) + values.shape[1:], values.dtype)
    everything = lax.dynamic_update_slice_in_dim(everything, values, place * rows, 0)
    for ahead in range(1, size):
        piece = jnp.where(place + ahead < size, above[ahead - 1], below[size - ahead - 1])
        everything = lax.dynamic_update_slice_in_dim(everything, piece, lax.rem(place + ahead, size) * rows, 0)
    return everything


def exchange_doubling(values):
    far = swap_tensor(values, 2)
    return [swap_tensor(values, 1), far, swap_tensor(far, 1)]


def start_gather(values):
    return [swap_tensor(values, bits) for bits in range(1, lax.axis_size(TENSOR))]


def end_gather(values, came):
    place = lax.axis_index(TENSOR)
    rows = values.shape[0]
    everything = jnp.zeros((rows * (1 + len(came)),) + values.shape[1:], values.dtype)
    for bits, piece in enumerate((values, *came)):
        everything = lax.dynamic_update_slice_in_dim(everything, piece, (place ^ bits) * rows, 0)
    return everything


def gather_doubling(values):
    place = lax.axis_index(TENSOR)
    rows = values.shape[0]
    far = swap_tensor(values, 2)
    pieces = {0: values, 1: swap_tensor(values, 1), 2: far, 3: swap_tensor(far, 1)}
    everything = jnp.zeros((rows * lax.axis_size(TENSOR),) + values.shape[1:], values.dtype)
    for bits, piece in pieces.items():
        everything = lax.dynamic_update_slice_in_dim(everything, piece, (place ^ bits) * rows, 0)
    return everything


def mix_halves(values):
    size = lax.axis_size(TENSOR)
    view = values.reshape(HALVES, size, -1, values.shape[-1])
    return jnp.swapaxes(view, 0, 1).reshape(values.shape)


def unmix_halves(values):
    size = lax.axis_size(TENSOR)
    view = values.reshape(size, HALVES, -1, values.shape[-1])
    return jnp.swapaxes(view, 0, 1).reshape(values.shape)


def rotations():
    size = lax.axis_size(TENSOR)
    return [[(i, (i + d) % size) for i in range(size)] for d in range(1, size)]


def sum_small(values):
    total = values
    for pairs in rotations():
        total = total + lax.ppermute(values, TENSOR, pairs)
    return total


def gather_small(values):
    rows = values.shape[0]
    size = lax.axis_size(TENSOR)
    place = lax.axis_index(TENSOR)
    whole_rows = jnp.zeros((rows * size,) + values.shape[1:], values.dtype)
    whole_rows = lax.dynamic_update_slice_in_dim(whole_rows, values, place * rows, 0)
    for d, pairs in enumerate(rotations(), 1):
        came = lax.ppermute(values, TENSOR, pairs)
        whole_rows = lax.dynamic_update_slice_in_dim(whole_rows, came, lax.rem(place + size - d, size) * rows, 0)
    return whole_rows


def scatter_small(values):
    size = lax.axis_size(TENSOR)
    place = lax.axis_index(TENSOR)
    rows = values.shape[0] // size
    cut = lambda index: lax.dynamic_slice_in_dim(values, index * rows, rows, 0)
    total = cut(place)
    for d, pairs in enumerate(rotations(), 1):
        total = total + lax.ppermute(cut(lax.rem(place + d, size)), TENSOR, pairs)
    return total


NEAR_GROUPS = 8


def solution(mesh):
    placed = (
        P(EXPERT, None),
        P(EXPERT, None),
        P(EXPERT),
        P(EXPERT, None),
        P(EXPERT, None),
        P(None, TENSOR),
        P(None, TENSOR),
        P(None, TENSOR),
        P(TENSOR, None),
        P(TENSOR),
        P(TENSOR),
        P(),
        P(),
        P(),
        P(EXPERT, None, TENSOR),
        P(EXPERT, None, TENSOR),
        P(EXPERT, TENSOR, None),
    )
    return jax.shard_map(
        shards_near if mesh.shape[EXPERT] == NEAR_GROUPS else shards,
        mesh=mesh,
        in_specs=placed,
        out_specs=(
            P(EXPERT, None),
            P(EXPERT, None),
            P(EXPERT, TENSOR),
            P(EXPERT, TENSOR),
            P(EXPERT, TENSOR),
            P(TENSOR, EXPERT),
            P((TENSOR, EXPERT)),
            P((TENSOR, EXPERT)),
            P(EXPERT),
            P(EXPERT),
            P(EXPERT, None),
            P(EXPERT, None, TENSOR),
            P(EXPERT, None, TENSOR),
            P(EXPERT, TENSOR, None),
        ),
        check_vma=False,
    )
```

```python
import functools

import jax
import jax.numpy as jnp
from jax import lax
from jax.experimental import pallas as pl
from jax.experimental.pallas import tpu as pltpu
from jax.sharding import PartitionSpec as P

HEAD_DIM = 128
EXPERT = "expert"
TENSOR = "tensor"
TOP = 8


EPS = 1e-05
THETA = 10000.0
NEG = -1e30


def norm_rows(values, gain):
    inverse = lax.rsqrt(jnp.mean(values * values, axis=-1, keepdims=True) + EPS)
    return (values * inverse * gain, inverse)


def norm_back(values, inverse, gain, upstream):
    scaled = upstream * gain
    inner = jnp.mean(values * scaled, axis=-1, keepdims=True)
    grad_values = inverse * scaled - values * inverse * inverse * inverse * inner
    grad_gain = jnp.sum(upstream * values * inverse, axis=0)
    return (grad_values, grad_gain)


def layout(lengths, rows):
    ends = jnp.cumsum(lengths, axis=-1)
    starts = ends - lengths
    places = jnp.arange(rows, dtype=jnp.int32)
    inside = (
        (places[..., :, None] >= starts[..., None, :]) & (places[..., :, None] < ends[..., None, :])
    ).astype(jnp.int32)
    number = jnp.arange(lengths.shape[-1], dtype=jnp.int32)
    alive = jnp.sum(inside, axis=-1)
    segment = jnp.sum(inside * number, axis=-1) + (1 - alive) * (lengths.shape[-1] + places)
    position = jnp.sum(inside * (places[..., :, None] - starts[..., None, :]), axis=-1)
    return (segment, position)


def rope_angles(position, head_size):
    half = head_size // 2
    freq = THETA ** (-2.0 * jnp.arange(half, dtype=jnp.float32) / head_size)
    angle = position.astype(jnp.float32)[..., None] * freq
    return (jnp.cos(angle), jnp.sin(angle))


def rotate(values, cosine, sine):
    half = values.shape[-1] // 2
    first, second = (values[..., :half], values[..., half:])
    cos_here = cosine[..., None, :]
    sin_here = sine[..., None, :]
    return jnp.concatenate(
        [first * cos_here - second * sin_here, second * cos_here + first * sin_here], axis=-1
    )


def unrotate(grads, cosine, sine):
    half = grads.shape[-1] // 2
    first, second = (grads[..., :half], grads[..., half:])
    cos_here = cosine[..., None, :]
    sin_here = sine[..., None, :]
    return jnp.concatenate(
        [first * cos_here + second * sin_here, second * cos_here - first * sin_here], axis=-1
    )


def block_scores(query_block, keys, seg_block, segment, start):
    scores = jnp.einsum(
        "qhd,khd->hqk", query_block, keys, preferred_element_type=jnp.float32
    ) * HEAD_DIM ** (-0.5)
    rows_query = start + jnp.arange(query_block.shape[0], dtype=jnp.int32)
    rows_key = jnp.arange(keys.shape[0], dtype=jnp.int32)
    allowed = (seg_block[:, None] == segment[None, :]) & (rows_key[None, :] <= rows_query[:, None])
    return jnp.where(allowed[None], scores, NEG)


def attention_forward(queries, keys, values, segment, block):
    rows = queries.shape[0]

    def one_block(index):
        start = index * block
        query_block = lax.dynamic_slice_in_dim(queries, start, block, 0)
        seg_block = lax.dynamic_slice_in_dim(segment, start, block, 0)
        scores = block_scores(query_block, keys, seg_block, segment, start)
        top = jnp.max(scores, axis=-1, keepdims=True)
        raised = jnp.exp(scores - top)
        total = jnp.sum(raised, axis=-1, keepdims=True)
        weights = (raised / total).astype(jnp.bfloat16)
        context = jnp.einsum("hqk,khd->qhd", weights, values, preferred_element_type=jnp.float32)
        return (context, top, total)

    context, top, total = lax.map(one_block, jnp.arange(rows // block, dtype=jnp.int32))
    return (context.reshape(queries.shape), top, total)


def attention_backward(queries, keys, values, segment, block, top, total, grad_context):
    rows = queries.shape[0]
    scale = HEAD_DIM ** (-0.5)

    def one_block(carry, index):
        grad_keys, grad_values = carry
        start = index * block
        query_block = lax.dynamic_slice_in_dim(queries, start, block, 0)
        seg_block = lax.dynamic_slice_in_dim(segment, start, block, 0)
        grad_block = lax.dynamic_slice_in_dim(grad_context, start, block, 0)
        scores = block_scores(query_block, keys, seg_block, segment, start)
        weights_f = jnp.exp(scores - top[index]) / total[index]
        weights = weights_f.astype(jnp.bfloat16)
        grad_weights = jnp.einsum(
            "qhd,khd->hqk", grad_block, values, preferred_element_type=jnp.float32
        )
        inner = jnp.sum(weights_f * grad_weights, axis=-1, keepdims=True)
        grad_scores = (weights_f * (grad_weights - inner)).astype(jnp.bfloat16)
        grad_query = (
            jnp.einsum("hqk,khd->qhd", grad_scores, keys, preferred_element_type=jnp.float32)
            * scale
        )
        grad_keys = (
            grad_keys
            + jnp.einsum(
                "hqk,qhd->khd", grad_scores, query_block, preferred_element_type=jnp.float32
            )
            * scale
        )
        grad_values = grad_values + jnp.einsum(
            "hqk,qhd->khd", weights, grad_block, preferred_element_type=jnp.float32
        )
        return ((grad_keys, grad_values), grad_query)

    empty = jnp.zeros(keys.shape, jnp.float32)
    (grad_keys, grad_values), grad_query = lax.scan(
        one_block, (empty, empty), jnp.arange(rows // block, dtype=jnp.int32)
    )
    return (grad_query.reshape(queries.shape), grad_keys, grad_values)


def shards(
    tokens,
    cotangent,
    seq_lengths,
    expert_ids,
    slot_index,
    w_query,
    w_key,
    w_value,
    w_output,
    query_gain,
    key_gain,
    attn_gain,
    moe_gain,
    router,
    w_gate,
    w_up,
    w_down,
):
    rows, width = tokens.shape
    local = w_query.shape[1]
    heads_here = local // HEAD_DIM
    groups = lax.axis_size(EXPERT)
    experts_here = w_gate.shape[0]
    experts_all = experts_here * groups
    capacity = max(2, 3 * rows * TOP // (4 * experts_all))
    block = min(512, rows)
    shape_heads = (rows, heads_here, HEAD_DIM)
    segment, position = layout(seq_lengths, rows)
    cosine, sine = rope_angles(position, HEAD_DIM)
    inputs = tokens.astype(jnp.float32)
    normed, inverse_in = norm_rows(inputs, attn_gain)
    attn_in = normed.astype(jnp.bfloat16)
    query_raw = jnp.dot(attn_in, w_query, preferred_element_type=jnp.float32)
    key_raw = jnp.dot(attn_in, w_key, preferred_element_type=jnp.float32)
    value_raw = jnp.dot(attn_in, w_value, preferred_element_type=jnp.float32)
    query_total, key_total = lax.psum(
        (jnp.sum(query_raw * query_raw, axis=-1), jnp.sum(key_raw * key_raw, axis=-1)), TENSOR
    )
    query_inverse = lax.rsqrt(query_total / width + EPS)[:, None]
    key_inverse = lax.rsqrt(key_total / width + EPS)[:, None]
    queries = rotate(
        (query_raw * query_inverse * query_gain).reshape(shape_heads), cosine, sine
    ).astype(jnp.bfloat16)
    keys = rotate((key_raw * key_inverse * key_gain).reshape(shape_heads), cosine, sine).astype(
        jnp.bfloat16
    )
    values = value_raw.reshape(shape_heads).astype(jnp.bfloat16)
    context, top, total = attention_forward(queries, keys, values, segment, block)
    context_low = context.reshape(rows, local).astype(jnp.bfloat16)
    attn = lax.psum(
        jnp.dot(context_low, w_output, preferred_element_type=jnp.float32).astype(jnp.bfloat16),
        TENSOR,
    ).astype(jnp.float32)
    hidden_in = inputs + attn
    moe_in, inverse_moe = norm_rows(hidden_in, moe_gain)
    router_wide = router.astype(jnp.float32)
    shares = jax.nn.softmax(jnp.dot(moe_in, router_wide, precision=lax.Precision.HIGHEST), axis=-1)
    chosen = expert_ids[:, :, None] == jnp.arange(experts_all, dtype=jnp.int32)[None, None, :]
    gates = jnp.sum(jnp.where(chosen, shares[:, None, :], 0.0), axis=-1)
    kept = slot_index >= 0
    target_slot = jnp.where(
        kept, expert_ids * capacity + slot_index, experts_all * capacity
    ).reshape(-1)
    token_of = (
        jnp.full((experts_all * capacity,), -1, jnp.int32)
        .at[target_slot]
        .set(jnp.repeat(jnp.arange(rows, dtype=jnp.int32), TOP), mode="drop")
    )
    gate_of = (
        jnp.zeros((experts_all * capacity,), jnp.float32)
        .at[target_slot]
        .set(gates.reshape(-1), mode="drop")
    )
    filled = (token_of >= 0)[:, None]
    source_row = jnp.maximum(token_of, 0)
    moe_low = moe_in.astype(jnp.bfloat16)
    send_rows = jnp.where(filled, moe_low[source_row], jnp.zeros((), jnp.bfloat16)).reshape(
        groups, experts_here * capacity, width
    )
    arrived = lax.all_to_all(send_rows, EXPERT, split_axis=0, concat_axis=0, tiled=True)
    arrived = arrived.reshape(groups, experts_here, capacity, width)
    gate_pre = jnp.einsum("secd,edf->secf", arrived, w_gate, preferred_element_type=jnp.float32)
    up_pre = jnp.einsum("secd,edf->secf", arrived, w_up, preferred_element_type=jnp.float32)
    activated = jax.nn.silu(gate_pre)
    hidden = (activated * up_pre).astype(jnp.bfloat16)
    partial_value = jnp.einsum(
        "secf,efd->secd", hidden, w_down, preferred_element_type=jnp.float32
    ).astype(jnp.bfloat16)
    dy_rows = jnp.where(filled, cotangent[source_row], jnp.zeros((), jnp.bfloat16))
    returned = lax.all_to_all(partial_value, EXPERT, split_axis=0, concat_axis=0, tiled=True)
    returned = returned.reshape(experts_all * capacity, width).astype(jnp.float32)
    moe_part = jax.ops.segment_sum(returned * gate_of[:, None], source_row, num_segments=rows)
    moe = lax.psum(moe_part.astype(jnp.bfloat16), TENSOR).astype(jnp.float32)
    row_dots = jnp.sum(dy_rows.astype(jnp.float32) * returned, axis=-1)
    out = (hidden_in + moe).astype(jnp.bfloat16)
    grad_gate = jnp.take(row_dots, target_slot, mode="fill", fill_value=0.0).reshape(rows, TOP)
    grad_shares = jnp.sum(jnp.where(chosen, grad_gate[:, :, None], 0.0), axis=1)
    grad_logits = shares * (grad_shares - jnp.sum(shares * grad_shares, axis=-1, keepdims=True))
    router_back = jnp.einsum("te,de->td", grad_logits, router_wide, precision=lax.Precision.HIGHEST)
    router_part = jnp.einsum("td,te->de", moe_in, grad_logits, precision=lax.Precision.HIGHEST)
    grad_rows = (
        (dy_rows.astype(jnp.float32) * gate_of[:, None])
        .astype(jnp.bfloat16)
        .reshape(groups, experts_here * capacity, width)
    )
    grad_arrived = lax.all_to_all(grad_rows, EXPERT, split_axis=0, concat_axis=0, tiled=True)
    grad_arrived = grad_arrived.reshape(groups, experts_here, capacity, width)
    grad_hidden = jnp.einsum(
        "secd,efd->secf", grad_arrived, w_down, preferred_element_type=jnp.float32
    )
    grad_w_down = jnp.einsum(
        "secf,secd->efd", hidden, grad_arrived, preferred_element_type=jnp.float32
    )
    sigma = jax.nn.sigmoid(gate_pre)
    grad_gate_pre = (grad_hidden * up_pre * sigma * (1.0 + gate_pre * (1.0 - sigma))).astype(
        jnp.bfloat16
    )
    grad_up_pre = (grad_hidden * activated).astype(jnp.bfloat16)
    grad_w_gate = jnp.einsum(
        "secd,secf->edf", arrived, grad_gate_pre, preferred_element_type=jnp.float32
    )
    grad_w_up = jnp.einsum(
        "secd,secf->edf", arrived, grad_up_pre, preferred_element_type=jnp.float32
    )
    grad_in_rows = jnp.einsum(
        "secf,edf->secd", grad_gate_pre, w_gate, preferred_element_type=jnp.float32
    )
    grad_in_rows = (
        grad_in_rows
        + jnp.einsum("secf,edf->secd", grad_up_pre, w_up, preferred_element_type=jnp.float32)
    ).astype(jnp.bfloat16)
    back_rows = lax.all_to_all(
        grad_in_rows.reshape(groups, experts_here * capacity, width),
        EXPERT,
        split_axis=0,
        concat_axis=0,
        tiled=True,
    )
    back_rows = back_rows.reshape(experts_all * capacity, width).astype(jnp.float32)
    moe_back = jax.ops.segment_sum(back_rows, source_row, num_segments=rows)
    grad_moe_in, grad_router_rows = (
        lax.psum((moe_back + router_back).astype(jnp.bfloat16), TENSOR).astype(jnp.float32),
        lax.psum(router_part.astype(jnp.bfloat16), TENSOR).astype(jnp.float32),
    )
    grad_norm_moe, grad_moe_gain = norm_back(hidden_in, inverse_moe, moe_gain, grad_moe_in)
    grad_hidden_in = cotangent.astype(jnp.float32) + grad_norm_moe
    grad_low = grad_hidden_in.astype(jnp.bfloat16)
    grad_w_output = jnp.einsum(
        "tf,td->fd", context_low, grad_low, preferred_element_type=jnp.float32
    )
    grad_context = (
        jnp.einsum("td,fd->tf", grad_low, w_output, preferred_element_type=jnp.float32)
        .astype(jnp.bfloat16)
        .reshape(shape_heads)
    )
    grad_queries, grad_keys, grad_values = attention_backward(
        queries, keys, values, segment, block, top, total, grad_context
    )
    grad_query_normed = unrotate(grad_queries, cosine, sine).reshape(rows, local)
    grad_key_normed = unrotate(grad_keys, cosine, sine).reshape(rows, local)
    query_scaled = grad_query_normed * query_gain
    key_scaled = grad_key_normed * key_gain
    query_inner, key_inner = lax.psum(
        (jnp.sum(query_raw * query_scaled, axis=-1), jnp.sum(key_raw * key_scaled, axis=-1)),
        TENSOR,
    )
    grad_query_raw = (
        query_inverse * query_scaled
        - query_raw * query_inverse * query_inverse * query_inverse * (query_inner / width)[:, None]
    )
    grad_key_raw = (
        key_inverse * key_scaled
        - key_raw * key_inverse * key_inverse * key_inverse * (key_inner / width)[:, None]
    )
    grad_query_gain = jnp.sum(grad_query_normed * query_raw * query_inverse, axis=0)
    grad_key_gain = jnp.sum(grad_key_normed * key_raw * key_inverse, axis=0)
    query_low = grad_query_raw.astype(jnp.bfloat16)
    key_low = grad_key_raw.astype(jnp.bfloat16)
    value_low = grad_values.reshape(rows, local).astype(jnp.bfloat16)
    grad_w_query = jnp.einsum("td,tf->df", attn_in, query_low, preferred_element_type=jnp.float32)
    grad_w_key = jnp.einsum("td,tf->df", attn_in, key_low, preferred_element_type=jnp.float32)
    grad_w_value = jnp.einsum("td,tf->df", attn_in, value_low, preferred_element_type=jnp.float32)
    terms_in = jnp.einsum("tf,df->td", query_low, w_query, preferred_element_type=jnp.float32)
    terms_in = terms_in + jnp.einsum(
        "tf,df->td", key_low, w_key, preferred_element_type=jnp.float32
    )
    terms_in = terms_in + jnp.einsum(
        "tf,df->td", value_low, w_value, preferred_element_type=jnp.float32
    )
    grad_normed = lax.psum(terms_in.astype(jnp.bfloat16), TENSOR).astype(jnp.float32)
    grad_norm_in, grad_attn_gain = norm_back(inputs, inverse_in, attn_gain, grad_normed)
    grad_input = (grad_hidden_in + grad_norm_in).astype(jnp.bfloat16)
    sums = (
        lax.psum_scatter(
            grad_w_query.astype(jnp.bfloat16), EXPERT, scatter_dimension=0, tiled=True
        ).astype(jnp.float32),
        lax.psum_scatter(
            grad_w_key.astype(jnp.bfloat16), EXPERT, scatter_dimension=0, tiled=True
        ).astype(jnp.float32),
        lax.psum_scatter(
            grad_w_value.astype(jnp.bfloat16), EXPERT, scatter_dimension=0, tiled=True
        ).astype(jnp.float32),
        lax.psum_scatter(
            grad_w_output.astype(jnp.bfloat16), EXPERT, scatter_dimension=1, tiled=True
        ).astype(jnp.float32),
        lax.psum_scatter(
            grad_query_gain.astype(jnp.bfloat16), EXPERT, scatter_dimension=0, tiled=True
        ).astype(jnp.float32),
        lax.psum_scatter(
            grad_key_gain.astype(jnp.bfloat16), EXPERT, scatter_dimension=0, tiled=True
        ).astype(jnp.float32),
        lax.psum_scatter(
            grad_attn_gain.astype(jnp.bfloat16), EXPERT, scatter_dimension=0, tiled=True
        ).astype(jnp.float32),
        lax.psum_scatter(
            grad_moe_gain.astype(jnp.bfloat16), EXPERT, scatter_dimension=0, tiled=True
        ).astype(jnp.float32),
        lax.psum_scatter(
            grad_router_rows.astype(jnp.bfloat16), EXPERT, scatter_dimension=0, tiled=True
        ).astype(jnp.float32),
    )
    lows = tuple((item.astype(jnp.bfloat16) for item in sums))
    return (
        out,
        grad_input,
        lows[0],
        lows[1],
        lows[2],
        lows[3],
        lows[4],
        lows[5],
        lows[6],
        lows[7],
        lows[8],
        grad_w_gate.astype(jnp.bfloat16),
        grad_w_up.astype(jnp.bfloat16),
        grad_w_down.astype(jnp.bfloat16),
    )


F32 = jnp.float32
BF = jnp.bfloat16
NN = (((1,), (0,)), ((), ()))
NT = (((1,), (1,)), ((), ()))
TN = (((0,), (0,)), ((), ()))
VMEM_BYTES = 62 * 2**20
COLUMN_TILE = 512
ROW_TILE = 512
QUERY_TILE = 512
BACK_TILE = 128
HIDDEN_TILE = 256
LANES = 128
LOG2_E = 1.4426950408889634


def mul(left, right, dims=NN):
    return lax.dot_general(left, right, dims, preferred_element_type=F32)


def kernel_params():
    return pltpu.CompilerParams(vmem_limit_bytes=VMEM_BYTES)


def whole(shape):
    return pl.BlockSpec(shape, lambda i: (0,) * len(shape), pipeline_mode=pl.Buffered(1))


def fill_bias(bias, row_ref, col_ref):
    @pl.when(pl.program_id(0) == 0)
    def _():
        rows = lax.broadcasted_iota(jnp.int32, bias.shape, 0)
        columns = lax.broadcasted_iota(jnp.int32, bias.shape, 1)
        allowed = (row_ref[...] == col_ref[...]) & (columns <= rows)
        bias[...] = jnp.where(allowed, 0.0, NEG)


def score_block(queries, keys, bias):
    return mul(queries, keys, NT) * (HEAD_DIM**-0.5 * LOG2_E) + bias


ANYWHERE = pl.BlockSpec(memory_space=pl.ANY)


def front_kernel(tokens_ref, gain_ref, wq_ref, wk_ref, wv_ref, *refs):
    low_ref, inverse_ref, q_ref, k_ref, v_ref, sums_ref = refs[-6:]
    rows = tokens_ref[...].astype(F32)
    inverse = lax.rsqrt(jnp.mean(rows * rows, axis=1, keepdims=True) + EPS)
    low = (rows * inverse * gain_ref[...]).astype(BF)
    low_ref[...] = low
    inverse_ref[...] = inverse
    sums = []
    for w_ref, out_ref in ((wq_ref, q_ref), (wk_ref, k_ref)):
        raw = mul(low, w_ref[...])
        out_ref[...] = raw
        sums.append(jnp.sum(raw * raw, axis=1, keepdims=True))
    v_ref[...] = mul(low, wv_ref[...]).astype(BF)
    sums_ref[...] = jnp.concatenate(sums, axis=1)


def front_call(tokens, gain, w_query, w_key, w_value, waits):
    rows, width = tokens.shape
    local = w_query.shape[1]
    tile = min(HIDDEN_TILE, rows)
    row = lambda c: pl.BlockSpec((tile, c), lambda i: (i, 0))
    shape = jax.ShapeDtypeStruct
    return pl.pallas_call(
        front_kernel,
        grid=(rows // tile,),
        in_specs=[row(width), whole((1, width))] + [whole(w_query.shape)] * 3 + [ANYWHERE] * len(waits),
        out_specs=[row(width), row(1)] + [row(local)] * 3 + [row(2)],
        out_shape=[shape((rows, width), BF), shape((rows, 1), F32)]
        + [shape((rows, local), F32)] * 2
        + [shape((rows, local), BF), shape((rows, 2), F32)],
        compiler_params=kernel_params(),
        cost_estimate=pl.CostEstimate(
            flops=6 * rows * width * local, bytes_accessed=4 * rows * width + 6 * width * local, transcendentals=0
        ),
        name="front_rows",
    )(tokens, gain, w_query, w_key, w_value, *waits)


def attention_kernel(
    q_ref, k_ref, v_ref, qi_ref, ki_ref, qg_ref, kg_ref, cos_ref, sin_ref, row_ref, col_ref,
    qh_ref, kh_ref, ctx_ref, lse_ref, bias,
):
    rows, size = q_ref.shape
    tile = min(QUERY_TILE, rows)
    fill_bias(bias, row_ref, col_ref)
    for raw, inverse, gain, low in ((q_ref, qi_ref, qg_ref, qh_ref), (k_ref, ki_ref, kg_ref, kh_ref)):
        normed = raw[...] * inverse[...] * gain[...]
        turned = normed * cos_ref[...] + pltpu.roll(normed, size // 2, 1) * sin_ref[...]
        low[...] = turned.astype(BF)
    for start in range(0, rows, tile):
        end = start + tile
        scores = score_block(qh_ref[start:end], kh_ref[:end], bias[start:end, :end])
        top = jnp.max(scores, axis=-1, keepdims=True)
        raised = jnp.exp2(scores - top)
        total = jnp.sum(raised, axis=-1, keepdims=True)
        weights = (raised * (1.0 / total)).astype(BF)
        ctx_ref[start:end] = mul(weights, v_ref[:end]).astype(BF)
        lse_ref[0, start:end] = top + jnp.log2(total)


def attention_back_kernel(
    q_ref, k_ref, v_ref, qi_ref, ki_ref, qg_ref, kg_ref, cos_ref, sin_ref, row_ref, col_ref,
    qh_ref, kh_ref, ctx_ref, lse_ref, dctx_ref, *rest,
):
    dq_ref, dk_ref, dv_ref, inner_ref, dqg_ref, dkg_ref, dq_total, dk_total, dv_total, bias = rest[-10:]
    rows, size = q_ref.shape
    scale = size**-0.5
    tile = min(BACK_TILE, rows)
    fill_bias(bias, row_ref, col_ref)
    dk_total[...] = jnp.zeros_like(dk_total)
    dv_total[...] = jnp.zeros_like(dv_total)
    inner = jnp.sum(dctx_ref[...].astype(F32) * ctx_ref[...].astype(F32), axis=1, keepdims=True)
    for start in range(0, rows, tile):
        end = start + tile
        keys = kh_ref[:end]
        scores = score_block(qh_ref[start:end], keys, bias[start:end, :end])
        weights = jnp.exp2(scores - lse_ref[0, start:end])
        grad_weights = mul(dctx_ref[start:end], v_ref[:end], NT)
        grad_scores = (weights * (grad_weights - inner[start:end])).astype(BF)
        dq_total[start:end] = mul(grad_scores, keys) * scale
        dk_total[:end] += mul(grad_scores, qh_ref[start:end], TN) * scale
        dv_total[:end] += mul(weights.astype(BF), dctx_ref[start:end], TN)
    dv_ref[...] = dv_total[...].astype(BF)
    inners = []
    for total, raw, inverse, gain, out, dgain in (
        (dq_total, q_ref, qi_ref, qg_ref, dq_ref, dqg_ref),
        (dk_total, k_ref, ki_ref, kg_ref, dk_ref, dkg_ref),
    ):
        grad = total[...]
        grad = grad * cos_ref[...] - pltpu.roll(grad, size // 2, 1) * sin_ref[...]
        values = raw[...]
        dgain[...] = jnp.sum(grad * values * inverse[...], axis=0, keepdims=True)
        scaled = grad * gain[...]
        inners.append(jnp.sum(values * scaled, axis=1, keepdims=True))
        out[...] = scaled
    inner_ref[0] = jnp.concatenate(inners, axis=1)


def head_specs(rows):
    head = pl.BlockSpec((rows, HEAD_DIM), lambda h: (0, h))
    gain = pl.BlockSpec((1, HEAD_DIM), lambda h: (0, h))
    column = whole((rows, 1))
    table = whole((rows, HEAD_DIM))
    own_column = pl.BlockSpec((1, rows, 1), lambda h: (h, 0, 0))
    specs = [head, head, head, column, column, gain, gain, table, table, column, whole((1, rows))]
    return head, gain, own_column, specs


def attention_call(operands, rows, local):
    head, gain, own_column, specs = head_specs(rows)
    heads = local // HEAD_DIM
    return pl.pallas_call(
        attention_kernel,
        grid=(heads,),
        in_specs=specs,
        out_specs=[head] * 3 + [own_column],
        out_shape=[jax.ShapeDtypeStruct((rows, local), BF)] * 3 + [jax.ShapeDtypeStruct((heads, rows, 1), F32)],
        scratch_shapes=[pltpu.VMEM((rows, rows), F32)],
        compiler_params=kernel_params(),
        cost_estimate=pl.CostEstimate(
            flops=2 * rows * rows * local, bytes_accessed=12 * rows * local, transcendentals=rows * rows * heads // 2
        ),
        name="attention_rows",
    )(*operands)


def attention_back_call(operands, rows, local, waits=()):
    head, gain, own_column, specs = head_specs(rows)
    heads = local // HEAD_DIM
    return pl.pallas_call(
        attention_back_kernel,
        grid=(heads,),
        in_specs=specs + [head] * 3 + [own_column, head] + [ANYWHERE] * len(waits),
        out_specs=[head] * 3 + [pl.BlockSpec((1, rows, 2), lambda h: (h, 0, 0)), gain, gain],
        out_shape=[jax.ShapeDtypeStruct((rows, local), F32)] * 2
        + [jax.ShapeDtypeStruct((rows, local), BF), jax.ShapeDtypeStruct((heads, rows, 2), F32)]
        + [jax.ShapeDtypeStruct((1, local), F32)] * 2,
        scratch_shapes=[pltpu.VMEM((rows, HEAD_DIM), F32)] * 3 + [pltpu.VMEM((rows, rows), F32)],
        compiler_params=kernel_params(),
        cost_estimate=pl.CostEstimate(
            flops=8 * rows * rows * local, bytes_accessed=24 * rows * local, transcendentals=rows * rows * heads // 2
        ),
        name="attention_rows_back",
    )(*operands, *waits)


def hidden_kernel(pieces, core_ref, tokens_ref, gain_ref, *refs):
    ctx_refs, w_refs = refs[:pieces], refs[pieces : pieces + 3]
    hidden_ref, low_ref, inverse_ref, heads = refs[pieces + 3 :]
    local = ctx_refs[0].shape[1]
    half = local // 2
    near = pl.ds(pl.multiple_of(core_ref[0] * half, half), half)
    far = pl.ds(pl.multiple_of((1 - core_ref[0]) * half, half), half)
    heads[:, :local] = ctx_refs[0][...]
    for number in range(1, pieces):
        mine = local + (number - 1) * half
        other = mine + (pieces - 1) * half
        heads[:, mine : mine + half] = ctx_refs[number][:, near]
        heads[:, other : other + half] = ctx_refs[number][:, far]
    total = tokens_ref[...].astype(F32)
    begin = 0
    for w_ref in w_refs:
        end = begin + w_ref.shape[0]
        total = total + mul(heads[:, begin:end], w_ref[...])
        begin = end
    inverse = lax.rsqrt(jnp.mean(total * total, axis=1, keepdims=True) + EPS)
    low_ref[...] = (total * inverse * gain_ref[...]).astype(BF)

    @pl.when(pl.program_id(0) == core_ref[1])
    def _():
        hidden_ref[...] = total
        inverse_ref[...] = inverse


def hidden_call(places, tokens, gain, context, weights):
    rows, width = tokens.shape
    tile = rows // len(context)
    row = lambda c: pl.BlockSpec((tile, c), lambda i: (i, 0))
    return pl.pallas_call(
        functools.partial(hidden_kernel, len(context)),
        grid=(rows // tile,),
        in_specs=[pl.BlockSpec(memory_space=pltpu.SMEM), row(width), whole((1, width))]
        + [row(context[0].shape[1])] * len(context)
        + [whole(array.shape) for array in weights],
        out_specs=[whole((tile, width)), row(width), whole((tile, 1))],
        out_shape=[
            jax.ShapeDtypeStruct((tile, width), F32),
            jax.ShapeDtypeStruct((rows, width), BF),
            jax.ShapeDtypeStruct((tile, 1), F32),
        ],
        scratch_shapes=[pltpu.VMEM((tile, width), BF)],
        compiler_params=kernel_params(),
        cost_estimate=pl.CostEstimate(
            flops=2 * rows * width * width, bytes_accessed=10 * rows * width + 2 * width * width, transcendentals=0
        ),
        name="hidden_rows",
    )(places, tokens, gain, *context, *weights)


def rows_kernel(place, number_here, each_device, added, waits, *refs):
    core_ref, router_ref = refs[:2]
    x_refs, dy_refs, carried_refs, w_ref = refs[2:4], refs[4:6], refs[6:8], refs[8]
    rest = refs[9:]
    if added:
        before, rest = rest[:4], rest[4:]
    rest = rest[waits:]
    moe_refs, dx_refs, kept_ref, share_ref = rest[:2], rest[2:4], rest[4], rest[5]
    x, dy, down, both_w, kept, moe, dx, gates, dots, in_sems, w_sems, before_sems, out_sems = rest[6:]
    blocks, _, own, width = x_refs[0].shape
    rows = blocks * own
    total = 2 * rows
    experts = w_ref.shape[0]
    hid = w_ref.shape[1] // 3

    def fetch_rows(refs, held, first):
        copies = []
        for side in range(2):
            for block in range(blocks):
                to = held.at[pl.ds(side * rows + block * own, own)]
                copies.append(pltpu.make_async_copy(refs[side].at[block, place], to, in_sems.at[first + side * blocks + block]))
        return copies

    x_copies = fetch_rows(x_refs, x, 0)
    dy_copies = fetch_rows(dy_refs, dy, 2 * blocks)
    w_copies = [
        (
            pltpu.make_async_copy(w_ref.at[e, pl.ds(hid, 2 * hid)], both_w.at[pl.ds(2 * e * hid, 2 * hid)], w_sems.at[2 * e]),
            pltpu.make_async_copy(w_ref.at[e, pl.ds(0, hid)], down.at[pl.ds(e * hid, hid)], w_sems.at[2 * e + 1]),
        )
        for e in range(experts)
    ]
    for copy in x_copies + [w_copies[0][0]] + dy_copies + [w_copies[0][1]]:
        copy.start()
    for pair in w_copies[1:]:
        for copy in pair:
            copy.start()
    earlier = []
    if added:
        for side in range(2):
            here = pl.ds(side * rows, rows)
            earlier.append(pltpu.make_async_copy(before[side], moe.at[here], before_sems.at[side]))
            earlier.append(pltpu.make_async_copy(before[2 + side], dx.at[here], before_sems.at[2 + side]))
    for copy in earlier:
        copy.start()
    for copy in x_copies:
        copy.wait()
    for side in range(2):
        here = slice(side * rows, (side + 1) * rows)
        logits = mul(x[here], router_ref[...])
        raised = jnp.exp(logits - jnp.max(logits, axis=1, keepdims=True))
        shares = raised / jnp.sum(raised, axis=1, keepdims=True)
        if side == 0:
            share_ref[...] = shares
        gates[here] = shares * carried_refs[side][:, 0].reshape(rows, -1).astype(F32)
    dots[...] = jnp.zeros_like(dots)
    w_copies[0][0].wait()
    for copy in dy_copies:
        copy.wait()
    out_copies = []
    for e in range(experts):
        if e:
            w_copies[e][0].wait()
        w_copies[e][1].wait()
        index = (e * 2 + core_ref[0]) * each_device + number_here
        gh = slice(e * hid, (e + 1) * hid)
        wide = experts * hid + 2 * e * hid
        for first in range(0, total, ROW_TILE):
            here = slice(first, first + ROW_TILE)
            both = mul(x[here], both_w[2 * e * hid : 2 * (e + 1) * hid], NT)
            back = mul(dy[here], down[gh], NT)
            pre, up = both[:, :hid], both[:, hid:]
            sigma = 0.5 * jnp.tanh(0.5 * pre) + 0.5
            active = pre * sigma
            chosen = lax.broadcasted_iota(jnp.int32, (ROW_TILE, gates.shape[1]), 1) == index
            gate = jnp.sum(jnp.where(chosen, gates[here], 0.0), axis=1, keepdims=True)
            column = lax.broadcasted_iota(jnp.int32, (ROW_TILE, LANES), 1) == index
            hidden = active * up
            dots[here] += jnp.where(column, jnp.sum(hidden * back, axis=1, keepdims=True), 0.0)
            back = back * gate
            kept[here, gh] = (hidden * gate).astype(BF)
            kept[here, wide : wide + hid] = (back * up * sigma * (1.0 + pre * (1.0 - sigma))).astype(BF)
            kept[here, wide + hid : wide + 2 * hid] = (back * active).astype(BF)
    copy = pltpu.make_async_copy(kept, kept_ref, out_sems.at[0])
    copy.start()
    out_copies.append(copy)
    for copy in earlier:
        copy.wait()
    for number, first in enumerate(range(0, width, COLUMN_TILE)):
        here = slice(first, first + COLUMN_TILE)
        for what, (held, w_held, begin, end) in enumerate((
            (moe, down, 0, experts * hid), (dx, both_w, experts * hid, 3 * experts * hid)
        )):
            value = mul(kept[:, begin:end], w_held[:, here])
            if added:
                value = value + held[:, here].astype(F32)
            held[:, here] = value.astype(BF)
            for side in range(2):
                ref = (moe_refs, dx_refs)[what][side]
                copy = pltpu.make_async_copy(
                    held.at[pl.ds(side * rows, rows), pl.ds(first, COLUMN_TILE)],
                    ref.at[:, pl.ds(first, COLUMN_TILE)], out_sems.at[1 + 4 * number + 2 * what + side])
                copy.start()
                out_copies.append(copy)
    value = dots[...]
    if added:
        value = value + dx[:, width:].astype(F32)
    dx[:, width:] = value.astype(BF)
    last = 1 + 4 * (width // COLUMN_TILE)
    for side in range(2):
        copy = pltpu.make_async_copy(
            dx.at[pl.ds(side * rows, rows), pl.ds(width, LANES)], dx_refs[side].at[:, pl.ds(width, LANES)],
            out_sems.at[last + side])
        copy.start()
        out_copies.append(copy)
    for copy in out_copies:
        copy.wait()

def rows_call(core, router, moe_in, cotangent, carried, place, weights, number_here, each_device, before=None, waits=()):
    blocks, _, own, width = moe_in[0].shape
    rows = blocks * own
    experts, depth, _ = weights.shape
    number = router.shape[1]
    total = 2 * rows
    small = pl.BlockSpec((blocks, 1, own, number), lambda i: (0, place, 0, 0), pipeline_mode=pl.Buffered(1))
    operands = [core, router, *moe_in, *cotangent, *carried, weights]
    specs = [pl.BlockSpec(memory_space=pltpu.SMEM), whole(router.shape)] + [ANYWHERE] * 4 + [small] * 2 + [ANYWHERE]
    if before is not None:
        operands += before
        specs += [ANYWHERE] * 4
    operands += waits
    specs += [ANYWHERE] * len(waits)
    return pl.pallas_call(
        functools.partial(rows_kernel, place, number_here, each_device, before is not None, len(waits)),
        grid=(1,),
        in_specs=specs,
        out_specs=[ANYWHERE] * 5 + [whole((rows, number))],
        out_shape=[jax.ShapeDtypeStruct((rows, width), BF)] * 2
        + [jax.ShapeDtypeStruct((rows, width + LANES), BF)] * 2
        + [jax.ShapeDtypeStruct((total, experts * depth), BF), jax.ShapeDtypeStruct((rows, number), F32)],
        scratch_shapes=[
            pltpu.VMEM((total, width), BF), pltpu.VMEM((total, width), BF),
            pltpu.VMEM((experts * depth // 3, width), BF), pltpu.VMEM((2 * experts * depth // 3, width), BF),
            pltpu.VMEM((total, experts * depth), BF), pltpu.VMEM((total, width), BF), pltpu.VMEM((total, width + LANES), BF),
            pltpu.VMEM((total, number), F32), pltpu.VMEM((total, LANES), F32),
            pltpu.SemaphoreType.DMA((4 * blocks,)), pltpu.SemaphoreType.DMA((2 * experts,)), pltpu.SemaphoreType.DMA((4,)),
            pltpu.SemaphoreType.DMA((3 + 4 * (width // COLUMN_TILE),)),
        ],
        compiler_params=kernel_params(),
        cost_estimate=pl.CostEstimate(
            flops=4 * total * width * experts * depth, bytes_accessed=8 * total * width, transcendentals=0
        ),
        name="expert_rows",
    )(*operands)


def weight_grads_kernel(sides, halves, outs, added, skipped, order_ref, *refs):
    parts = sides * halves
    x_refs, dy_refs = refs[:parts], refs[parts : 2 * parts]
    kept_refs = refs[2 * parts : 2 * parts + 4 * halves]
    add_refs = refs[2 * parts + 4 * halves : 2 * parts + 4 * halves + added]
    out_refs, turned = refs[2 * parts + 4 * halves + added + skipped : -1], refs[-1]
    hid = turned.shape[0] // 6
    span = kept_refs[0].shape[0]
    rows = span // sides

    @pl.when(pl.program_id(0) == 0)
    def _():
        for h in range(halves):
            there = slice(h * span, (h + 1) * span)
            for one in range(2):
                units, grads = kept_refs[4 * h + 2 * one : 4 * h + 2 * one + 2]
                turned[one * hid : (one + 1) * hid, there] = units[...].T
                place = 2 * hid + one * 2 * hid
                turned[place : place + 2 * hid, there] = grads[...].T

    def total(first, last, refs):
        return sum(
            mul(turned[first:last, p * rows : (p + 1) * rows], ref[:, 0].reshape(rows, ref.shape[-1]))
            for p, ref in enumerate(refs)
        )

    down = total(0, 2 * hid, dy_refs)
    both = total(2 * hid, 6 * hid, x_refs)
    for one in range(2):
        value = jnp.concatenate(
            [down[one * hid : (one + 1) * hid], both[one * 2 * hid : (one + 1) * 2 * hid]], axis=0
        )
        if outs == 1:
            out_refs[0][one] = value.astype(BF)
            continue
        middle = value.shape[0] // 2
        for number, part in enumerate((value[:middle], value[middle:])):
            if added and number == one:
                part = part + add_refs[one][...].astype(F32)
            out_refs[2 * one + number][...] = part.astype(BF)


def weight_grads_call(moe_in, cotangent, kept, order, depth, addends=(), waits=(), pair=None, into=None):
    blocks, halves, own, width = moe_in[0].shape
    sides = len(moe_in)
    tile = COLUMN_TILE
    span = kept[0].shape[0]
    parts = [(h, side) for h in range(halves) for side in range(sides)]

    def column(h):
        return pl.BlockSpec((blocks, 1, own, tile), lambda i, order: (0, h, 0, i))

    hid = depth // 3
    experts = kept[0].shape[1] // depth

    def expert(one):
        return [
            pl.BlockSpec((span, hid), lambda i, order: (0, order[one]), pipeline_mode=pl.Buffered(1)),
            pl.BlockSpec((span, 2 * hid), lambda i, order: (0, experts // 2 + order[one]), pipeline_mode=pl.Buffered(1)),
        ]

    operands = [moe_in[side] for _, side in parts] + [cotangent[side] for _, side in parts]
    operands += [kept[h] for h in range(halves) for _ in range(4)]
    specs = [column(h) for h, _ in parts] * 2 + [spec for _ in range(halves) for one in range(2) for spec in expert(one)]
    operands += addends
    specs += [pl.BlockSpec((addend.shape[0], tile), lambda i, order: (0, i)) for addend in addends]
    aliases = {}
    if into is not None:
        waits = [into, *waits]
        aliases = {1 + len(operands): 0}
    if pair is None:
        outs = 4
        out_specs = [pl.BlockSpec((depth // 2, tile), lambda i, order: (0, i))] * 4
        out_shape = [jax.ShapeDtypeStruct((depth // 2, width), BF)] * 4
    else:
        outs = 1
        out_specs = pl.BlockSpec((2, depth, tile), lambda i, order: (pair, 0, i))
        out_shape = jax.ShapeDtypeStruct((kept[0].shape[1] // depth, depth, width), BF)
    return pl.pallas_call(
        functools.partial(weight_grads_kernel, sides, halves, outs, len(addends), len(waits)),
        grid_spec=pltpu.PrefetchScalarGridSpec(
            num_scalar_prefetch=1,
            grid=(width // tile,),
            in_specs=specs + [ANYWHERE] * len(waits),
            out_specs=out_specs,
            scratch_shapes=[pltpu.VMEM((2 * depth, halves * span), BF)],
        ),
        out_shape=out_shape,
        input_output_aliases=aliases,
        compiler_params=kernel_params(),
        cost_estimate=pl.CostEstimate(
            flops=4 * halves * span * width * depth,
            bytes_accessed=4 * halves * span * width + 8 * depth * width,
            transcendentals=0,
        ),
        name="expert_weight_grads",
    )(order, *operands, *waits)


def swap(values, bit):
    size = lax.axis_size(EXPERT)
    return lax.ppermute(values, EXPERT, [(i, i ^ bit) for i in range(size)])


def plus(left, right):
    return (left.astype(F32) + right.astype(F32)).astype(BF)


def relative_columns(values):
    here = lax.axis_index(EXPERT)
    size = lax.axis_size(EXPERT)
    span = values.shape[1] // size
    order = [*range(0, size, 2), *range(1, size, 2)]
    return jnp.concatenate(
        [lax.dynamic_slice_in_dim(values, (here ^ r) * span, span, 1) for r in order], axis=1
    )


def block_terms(values):
    rows = values.shape[0] // 4
    mine, to_two, to_four, across = (values[n * rows : (n + 1) * rows] for n in range(4))
    return (across[: rows // 2], across[rows // 2 :]), to_four, to_two, mine


def beside(terms, via):
    _, to_four, to_two, _ = terms
    middle = to_four.shape[0] // 2
    return (
        jnp.concatenate([plus(to_four[:middle], via[0]), to_four[middle:]], axis=0),
        jnp.concatenate([to_two[:middle], plus(to_two[middle:], via[1])], axis=0),
    )


def join(*values):
    return lax.optimization_barrier(values)


def scatter_tensor(values):
    return lax.psum_scatter(values, TENSOR, scatter_dimension=0, tiled=True)


HALVES = 2


def shards_near(
    tokens, cotangent, seq_lengths, expert_ids, slot_index, w_query, w_key, w_value, w_output,
    query_gain, key_gain, attn_gain, moe_gain, router, w_gate, w_up, w_down,
):
    rows, width = tokens.shape
    local = w_query.shape[1]
    groups = lax.axis_size(EXPERT)
    n_tensor = lax.axis_size(TENSOR)
    here = lax.axis_index(EXPERT)
    layer = lax.axis_index(TENSOR)
    experts_here, hid = w_gate.shape[0], w_gate.shape[2]
    experts_all = experts_here * groups
    own_rows = rows // n_tensor
    own = lambda array: lax.dynamic_slice_in_dim(array, layer * own_rows, own_rows, 0)
    view = lambda array: array.reshape(n_tensor, HALVES, own_rows // HALVES, array.shape[-1])
    half = range(HALVES)

    chips = groups // 2
    sides_of = [[2 * chip + core for chip in range(chips)] for core in (0, 1)]
    core = lax.rem(here, 2)

    core_rows = local // 2
    w_half = lax.dynamic_slice_in_dim(w_output, core * core_rows, core_rows, 0)
    w_mine = [swap_tensor(w_half, bits) for bits in (1, 2)]

    def pack(gate, up, down):
        return jnp.concatenate([down, gate.T, up.T], axis=0)

    def spread(value):
        return lax.all_gather(value, EXPERT, axis_index_groups=sides_of)

    depth = 3 * hid
    packed = [pack(w_gate[j], w_up[j], w_down[j]) for j in range(experts_here)]
    weights = [spread(packed[0])]
    number = jnp.arange(experts_all, dtype=jnp.int32)
    carried = (expert_ids[:, :, None] == number) & (slot_index >= 0)[:, :, None]
    carried = jnp.sum(carried.astype(BF), axis=1)
    segment, position = layout(seq_lengths, rows)
    cosine, sine = rope_angles(position, HEAD_DIM)
    cos_table = jnp.concatenate([cosine, cosine], axis=1)
    sin_table = jnp.concatenate([-sine, sine], axis=1)
    attn_in, inverse_in, query_raw, key_raw, values, totals = front_call(
        tokens, attn_gain[None], w_query, w_key, w_value, [*packed, cos_table, sin_table]
    )
    total = sum_small(totals.T.reshape(-1, LANES)).reshape(2, rows)
    total, w_mine[0], w_mine[1] = join(total, *w_mine)
    w_mine.append(swap_tensor(w_mine[1], 1))
    query_inverse = lax.rsqrt(total[0] / width + EPS)[:, None]
    key_inverse = lax.rsqrt(total[1] / width + EPS)[:, None]
    operands = [
        query_raw, key_raw, values, query_inverse, key_inverse, query_gain[None], key_gain[None],
        cos_table, sin_table, segment[:, None], segment[None],
    ]
    queries, keys, context, lse = attention_call(operands, rows, local)
    context_here = context
    far_context = swap_tensor(context, 2)
    near_context = swap_tensor(context, 1)
    w_mine[2], context = join(w_mine[2], context)
    near_context, far_context, *w_mine = join(near_context, far_context, *w_mine)
    contexts = [context, near_context, far_context, swap_tensor(far_context, 1)]
    w_mine = jnp.concatenate(w_mine, axis=0)
    w_other, packed[1], contexts[3] = join(swap(w_mine, 1), packed[1], contexts[3])
    w_all = [w_output, w_mine, w_other]
    weights.append(spread(packed[1]))
    carried_later, cotangent_later, contexts[0] = lax.optimization_barrier((carried, cotangent, contexts[0]))
    carried_sides = [view(carried), view(swap(carried_later, 1))]
    cotangent_sides = [view(cotangent), view(swap(cotangent_later, 1))]
    hidden_own, moe_low, inverse_own = hidden_call(
        jnp.stack([core, layer]).astype(jnp.int32), tokens, moe_gain[None], contexts, w_all
    )
    sides = [view(moe_low), view(swap(moe_low, 1))]
    router_wide = router.astype(F32)
    calls, kept, shares = [None, None], [{}, {}], [None, None]

    def run(h, j, *waits):
        before = None if calls[h] is None else calls[h][:4]
        calls[h] = rows_call(
            core[None], router, sides, cotangent_sides, carried_sides, h, weights[j], j, experts_here, before, waits
        )
        kept[h][j] = calls[h][4]
        shares[h] = calls[h][5]

    def send_back(h):
        terms = plus(calls[h][2], swap(calls[h][3], 1))
        return terms, scatter_tensor(terms)

    chip = here // 2

    def part(j, first, second, *rest, **more):
        order = jnp.stack([first, second]).astype(jnp.int32)
        return weight_grads_call(
            sides, cotangent_sides, [kept[h][j] for h in half], order, depth, *rest, **more
        )

    def send(terms, bits):
        return [swap(term, bit) for term, bit in zip(terms, bits)]

    run(0, 0)
    run(1, 0, calls[0][4])
    *far, mine_low, mine_high = part(0, chip ^ 3, chip)
    via = send(far, (2, 4))
    run(0, 1, *far)
    *calls[0], via[0], via[1] = join(*calls[0], *via)
    kept[0][1] = calls[0][4]
    terms, sums_first = send_back(0)
    run(1, 1, terms)
    *calls[1], sums_first = join(*calls[1], sums_first)
    kept[1][1] = calls[1][4]
    terms, sums_second = send_back(1)
    near = part(0, chip ^ 2, chip ^ 1, via, [terms])
    near_low = send(near[::2], (4, 2))
    second = part(1, 0 * chip, 0 * chip + 1, (), [near[0]], pair=0)
    sums_second, second, attn_in, *moe_terms = join(sums_second, second, attn_in, *calls[0][:2], *calls[1][:2])
    moe_terms = [plus(moe_terms[2 * h], swap(moe_terms[2 * h + 1], 1)) for h in half]
    moe_terms = jnp.stack([term.reshape(n_tensor, -1, width) for term in moe_terms], axis=1).reshape(rows, width)
    sums = jnp.concatenate([sums_first, sums_second], axis=0)
    dshares = sums[:, width : width + experts_all].astype(F32) * own(carried).astype(F32)
    share = jnp.concatenate(
        [lax.dynamic_slice_in_dim(item, layer * (own_rows // HALVES), own_rows // HALVES, 0) for item in shares], axis=0
    )
    moe_in = hidden_own * inverse_own * moe_gain
    dlogits = share * (dshares - jnp.sum(share * dshares, axis=-1, keepdims=True))
    router_back = jnp.einsum("te,de->td", dlogits, router_wide, precision=lax.Precision.HIGHEST)
    grad_norm_moe, grad_moe_gain = norm_back(
        hidden_own, inverse_own, moe_gain, sums[:, :width].astype(F32) + router_back
    )
    grad_hidden = own(cotangent).astype(F32) + grad_norm_moe
    grad_low = grad_hidden.astype(BF)

    by_head, by_mine, by_other = (mul(grad_low, weight, NT).astype(BF) for weight in w_all)
    core_columns = local // 2
    grad_context = jnp.zeros((rows, local), BF)
    for bits in range(n_tensor):
        if bits == 0:
            came = by_head
        else:
            columns = slice((bits - 1) * core_columns, bits * core_columns)
            mine, other = by_mine[:, columns], by_other[:, columns]
            lower = jnp.where(core == 0, mine, other)
            upper = jnp.where(core == 0, other, mine)
            came = swap_tensor(jnp.concatenate([lower, upper], axis=1), bits)
        grad_context = lax.dynamic_update_slice_in_dim(grad_context, came, (layer ^ bits) * own_rows, 0)
    heads_own = jnp.concatenate([own(item) for item in contexts], axis=1)
    output_grads = mul(relative_columns(grad_low), heads_own, TN).astype(BF)
    output_grads = [output_grads[: width // 2], output_grads[width // 2 :]]
    attn_relative = relative_columns(attn_in)
    router_part = jnp.einsum("td,te->de", moe_in, dlogits, precision=lax.Precision.HIGHEST)
    grad_context, moe_terms, attn_relative, router_part, *output_grads = join(
        grad_context, moe_terms, attn_relative, router_part, *output_grads
    )
    moe = scatter_tensor(moe_terms)
    came = swap(output_grads[1], 1)
    back = attention_back_call(
        operands + [queries, keys, context_here, lse, grad_context], rows, local, [output_grads[1]]
    )
    *back, came, near_low[0], near_low[1] = join(*back, came, *near_low)
    near_high = send(near[1::2], (4, 2))
    dq, dk, value_low, inner, grad_query_gain, grad_key_gain = back
    inner = jnp.sum(inner, axis=0).T
    inner = sum_small(inner.reshape(-1, LANES)).reshape(inner.shape)
    output_grads = block_terms(plus(output_grads[0], came))
    output_via = send(output_grads[0], (2, 4))
    second = part(1, 0 * chip + 2, 0 * chip + 3, (), [inner], pair=1, into=second)
    inner, moe, second, *output_via, near_high[0], near_high[1] = join(inner, moe, second, *output_via, *near_high)
    grads_one = lax.psum_scatter(
        second.reshape(-1, width), EXPERT, scatter_dimension=0, axis_index_groups=sides_of, tiled=True
    )
    out_own = (hidden_own + moe.astype(F32)).astype(BF)
    came = exchange(out_own, out_own)

    def raw_grad(scaled, raw, inverse, total):
        return (inverse * scaled - raw * inverse * inverse * inverse * (total / width)[:, None]).astype(BF)

    query_low = raw_grad(dq, query_raw, query_inverse, inner[0])
    key_low = raw_grad(dk, key_raw, key_inverse, inner[1])
    lows = jnp.concatenate([query_low, key_low, value_low], axis=1)
    wide = jnp.concatenate([w_query, w_key, w_value], axis=1)
    terms_in = mul(lows, wide, NT).astype(BF)
    def expert_outputs(grads):
        return grads[hid : 2 * hid].T, grads[2 * hid :].T, grads[:hid]

    outputs_zero = jnp.concatenate([
        (mine.astype(F32) + near[0].astype(F32) + near[1].astype(F32)).astype(BF)
        for mine, near in ((mine_low, near_low), (mine_high, near_high))], axis=0)
    outputs_zero = list(expert_outputs(outputs_zero))
    output_near = send(beside(output_grads, output_via), (4, 2))
    grad_attn_gain = jnp.sum(terms_in.astype(F32) * tokens.astype(F32) * inverse_in, axis=0)
    *came, terms_in, lows, grad_attn_gain = join(*came, terms_in, lows, grad_attn_gain)
    out_above, out_below = [from_above(came)], [from_below(came)]
    chunk = lambda place: lax.dynamic_slice_in_dim(terms_in, jnp.clip(place, 0, n_tensor - 1) * own_rows, own_rows, 0)
    sum_above = sum_below = jnp.zeros((), BF)
    for step in range(1, n_tensor):
        came = exchange(
            jnp.where(
                layer >= n_tensor - step, plus(chunk(layer - n_tensor + step), sum_above), out_above[-1]
            ),
            jnp.where(layer < step, plus(chunk(layer + n_tensor - step), sum_below), out_below[-1]),
        )
        if step == 1:
            own_width, span = width // groups, local // groups
            spread_gain = lambda gain: jnp.pad(
                gain.reshape(groups, span), ((0, 0), (0, own_width - span))
            ).reshape(width, 1)
            small = jnp.concatenate([
                router_part, grad_moe_gain[:, None], grad_attn_gain[:, None],
                spread_gain(grad_query_gain), spread_gain(grad_key_gain)], axis=1).astype(BF)
            small = jnp.pad(small, ((0, 0), (0, LANES - small.shape[1])))
            blocks = jnp.concatenate([
                mul(attn_relative, lows, TN).astype(BF), relative_columns(small.T).T], axis=1)
            blocks = [blocks[: width // 2], blocks[width // 2 :]]
            *came, blocks[0], blocks[1] = join(*came, *blocks)
            blocks_came = swap(blocks[1], 1)
        elif step == 2:
            came[0], came[1], blocks_came, *outputs_zero = join(*came, blocks_came, *outputs_zero)
            blocks = block_terms(plus(blocks[0], blocks_came))
            via = send(blocks[0], (2, 4))
        else:
            *came, via[0], via[1] = join(*came, *via)
        above, below = from_above(came), from_below(came)
        sum_above = jnp.where(layer == n_tensor - 1, 0, above)
        sum_below = jnp.where(layer == 0, 0, below)
        if step < n_tensor - 1:
            out_above.append(above)
            out_below.append(below)
    grad_normed = own(terms_in).astype(F32) + sum_above.astype(F32) + sum_below.astype(F32)
    out = end_line(out_own, out_above, out_below)

    grad_norm_in, _ = norm_back(own(tokens).astype(F32), own(inverse_in), attn_gain, grad_normed)
    grad_input = (grad_hidden + grad_norm_in).astype(BF)
    input_above, input_below = [grad_input], [grad_input]
    for step in range(1, n_tensor):
        came = exchange(input_above[-1], input_below[-1])
        if step == 1:
            near = send(beside(blocks, via), (4, 2))
            *came, output_near[0], output_near[1] = join(*came, *output_near)
        if step == 2:
            *came, near[0], near[1], grads_one = join(*came, *near, grads_one)
        input_above.append(from_above(came))
        input_below.append(from_below(came))
    projections = sum((item.astype(F32) for item in near), blocks[3].astype(F32))
    small = projections[:, 3 * local :]
    projections = projections[:, : 3 * local].astype(BF)
    by_index = sum((item.astype(F32) for item in output_near), output_grads[3].astype(F32))
    grad_w_output, shared = by_index[:, :local], small
    for bits in range(1, n_tensor):
        terms = jnp.concatenate([by_index[:, bits * local : (bits + 1) * local], small], axis=1)
        came = swap_tensor(terms.astype(BF), bits).astype(F32)
        grad_w_output, shared = grad_w_output + came[:, :local], shared + came[:, local:]
    grad_w_output = grad_w_output.T
    grad_input = end_line(grad_input, input_above[1:], input_below[1:])

    gains = small[:span, experts_all + 2 : experts_all + 4].astype(BF)
    return (
        out, grad_input,
        projections[:, :local], projections[:, local : 2 * local], projections[:, 2 * local : 3 * local],
        grad_w_output.astype(BF),
        gains[:, 0], gains[:, 1], shared[:, experts_all + 1].astype(BF), shared[:, experts_all].astype(BF),
        shared[:, :experts_all].astype(BF),
        *(jnp.stack(pair) for pair in zip(outputs_zero, expert_outputs(grads_one))),
    )


def swap_tensor(values, bit):
    size = lax.axis_size(TENSOR)
    return lax.ppermute(values, TENSOR, [(i, i ^ bit) for i in range(size)])


def scatter_halving(values):
    place = lax.axis_index(TENSOR)
    rows = values.shape[0] // lax.axis_size(TENSOR)
    cut = lambda bits: lax.dynamic_slice_in_dim(values, (place ^ bits) * rows, rows, 0)
    passed = swap_tensor(plus(cut(2), swap_tensor(cut(3), 1)), 2)
    return cut(0).astype(F32) + swap_tensor(cut(1), 1).astype(F32) + passed.astype(F32), passed


def scatter_direct(values):
    place = lax.axis_index(TENSOR)
    size = lax.axis_size(TENSOR)
    rows = values.shape[0] // size
    cut = lambda bits: lax.dynamic_slice_in_dim(values, (place ^ bits) * rows, rows, 0)
    return sum((swap_tensor(cut(bits), bits).astype(F32) for bits in range(1, size)), cut(0).astype(F32))


def exchange(to_below, to_above):
    place = lax.axis_index(TENSOR)
    even = lax.rem(place, 2) == 0
    outer = lax.ppermute(jnp.where(even, to_above, to_below), TENSOR, [(0, 1), (1, 0), (2, 3), (3, 2)])
    inner = lax.ppermute(jnp.where(even, to_below, to_above), TENSOR, [(1, 2), (2, 1), (0, 0), (3, 3)])
    return [outer, inner]


def from_above(came):
    return jnp.where(lax.rem(lax.axis_index(TENSOR), 2) == 0, came[0], came[1])


def from_below(came):
    return jnp.where(lax.rem(lax.axis_index(TENSOR), 2) == 0, came[1], came[0])


def end_line(values, above, below):
    place = lax.axis_index(TENSOR)
    size = lax.axis_size(TENSOR)
    rows = values.shape[0]
    everything = jnp.zeros((rows * size,) + values.shape[1:], values.dtype)
    everything = lax.dynamic_update_slice_in_dim(everything, values, place * rows, 0)
    for ahead in range(1, size):
        piece = jnp.where(place + ahead < size, above[ahead - 1], below[size - ahead - 1])
        everything = lax.dynamic_update_slice_in_dim(everything, piece, lax.rem(place + ahead, size) * rows, 0)
    return everything


def exchange_doubling(values):
    far = swap_tensor(values, 2)
    return [swap_tensor(values, 1), far, swap_tensor(far, 1)]


def start_gather(values):
    return [swap_tensor(values, bits) for bits in range(1, lax.axis_size(TENSOR))]


def end_gather(values, came):
    place = lax.axis_index(TENSOR)
    rows = values.shape[0]
    everything = jnp.zeros((rows * (1 + len(came)),) + values.shape[1:], values.dtype)
    for bits, piece in enumerate((values, *came)):
        everything = lax.dynamic_update_slice_in_dim(everything, piece, (place ^ bits) * rows, 0)
    return everything


def gather_doubling(values):
    place = lax.axis_index(TENSOR)
    rows = values.shape[0]
    far = swap_tensor(values, 2)
    pieces = {0: values, 1: swap_tensor(values, 1), 2: far, 3: swap_tensor(far, 1)}
    everything = jnp.zeros((rows * lax.axis_size(TENSOR),) + values.shape[1:], values.dtype)
    for bits, piece in pieces.items():
        everything = lax.dynamic_update_slice_in_dim(everything, piece, (place ^ bits) * rows, 0)
    return everything


def mix_halves(values):
    size = lax.axis_size(TENSOR)
    view = values.reshape(HALVES, size, -1, values.shape[-1])
    return jnp.swapaxes(view, 0, 1).reshape(values.shape)


def unmix_halves(values):
    size = lax.axis_size(TENSOR)
    view = values.reshape(size, HALVES, -1, values.shape[-1])
    return jnp.swapaxes(view, 0, 1).reshape(values.shape)


def rotations():
    size = lax.axis_size(TENSOR)
    return [[(i, (i + d) % size) for i in range(size)] for d in range(1, size)]


def sum_small(values):
    total = values
    for pairs in rotations():
        total = total + lax.ppermute(values, TENSOR, pairs)
    return total


def gather_small(values):
    rows = values.shape[0]
    size = lax.axis_size(TENSOR)
    place = lax.axis_index(TENSOR)
    whole_rows = jnp.zeros((rows * size,) + values.shape[1:], values.dtype)
    whole_rows = lax.dynamic_update_slice_in_dim(whole_rows, values, place * rows, 0)
    for d, pairs in enumerate(rotations(), 1):
        came = lax.ppermute(values, TENSOR, pairs)
        whole_rows = lax.dynamic_update_slice_in_dim(whole_rows, came, lax.rem(place + size - d, size) * rows, 0)
    return whole_rows


def scatter_small(values):
    size = lax.axis_size(TENSOR)
    place = lax.axis_index(TENSOR)
    rows = values.shape[0] // size
    cut = lambda index: lax.dynamic_slice_in_dim(values, index * rows, rows, 0)
    total = cut(place)
    for d, pairs in enumerate(rotations(), 1):
        total = total + lax.ppermute(cut(lax.rem(place + d, size)), TENSOR, pairs)
    return total


NEAR_GROUPS = 8


def solution(mesh):
    placed = (
        P(EXPERT, None),
        P(EXPERT, None),
        P(EXPERT),
        P(EXPERT, None),
        P(EXPERT, None),
        P(None, TENSOR),
        P(None, TENSOR),
        P(None, TENSOR),
        P(TENSOR, None),
        P(TENSOR),
        P(TENSOR),
        P(),
        P(),
        P(),
        P(EXPERT, None, TENSOR),
        P(EXPERT, None, TENSOR),
        P(EXPERT, TENSOR, None),
    )
    return jax.shard_map(
        shards_near if mesh.shape[EXPERT] == NEAR_GROUPS else shards,
        mesh=mesh,
        in_specs=placed,
        out_specs=(
            P(EXPERT, None),
            P(EXPERT, None),
            P(EXPERT, TENSOR),
            P(EXPERT, TENSOR),
            P(EXPERT, TENSOR),
            P(TENSOR, EXPERT),
            P((TENSOR, EXPERT)),
            P((TENSOR, EXPERT)),
            P(EXPERT),
            P(EXPERT),
            P(EXPERT, None),
            P(EXPERT, None, TENSOR),
            P(EXPERT, None, TENSOR),
            P(EXPERT, TENSOR, None),
        ),
        check_vma=False,
    )
```

```python
import functools

import jax
import jax.numpy as jnp
from jax import lax
from jax.experimental import pallas as pl
from jax.experimental.pallas import tpu as pltpu
from jax.sharding import PartitionSpec as P

HEAD_DIM = 128
EXPERT = "expert"
TENSOR = "tensor"
TOP = 8


EPS = 1e-05
THETA = 10000.0
NEG = -1e30


def norm_rows(values, gain):
    inverse = lax.rsqrt(jnp.mean(values * values, axis=-1, keepdims=True) + EPS)
    return (values * inverse * gain, inverse)


def norm_back(values, inverse, gain, upstream):
    scaled = upstream * gain
    inner = jnp.mean(values * scaled, axis=-1, keepdims=True)
    grad_values = inverse * scaled - values * inverse * inverse * inverse * inner
    grad_gain = jnp.sum(upstream * values * inverse, axis=0)
    return (grad_values, grad_gain)


def layout(lengths, rows):
    ends = jnp.cumsum(lengths, axis=-1)
    starts = ends - lengths
    places = jnp.arange(rows, dtype=jnp.int32)
    inside = (
        (places[..., :, None] >= starts[..., None, :]) & (places[..., :, None] < ends[..., None, :])
    ).astype(jnp.int32)
    number = jnp.arange(lengths.shape[-1], dtype=jnp.int32)
    alive = jnp.sum(inside, axis=-1)
    segment = jnp.sum(inside * number, axis=-1) + (1 - alive) * (lengths.shape[-1] + places)
    position = jnp.sum(inside * (places[..., :, None] - starts[..., None, :]), axis=-1)
    return (segment, position)


def rope_angles(position, head_size):
    half = head_size // 2
    freq = THETA ** (-2.0 * jnp.arange(half, dtype=jnp.float32) / head_size)
    angle = position.astype(jnp.float32)[..., None] * freq
    return (jnp.cos(angle), jnp.sin(angle))


def rotate(values, cosine, sine):
    half = values.shape[-1] // 2
    first, second = (values[..., :half], values[..., half:])
    cos_here = cosine[..., None, :]
    sin_here = sine[..., None, :]
    return jnp.concatenate(
        [first * cos_here - second * sin_here, second * cos_here + first * sin_here], axis=-1
    )


def unrotate(grads, cosine, sine):
    half = grads.shape[-1] // 2
    first, second = (grads[..., :half], grads[..., half:])
    cos_here = cosine[..., None, :]
    sin_here = sine[..., None, :]
    return jnp.concatenate(
        [first * cos_here + second * sin_here, second * cos_here - first * sin_here], axis=-1
    )


def block_scores(query_block, keys, seg_block, segment, start):
    scores = jnp.einsum(
        "qhd,khd->hqk", query_block, keys, preferred_element_type=jnp.float32
    ) * HEAD_DIM ** (-0.5)
    rows_query = start + jnp.arange(query_block.shape[0], dtype=jnp.int32)
    rows_key = jnp.arange(keys.shape[0], dtype=jnp.int32)
    allowed = (seg_block[:, None] == segment[None, :]) & (rows_key[None, :] <= rows_query[:, None])
    return jnp.where(allowed[None], scores, NEG)


def attention_forward(queries, keys, values, segment, block):
    rows = queries.shape[0]

    def one_block(index):
        start = index * block
        query_block = lax.dynamic_slice_in_dim(queries, start, block, 0)
        seg_block = lax.dynamic_slice_in_dim(segment, start, block, 0)
        scores = block_scores(query_block, keys, seg_block, segment, start)
        top = jnp.max(scores, axis=-1, keepdims=True)
        raised = jnp.exp(scores - top)
        total = jnp.sum(raised, axis=-1, keepdims=True)
        weights = (raised / total).astype(jnp.bfloat16)
        context = jnp.einsum("hqk,khd->qhd", weights, values, preferred_element_type=jnp.float32)
        return (context, top, total)

    context, top, total = lax.map(one_block, jnp.arange(rows // block, dtype=jnp.int32))
    return (context.reshape(queries.shape), top, total)


def attention_backward(queries, keys, values, segment, block, top, total, grad_context):
    rows = queries.shape[0]
    scale = HEAD_DIM ** (-0.5)

    def one_block(carry, index):
        grad_keys, grad_values = carry
        start = index * block
        query_block = lax.dynamic_slice_in_dim(queries, start, block, 0)
        seg_block = lax.dynamic_slice_in_dim(segment, start, block, 0)
        grad_block = lax.dynamic_slice_in_dim(grad_context, start, block, 0)
        scores = block_scores(query_block, keys, seg_block, segment, start)
        weights_f = jnp.exp(scores - top[index]) / total[index]
        weights = weights_f.astype(jnp.bfloat16)
        grad_weights = jnp.einsum(
            "qhd,khd->hqk", grad_block, values, preferred_element_type=jnp.float32
        )
        inner = jnp.sum(weights_f * grad_weights, axis=-1, keepdims=True)
        grad_scores = (weights_f * (grad_weights - inner)).astype(jnp.bfloat16)
        grad_query = (
            jnp.einsum("hqk,khd->qhd", grad_scores, keys, preferred_element_type=jnp.float32)
            * scale
        )
        grad_keys = (
            grad_keys
            + jnp.einsum(
                "hqk,qhd->khd", grad_scores, query_block, preferred_element_type=jnp.float32
            )
            * scale
        )
        grad_values = grad_values + jnp.einsum(
            "hqk,qhd->khd", weights, grad_block, preferred_element_type=jnp.float32
        )
        return ((grad_keys, grad_values), grad_query)

    empty = jnp.zeros(keys.shape, jnp.float32)
    (grad_keys, grad_values), grad_query = lax.scan(
        one_block, (empty, empty), jnp.arange(rows // block, dtype=jnp.int32)
    )
    return (grad_query.reshape(queries.shape), grad_keys, grad_values)


def shards(
    tokens,
    cotangent,
    seq_lengths,
    expert_ids,
    slot_index,
    w_query,
    w_key,
    w_value,
    w_output,
    query_gain,
    key_gain,
    attn_gain,
    moe_gain,
    router,
    w_gate,
    w_up,
    w_down,
):
    rows, width = tokens.shape
    local = w_query.shape[1]
    heads_here = local // HEAD_DIM
    groups = lax.axis_size(EXPERT)
    experts_here = w_gate.shape[0]
    experts_all = experts_here * groups
    capacity = max(2, 3 * rows * TOP // (4 * experts_all))
    block = min(512, rows)
    shape_heads = (rows, heads_here, HEAD_DIM)
    segment, position = layout(seq_lengths, rows)
    cosine, sine = rope_angles(position, HEAD_DIM)
    inputs = tokens.astype(jnp.float32)
    normed, inverse_in = norm_rows(inputs, attn_gain)
    attn_in = normed.astype(jnp.bfloat16)
    query_raw = jnp.dot(attn_in, w_query, preferred_element_type=jnp.float32)
    key_raw = jnp.dot(attn_in, w_key, preferred_element_type=jnp.float32)
    value_raw = jnp.dot(attn_in, w_value, preferred_element_type=jnp.float32)
    query_total, key_total = lax.psum(
        (jnp.sum(query_raw * query_raw, axis=-1), jnp.sum(key_raw * key_raw, axis=-1)), TENSOR
    )
    query_inverse = lax.rsqrt(query_total / width + EPS)[:, None]
    key_inverse = lax.rsqrt(key_total / width + EPS)[:, None]
    queries = rotate(
        (query_raw * query_inverse * query_gain).reshape(shape_heads), cosine, sine
    ).astype(jnp.bfloat16)
    keys = rotate((key_raw * key_inverse * key_gain).reshape(shape_heads), cosine, sine).astype(
        jnp.bfloat16
    )
    values = value_raw.reshape(shape_heads).astype(jnp.bfloat16)
    context, top, total = attention_forward(queries, keys, values, segment, block)
    context_low = context.reshape(rows, local).astype(jnp.bfloat16)
    attn = lax.psum(
        jnp.dot(context_low, w_output, preferred_element_type=jnp.float32).astype(jnp.bfloat16),
        TENSOR,
    ).astype(jnp.float32)
    hidden_in = inputs + attn
    moe_in, inverse_moe = norm_rows(hidden_in, moe_gain)
    router_wide = router.astype(jnp.float32)
    shares = jax.nn.softmax(jnp.dot(moe_in, router_wide, precision=lax.Precision.HIGHEST), axis=-1)
    chosen = expert_ids[:, :, None] == jnp.arange(experts_all, dtype=jnp.int32)[None, None, :]
    gates = jnp.sum(jnp.where(chosen, shares[:, None, :], 0.0), axis=-1)
    kept = slot_index >= 0
    target_slot = jnp.where(
        kept, expert_ids * capacity + slot_index, experts_all * capacity
    ).reshape(-1)
    token_of = (
        jnp.full((experts_all * capacity,), -1, jnp.int32)
        .at[target_slot]
        .set(jnp.repeat(jnp.arange(rows, dtype=jnp.int32), TOP), mode="drop")
    )
    gate_of = (
        jnp.zeros((experts_all * capacity,), jnp.float32)
        .at[target_slot]
        .set(gates.reshape(-1), mode="drop")
    )
    filled = (token_of >= 0)[:, None]
    source_row = jnp.maximum(token_of, 0)
    moe_low = moe_in.astype(jnp.bfloat16)
    send_rows = jnp.where(filled, moe_low[source_row], jnp.zeros((), jnp.bfloat16)).reshape(
        groups, experts_here * capacity, width
    )
    arrived = lax.all_to_all(send_rows, EXPERT, split_axis=0, concat_axis=0, tiled=True)
    arrived = arrived.reshape(groups, experts_here, capacity, width)
    gate_pre = jnp.einsum("secd,edf->secf", arrived, w_gate, preferred_element_type=jnp.float32)
    up_pre = jnp.einsum("secd,edf->secf", arrived, w_up, preferred_element_type=jnp.float32)
    activated = jax.nn.silu(gate_pre)
    hidden = (activated * up_pre).astype(jnp.bfloat16)
    partial_value = jnp.einsum(
        "secf,efd->secd", hidden, w_down, preferred_element_type=jnp.float32
    ).astype(jnp.bfloat16)
    dy_rows = jnp.where(filled, cotangent[source_row], jnp.zeros((), jnp.bfloat16))
    returned = lax.all_to_all(partial_value, EXPERT, split_axis=0, concat_axis=0, tiled=True)
    returned = returned.reshape(experts_all * capacity, width).astype(jnp.float32)
    moe_part = jax.ops.segment_sum(returned * gate_of[:, None], source_row, num_segments=rows)
    moe = lax.psum(moe_part.astype(jnp.bfloat16), TENSOR).astype(jnp.float32)
    row_dots = jnp.sum(dy_rows.astype(jnp.float32) * returned, axis=-1)
    out = (hidden_in + moe).astype(jnp.bfloat16)
    grad_gate = jnp.take(row_dots, target_slot, mode="fill", fill_value=0.0).reshape(rows, TOP)
    grad_shares = jnp.sum(jnp.where(chosen, grad_gate[:, :, None], 0.0), axis=1)
    grad_logits = shares * (grad_shares - jnp.sum(shares * grad_shares, axis=-1, keepdims=True))
    router_back = jnp.einsum("te,de->td", grad_logits, router_wide, precision=lax.Precision.HIGHEST)
    router_part = jnp.einsum("td,te->de", moe_in, grad_logits, precision=lax.Precision.HIGHEST)
    grad_rows = (
        (dy_rows.astype(jnp.float32) * gate_of[:, None])
        .astype(jnp.bfloat16)
        .reshape(groups, experts_here * capacity, width)
    )
    grad_arrived = lax.all_to_all(grad_rows, EXPERT, split_axis=0, concat_axis=0, tiled=True)
    grad_arrived = grad_arrived.reshape(groups, experts_here, capacity, width)
    grad_hidden = jnp.einsum(
        "secd,efd->secf", grad_arrived, w_down, preferred_element_type=jnp.float32
    )
    grad_w_down = jnp.einsum(
        "secf,secd->efd", hidden, grad_arrived, preferred_element_type=jnp.float32
    )
    sigma = jax.nn.sigmoid(gate_pre)
    grad_gate_pre = (grad_hidden * up_pre * sigma * (1.0 + gate_pre * (1.0 - sigma))).astype(
        jnp.bfloat16
    )
    grad_up_pre = (grad_hidden * activated).astype(jnp.bfloat16)
    grad_w_gate = jnp.einsum(
        "secd,secf->edf", arrived, grad_gate_pre, preferred_element_type=jnp.float32
    )
    grad_w_up = jnp.einsum(
        "secd,secf->edf", arrived, grad_up_pre, preferred_element_type=jnp.float32
    )
    grad_in_rows = jnp.einsum(
        "secf,edf->secd", grad_gate_pre, w_gate, preferred_element_type=jnp.float32
    )
    grad_in_rows = (
        grad_in_rows
        + jnp.einsum("secf,edf->secd", grad_up_pre, w_up, preferred_element_type=jnp.float32)
    ).astype(jnp.bfloat16)
    back_rows = lax.all_to_all(
        grad_in_rows.reshape(groups, experts_here * capacity, width),
        EXPERT,
        split_axis=0,
        concat_axis=0,
        tiled=True,
    )
    back_rows = back_rows.reshape(experts_all * capacity, width).astype(jnp.float32)
    moe_back = jax.ops.segment_sum(back_rows, source_row, num_segments=rows)
    grad_moe_in, grad_router_rows = (
        lax.psum((moe_back + router_back).astype(jnp.bfloat16), TENSOR).astype(jnp.float32),
        lax.psum(router_part.astype(jnp.bfloat16), TENSOR).astype(jnp.float32),
    )
    grad_norm_moe, grad_moe_gain = norm_back(hidden_in, inverse_moe, moe_gain, grad_moe_in)
    grad_hidden_in = cotangent.astype(jnp.float32) + grad_norm_moe
    grad_low = grad_hidden_in.astype(jnp.bfloat16)
    grad_w_output = jnp.einsum(
        "tf,td->fd", context_low, grad_low, preferred_element_type=jnp.float32
    )
    grad_context = (
        jnp.einsum("td,fd->tf", grad_low, w_output, preferred_element_type=jnp.float32)
        .astype(jnp.bfloat16)
        .reshape(shape_heads)
    )
    grad_queries, grad_keys, grad_values = attention_backward(
        queries, keys, values, segment, block, top, total, grad_context
    )
    grad_query_normed = unrotate(grad_queries, cosine, sine).reshape(rows, local)
    grad_key_normed = unrotate(grad_keys, cosine, sine).reshape(rows, local)
    query_scaled = grad_query_normed * query_gain
    key_scaled = grad_key_normed * key_gain
    query_inner, key_inner = lax.psum(
        (jnp.sum(query_raw * query_scaled, axis=-1), jnp.sum(key_raw * key_scaled, axis=-1)),
        TENSOR,
    )
    grad_query_raw = (
        query_inverse * query_scaled
        - query_raw * query_inverse * query_inverse * query_inverse * (query_inner / width)[:, None]
    )
    grad_key_raw = (
        key_inverse * key_scaled
        - key_raw * key_inverse * key_inverse * key_inverse * (key_inner / width)[:, None]
    )
    grad_query_gain = jnp.sum(grad_query_normed * query_raw * query_inverse, axis=0)
    grad_key_gain = jnp.sum(grad_key_normed * key_raw * key_inverse, axis=0)
    query_low = grad_query_raw.astype(jnp.bfloat16)
    key_low = grad_key_raw.astype(jnp.bfloat16)
    value_low = grad_values.reshape(rows, local).astype(jnp.bfloat16)
    grad_w_query = jnp.einsum("td,tf->df", attn_in, query_low, preferred_element_type=jnp.float32)
    grad_w_key = jnp.einsum("td,tf->df", attn_in, key_low, preferred_element_type=jnp.float32)
    grad_w_value = jnp.einsum("td,tf->df", attn_in, value_low, preferred_element_type=jnp.float32)
    terms_in = jnp.einsum("tf,df->td", query_low, w_query, preferred_element_type=jnp.float32)
    terms_in = terms_in + jnp.einsum(
        "tf,df->td", key_low, w_key, preferred_element_type=jnp.float32
    )
    terms_in = terms_in + jnp.einsum(
        "tf,df->td", value_low, w_value, preferred_element_type=jnp.float32
    )
    grad_normed = lax.psum(terms_in.astype(jnp.bfloat16), TENSOR).astype(jnp.float32)
    grad_norm_in, grad_attn_gain = norm_back(inputs, inverse_in, attn_gain, grad_normed)
    grad_input = (grad_hidden_in + grad_norm_in).astype(jnp.bfloat16)
    sums = (
        lax.psum_scatter(
            grad_w_query.astype(jnp.bfloat16), EXPERT, scatter_dimension=0, tiled=True
        ).astype(jnp.float32),
        lax.psum_scatter(
            grad_w_key.astype(jnp.bfloat16), EXPERT, scatter_dimension=0, tiled=True
        ).astype(jnp.float32),
        lax.psum_scatter(
            grad_w_value.astype(jnp.bfloat16), EXPERT, scatter_dimension=0, tiled=True
        ).astype(jnp.float32),
        lax.psum_scatter(
            grad_w_output.astype(jnp.bfloat16), EXPERT, scatter_dimension=1, tiled=True
        ).astype(jnp.float32),
        lax.psum_scatter(
            grad_query_gain.astype(jnp.bfloat16), EXPERT, scatter_dimension=0, tiled=True
        ).astype(jnp.float32),
        lax.psum_scatter(
            grad_key_gain.astype(jnp.bfloat16), EXPERT, scatter_dimension=0, tiled=True
        ).astype(jnp.float32),
        lax.psum_scatter(
            grad_attn_gain.astype(jnp.bfloat16), EXPERT, scatter_dimension=0, tiled=True
        ).astype(jnp.float32),
        lax.psum_scatter(
            grad_moe_gain.astype(jnp.bfloat16), EXPERT, scatter_dimension=0, tiled=True
        ).astype(jnp.float32),
        lax.psum_scatter(
            grad_router_rows.astype(jnp.bfloat16), EXPERT, scatter_dimension=0, tiled=True
        ).astype(jnp.float32),
    )
    lows = tuple((item.astype(jnp.bfloat16) for item in sums))
    return (
        out,
        grad_input,
        lows[0],
        lows[1],
        lows[2],
        lows[3],
        lows[4],
        lows[5],
        lows[6],
        lows[7],
        lows[8],
        grad_w_gate.astype(jnp.bfloat16),
        grad_w_up.astype(jnp.bfloat16),
        grad_w_down.astype(jnp.bfloat16),
    )


F32 = jnp.float32
BF = jnp.bfloat16
NN = (((1,), (0,)), ((), ()))
NT = (((1,), (1,)), ((), ()))
TN = (((0,), (0,)), ((), ()))
VMEM_BYTES = 62 * 2**20
COLUMN_TILE = 512
ROW_TILE = 512
QUERY_TILE = 512
BACK_TILE = 128
HIDDEN_TILE = 256
LANES = 128
LOG2_E = 1.4426950408889634


def mul(left, right, dims=NN):
    return lax.dot_general(left, right, dims, preferred_element_type=F32)


def kernel_params():
    return pltpu.CompilerParams(vmem_limit_bytes=VMEM_BYTES)


def whole(shape):
    return pl.BlockSpec(shape, lambda i: (0,) * len(shape), pipeline_mode=pl.Buffered(1))


def fill_bias(bias, row_ref, col_ref):
    @pl.when(pl.program_id(0) == 0)
    def _():
        rows = lax.broadcasted_iota(jnp.int32, bias.shape, 0)
        columns = lax.broadcasted_iota(jnp.int32, bias.shape, 1)
        allowed = (row_ref[...] == col_ref[...]) & (columns <= rows)
        bias[...] = jnp.where(allowed, 0.0, NEG)


def score_block(queries, keys, bias):
    return mul(queries, keys, NT) * (HEAD_DIM**-0.5 * LOG2_E) + bias


ANYWHERE = pl.BlockSpec(memory_space=pl.ANY)


def front_kernel(tokens_ref, gain_ref, wq_ref, wk_ref, wv_ref, *refs):
    low_ref, inverse_ref, q_ref, k_ref, v_ref, sums_ref = refs[-6:]
    rows = tokens_ref[...].astype(F32)
    inverse = lax.rsqrt(jnp.mean(rows * rows, axis=1, keepdims=True) + EPS)
    low = (rows * inverse * gain_ref[...]).astype(BF)
    low_ref[...] = low
    inverse_ref[...] = inverse
    sums = []
    for w_ref, out_ref in ((wq_ref, q_ref), (wk_ref, k_ref)):
        raw = mul(low, w_ref[...])
        out_ref[...] = raw
        sums.append(jnp.sum(raw * raw, axis=1, keepdims=True))
    v_ref[...] = mul(low, wv_ref[...]).astype(BF)
    sums_ref[...] = jnp.concatenate(sums, axis=1)


def front_call(tokens, gain, w_query, w_key, w_value, waits):
    rows, width = tokens.shape
    local = w_query.shape[1]
    tile = min(HIDDEN_TILE, rows)
    row = lambda c: pl.BlockSpec((tile, c), lambda i: (i, 0))
    shape = jax.ShapeDtypeStruct
    return pl.pallas_call(
        front_kernel,
        grid=(rows // tile,),
        in_specs=[row(width), whole((1, width))] + [whole(w_query.shape)] * 3 + [ANYWHERE] * len(waits),
        out_specs=[row(width), row(1)] + [row(local)] * 3 + [row(2)],
        out_shape=[shape((rows, width), BF), shape((rows, 1), F32)]
        + [shape((rows, local), F32)] * 2
        + [shape((rows, local), BF), shape((rows, 2), F32)],
        compiler_params=kernel_params(),
        cost_estimate=pl.CostEstimate(
            flops=6 * rows * width * local, bytes_accessed=4 * rows * width + 6 * width * local, transcendentals=0
        ),
        name="front_rows",
    )(tokens, gain, w_query, w_key, w_value, *waits)


def attention_kernel(
    q_ref, k_ref, v_ref, qi_ref, ki_ref, qg_ref, kg_ref, cos_ref, sin_ref, row_ref, col_ref,
    qh_ref, kh_ref, ctx_ref, lse_ref, bias,
):
    rows, size = q_ref.shape
    tile = min(QUERY_TILE, rows)
    fill_bias(bias, row_ref, col_ref)
    for raw, inverse, gain, low in ((q_ref, qi_ref, qg_ref, qh_ref), (k_ref, ki_ref, kg_ref, kh_ref)):
        normed = raw[...] * inverse[...] * gain[...]
        turned = normed * cos_ref[...] + pltpu.roll(normed, size // 2, 1) * sin_ref[...]
        low[...] = turned.astype(BF)
    for start in range(0, rows, tile):
        end = start + tile
        scores = score_block(qh_ref[start:end], kh_ref[:end], bias[start:end, :end])
        top = jnp.max(scores, axis=-1, keepdims=True)
        raised = jnp.exp2(scores - top)
        total = jnp.sum(raised, axis=-1, keepdims=True)
        weights = (raised * (1.0 / total)).astype(BF)
        ctx_ref[start:end] = mul(weights, v_ref[:end]).astype(BF)
        lse_ref[0, start:end] = top + jnp.log2(total)


def attention_back_kernel(
    q_ref, k_ref, v_ref, qi_ref, ki_ref, qg_ref, kg_ref, cos_ref, sin_ref, row_ref, col_ref,
    qh_ref, kh_ref, ctx_ref, lse_ref, dctx_ref, *rest,
):
    dq_ref, dk_ref, dv_ref, inner_ref, dqg_ref, dkg_ref, dq_total, dk_total, dv_total, bias = rest[-10:]
    rows, size = q_ref.shape
    scale = size**-0.5
    tile = min(BACK_TILE, rows)
    fill_bias(bias, row_ref, col_ref)
    dk_total[...] = jnp.zeros_like(dk_total)
    dv_total[...] = jnp.zeros_like(dv_total)
    inner = jnp.sum(dctx_ref[...].astype(F32) * ctx_ref[...].astype(F32), axis=1, keepdims=True)
    for start in range(0, rows, tile):
        end = start + tile
        keys = kh_ref[:end]
        scores = score_block(qh_ref[start:end], keys, bias[start:end, :end])
        weights = jnp.exp2(scores - lse_ref[0, start:end])
        grad_weights = mul(dctx_ref[start:end], v_ref[:end], NT)
        grad_scores = (weights * (grad_weights - inner[start:end])).astype(BF)
        dq_total[start:end] = mul(grad_scores, keys) * scale
        dk_total[:end] += mul(grad_scores, qh_ref[start:end], TN) * scale
        dv_total[:end] += mul(weights.astype(BF), dctx_ref[start:end], TN)
    dv_ref[...] = dv_total[...].astype(BF)
    inners = []
    for total, raw, inverse, gain, out, dgain in (
        (dq_total, q_ref, qi_ref, qg_ref, dq_ref, dqg_ref),
        (dk_total, k_ref, ki_ref, kg_ref, dk_ref, dkg_ref),
    ):
        grad = total[...]
        grad = grad * cos_ref[...] - pltpu.roll(grad, size // 2, 1) * sin_ref[...]
        values = raw[...]
        dgain[...] = jnp.sum(grad * values * inverse[...], axis=0, keepdims=True)
        scaled = grad * gain[...]
        inners.append(jnp.sum(values * scaled, axis=1, keepdims=True))
        out[...] = scaled
    inner_ref[0] = jnp.concatenate(inners, axis=1)


def head_specs(rows):
    head = pl.BlockSpec((rows, HEAD_DIM), lambda h: (0, h))
    gain = pl.BlockSpec((1, HEAD_DIM), lambda h: (0, h))
    column = whole((rows, 1))
    table = whole((rows, HEAD_DIM))
    own_column = pl.BlockSpec((1, rows, 1), lambda h: (h, 0, 0))
    specs = [head, head, head, column, column, gain, gain, table, table, column, whole((1, rows))]
    return head, gain, own_column, specs


def attention_call(operands, rows, local):
    head, gain, own_column, specs = head_specs(rows)
    heads = local // HEAD_DIM
    return pl.pallas_call(
        attention_kernel,
        grid=(heads,),
        in_specs=specs,
        out_specs=[head] * 3 + [own_column],
        out_shape=[jax.ShapeDtypeStruct((rows, local), BF)] * 3 + [jax.ShapeDtypeStruct((heads, rows, 1), F32)],
        scratch_shapes=[pltpu.VMEM((rows, rows), F32)],
        compiler_params=kernel_params(),
        cost_estimate=pl.CostEstimate(
            flops=2 * rows * rows * local, bytes_accessed=12 * rows * local, transcendentals=rows * rows * heads // 2
        ),
        name="attention_rows",
    )(*operands)


def attention_back_call(operands, rows, local, waits=()):
    head, gain, own_column, specs = head_specs(rows)
    heads = local // HEAD_DIM
    return pl.pallas_call(
        attention_back_kernel,
        grid=(heads,),
        in_specs=specs + [head] * 3 + [own_column, head] + [ANYWHERE] * len(waits),
        out_specs=[head] * 3 + [pl.BlockSpec((1, rows, 2), lambda h: (h, 0, 0)), gain, gain],
        out_shape=[jax.ShapeDtypeStruct((rows, local), F32)] * 2
        + [jax.ShapeDtypeStruct((rows, local), BF), jax.ShapeDtypeStruct((heads, rows, 2), F32)]
        + [jax.ShapeDtypeStruct((1, local), F32)] * 2,
        scratch_shapes=[pltpu.VMEM((rows, HEAD_DIM), F32)] * 3 + [pltpu.VMEM((rows, rows), F32)],
        compiler_params=kernel_params(),
        cost_estimate=pl.CostEstimate(
            flops=8 * rows * rows * local, bytes_accessed=24 * rows * local, transcendentals=rows * rows * heads // 2
        ),
        name="attention_rows_back",
    )(*operands, *waits)


def hidden_kernel(pieces, core_ref, tokens_ref, gain_ref, *refs):
    ctx_refs, w_refs = refs[:pieces], refs[pieces : pieces + 3]
    hidden_ref, low_ref, inverse_ref, heads = refs[pieces + 3 :]
    local = ctx_refs[0].shape[1]
    half = local // 2
    near = pl.ds(pl.multiple_of(core_ref[0] * half, half), half)
    far = pl.ds(pl.multiple_of((1 - core_ref[0]) * half, half), half)
    heads[:, :local] = ctx_refs[0][...]
    for number in range(1, pieces):
        mine = local + (number - 1) * half
        other = mine + (pieces - 1) * half
        heads[:, mine : mine + half] = ctx_refs[number][:, near]
        heads[:, other : other + half] = ctx_refs[number][:, far]
    total = tokens_ref[...].astype(F32)
    begin = 0
    for w_ref in w_refs:
        end = begin + w_ref.shape[0]
        total = total + mul(heads[:, begin:end], w_ref[...])
        begin = end
    inverse = lax.rsqrt(jnp.mean(total * total, axis=1, keepdims=True) + EPS)
    low_ref[...] = (total * inverse * gain_ref[...]).astype(BF)

    @pl.when(pl.program_id(0) == core_ref[1])
    def _():
        hidden_ref[...] = total
        inverse_ref[...] = inverse


def hidden_call(places, tokens, gain, context, weights):
    rows, width = tokens.shape
    tile = rows // len(context)
    row = lambda c: pl.BlockSpec((tile, c), lambda i: (i, 0))
    return pl.pallas_call(
        functools.partial(hidden_kernel, len(context)),
        grid=(rows // tile,),
        in_specs=[pl.BlockSpec(memory_space=pltpu.SMEM), row(width), whole((1, width))]
        + [row(context[0].shape[1])] * len(context)
        + [whole(array.shape) for array in weights],
        out_specs=[whole((tile, width)), row(width), whole((tile, 1))],
        out_shape=[
            jax.ShapeDtypeStruct((tile, width), F32),
            jax.ShapeDtypeStruct((rows, width), BF),
            jax.ShapeDtypeStruct((tile, 1), F32),
        ],
        scratch_shapes=[pltpu.VMEM((tile, width), BF)],
        compiler_params=kernel_params(),
        cost_estimate=pl.CostEstimate(
            flops=2 * rows * width * width, bytes_accessed=10 * rows * width + 2 * width * width, transcendentals=0
        ),
        name="hidden_rows",
    )(places, tokens, gain, *context, *weights)


def rows_kernel(place, number_here, each_device, added, waits, *refs):
    core_ref, router_ref = refs[:2]
    x_refs, dy_refs, carried_refs, w_ref = refs[2:4], refs[4:6], refs[6:8], refs[8]
    rest = refs[9:]
    if added:
        before, rest = rest[:4], rest[4:]
    rest = rest[waits:]
    moe_refs, dx_refs, kept_ref, share_ref = rest[:2], rest[2:4], rest[4], rest[5]
    x, dy, down, both_w, kept, moe, dx, gates, dots, in_sems, w_sems, before_sems, out_sems = rest[6:]
    blocks, _, own, width = x_refs[0].shape
    rows = blocks * own
    total = 2 * rows
    experts = w_ref.shape[0]
    hid = w_ref.shape[1] // 3

    def fetch_rows(refs, held, first):
        copies = []
        for side in range(2):
            for block in range(blocks):
                to = held.at[pl.ds(side * rows + block * own, own)]
                copies.append(pltpu.make_async_copy(refs[side].at[block, place], to, in_sems.at[first + side * blocks + block]))
        return copies

    x_copies = fetch_rows(x_refs, x, 0)
    dy_copies = fetch_rows(dy_refs, dy, 2 * blocks)
    w_copies = [
        (
            pltpu.make_async_copy(w_ref.at[e, pl.ds(hid, 2 * hid)], both_w.at[pl.ds(2 * e * hid, 2 * hid)], w_sems.at[2 * e]),
            pltpu.make_async_copy(w_ref.at[e, pl.ds(0, hid)], down.at[pl.ds(e * hid, hid)], w_sems.at[2 * e + 1]),
        )
        for e in range(experts)
    ]
    for copy in x_copies + [w_copies[0][0]] + dy_copies + [w_copies[0][1]]:
        copy.start()
    for pair in w_copies[1:]:
        for copy in pair:
            copy.start()
    earlier = []
    if added:
        for side in range(2):
            here = pl.ds(side * rows, rows)
            earlier.append(pltpu.make_async_copy(before[side], moe.at[here], before_sems.at[side]))
            earlier.append(pltpu.make_async_copy(before[2 + side], dx.at[here], before_sems.at[2 + side]))
    for copy in earlier:
        copy.start()
    for copy in x_copies:
        copy.wait()
    for side in range(2):
        here = slice(side * rows, (side + 1) * rows)
        logits = mul(x[here], router_ref[...])
        raised = jnp.exp(logits - jnp.max(logits, axis=1, keepdims=True))
        shares = raised / jnp.sum(raised, axis=1, keepdims=True)
        if side == 0:
            share_ref[...] = shares
        gates[here] = shares * carried_refs[side][:, 0].reshape(rows, -1).astype(F32)
    dots[...] = jnp.zeros_like(dots)
    w_copies[0][0].wait()
    for copy in dy_copies:
        copy.wait()
    out_copies = []
    for e in range(experts):
        if e:
            w_copies[e][0].wait()
        w_copies[e][1].wait()
        index = (e * 2 + core_ref[0]) * each_device + number_here
        gh = slice(e * hid, (e + 1) * hid)
        wide = experts * hid + 2 * e * hid
        for first in range(0, total, ROW_TILE):
            here = slice(first, first + ROW_TILE)
            both = mul(x[here], both_w[2 * e * hid : 2 * (e + 1) * hid], NT)
            back = mul(dy[here], down[gh], NT)
            pre, up = both[:, :hid], both[:, hid:]
            sigma = 0.5 * jnp.tanh(0.5 * pre) + 0.5
            active = pre * sigma
            chosen = lax.broadcasted_iota(jnp.int32, (ROW_TILE, gates.shape[1]), 1) == index
            gate = jnp.sum(jnp.where(chosen, gates[here], 0.0), axis=1, keepdims=True)
            column = lax.broadcasted_iota(jnp.int32, (ROW_TILE, LANES), 1) == index
            hidden = active * up
            dots[here] += jnp.where(column, jnp.sum(hidden * back, axis=1, keepdims=True), 0.0)
            back = back * gate
            kept[here, gh] = (hidden * gate).astype(BF)
            kept[here, wide : wide + hid] = (back * up * sigma * (1.0 + pre * (1.0 - sigma))).astype(BF)
            kept[here, wide + hid : wide + 2 * hid] = (back * active).astype(BF)
    copy = pltpu.make_async_copy(kept, kept_ref, out_sems.at[0])
    copy.start()
    out_copies.append(copy)
    for copy in earlier:
        copy.wait()
    for number, first in enumerate(range(0, width, COLUMN_TILE)):
        here = slice(first, first + COLUMN_TILE)
        for what, (held, w_held, begin, end) in enumerate((
            (moe, down, 0, experts * hid), (dx, both_w, experts * hid, 3 * experts * hid)
        )):
            value = mul(kept[:, begin:end], w_held[:, here])
            if added:
                value = value + held[:, here].astype(F32)
            held[:, here] = value.astype(BF)
            for side in range(2):
                ref = (moe_refs, dx_refs)[what][side]
                copy = pltpu.make_async_copy(
                    held.at[pl.ds(side * rows, rows), pl.ds(first, COLUMN_TILE)],
                    ref.at[:, pl.ds(first, COLUMN_TILE)], out_sems.at[1 + 4 * number + 2 * what + side])
                copy.start()
                out_copies.append(copy)
    value = dots[...]
    if added:
        value = value + dx[:, width:].astype(F32)
    dx[:, width:] = value.astype(BF)
    last = 1 + 4 * (width // COLUMN_TILE)
    for side in range(2):
        copy = pltpu.make_async_copy(
            dx.at[pl.ds(side * rows, rows), pl.ds(width, LANES)], dx_refs[side].at[:, pl.ds(width, LANES)],
            out_sems.at[last + side])
        copy.start()
        out_copies.append(copy)
    for copy in out_copies:
        copy.wait()

def rows_call(core, router, moe_in, cotangent, carried, place, weights, number_here, each_device, before=None, waits=()):
    blocks, _, own, width = moe_in[0].shape
    rows = blocks * own
    experts, depth, _ = weights.shape
    number = router.shape[1]
    total = 2 * rows
    small = pl.BlockSpec((blocks, 1, own, number), lambda i: (0, place, 0, 0), pipeline_mode=pl.Buffered(1))
    operands = [core, router, *moe_in, *cotangent, *carried, weights]
    specs = [pl.BlockSpec(memory_space=pltpu.SMEM), whole(router.shape)] + [ANYWHERE] * 4 + [small] * 2 + [ANYWHERE]
    if before is not None:
        operands += before
        specs += [ANYWHERE] * 4
    operands += waits
    specs += [ANYWHERE] * len(waits)
    return pl.pallas_call(
        functools.partial(rows_kernel, place, number_here, each_device, before is not None, len(waits)),
        grid=(1,),
        in_specs=specs,
        out_specs=[ANYWHERE] * 5 + [whole((rows, number))],
        out_shape=[jax.ShapeDtypeStruct((rows, width), BF)] * 2
        + [jax.ShapeDtypeStruct((rows, width + LANES), BF)] * 2
        + [jax.ShapeDtypeStruct((total, experts * depth), BF), jax.ShapeDtypeStruct((rows, number), F32)],
        scratch_shapes=[
            pltpu.VMEM((total, width), BF), pltpu.VMEM((total, width), BF),
            pltpu.VMEM((experts * depth // 3, width), BF), pltpu.VMEM((2 * experts * depth // 3, width), BF),
            pltpu.VMEM((total, experts * depth), BF), pltpu.VMEM((total, width), BF), pltpu.VMEM((total, width + LANES), BF),
            pltpu.VMEM((total, number), F32), pltpu.VMEM((total, LANES), F32),
            pltpu.SemaphoreType.DMA((4 * blocks,)), pltpu.SemaphoreType.DMA((2 * experts,)), pltpu.SemaphoreType.DMA((4,)),
            pltpu.SemaphoreType.DMA((3 + 4 * (width // COLUMN_TILE),)),
        ],
        compiler_params=kernel_params(),
        cost_estimate=pl.CostEstimate(
            flops=4 * total * width * experts * depth, bytes_accessed=8 * total * width, transcendentals=0
        ),
        name="expert_rows",
    )(*operands)


def weight_grads_kernel(sides, halves, outs, added, skipped, order_ref, *refs):
    parts = sides * halves
    x_refs, dy_refs = refs[:parts], refs[parts : 2 * parts]
    kept_refs = refs[2 * parts : 2 * parts + 4 * halves]
    add_refs = refs[2 * parts + 4 * halves : 2 * parts + 4 * halves + added]
    out_refs, turned = refs[2 * parts + 4 * halves + added + skipped : -1], refs[-1]
    hid = turned.shape[0] // 6
    span = kept_refs[0].shape[0]
    rows = span // sides

    @pl.when(pl.program_id(0) == 0)
    def _():
        for h in range(halves):
            there = slice(h * span, (h + 1) * span)
            for one in range(2):
                units, grads = kept_refs[4 * h + 2 * one : 4 * h + 2 * one + 2]
                turned[one * hid : (one + 1) * hid, there] = units[...].T
                place = 2 * hid + one * 2 * hid
                turned[place : place + 2 * hid, there] = grads[...].T

    def total(first, last, refs):
        return sum(
            mul(turned[first:last, p * rows : (p + 1) * rows], ref[:, 0].reshape(rows, ref.shape[-1]))
            for p, ref in enumerate(refs)
        )

    down = total(0, 2 * hid, dy_refs)
    both = total(2 * hid, 6 * hid, x_refs)
    for one in range(2):
        value = jnp.concatenate(
            [down[one * hid : (one + 1) * hid], both[one * 2 * hid : (one + 1) * 2 * hid]], axis=0
        )
        if outs == 1:
            out_refs[0][one] = value.astype(BF)
            continue
        middle = value.shape[0] // 2
        for number, part in enumerate((value[:middle], value[middle:])):
            if added and number == one:
                part = part + add_refs[one][...].astype(F32)
            out_refs[2 * one + number][...] = part.astype(BF)


def weight_grads_call(moe_in, cotangent, kept, order, depth, addends=(), waits=(), pair=None, into=None):
    blocks, halves, own, width = moe_in[0].shape
    sides = len(moe_in)
    tile = COLUMN_TILE
    span = kept[0].shape[0]
    parts = [(h, side) for h in range(halves) for side in range(sides)]

    def column(h):
        return pl.BlockSpec((blocks, 1, own, tile), lambda i, order: (0, h, 0, i))

    hid = depth // 3
    experts = kept[0].shape[1] // depth

    def expert(one):
        return [
            pl.BlockSpec((span, hid), lambda i, order: (0, order[one]), pipeline_mode=pl.Buffered(1)),
            pl.BlockSpec((span, 2 * hid), lambda i, order: (0, experts // 2 + order[one]), pipeline_mode=pl.Buffered(1)),
        ]

    operands = [moe_in[side] for _, side in parts] + [cotangent[side] for _, side in parts]
    operands += [kept[h] for h in range(halves) for _ in range(4)]
    specs = [column(h) for h, _ in parts] * 2 + [spec for _ in range(halves) for one in range(2) for spec in expert(one)]
    operands += addends
    specs += [pl.BlockSpec((addend.shape[0], tile), lambda i, order: (0, i)) for addend in addends]
    aliases = {}
    if into is not None:
        waits = [into, *waits]
        aliases = {1 + len(operands): 0}
    if pair is None:
        outs = 4
        out_specs = [pl.BlockSpec((depth // 2, tile), lambda i, order: (0, i))] * 4
        out_shape = [jax.ShapeDtypeStruct((depth // 2, width), BF)] * 4
    else:
        outs = 1
        out_specs = pl.BlockSpec((2, depth, tile), lambda i, order: (pair, 0, i))
        out_shape = jax.ShapeDtypeStruct((kept[0].shape[1] // depth, depth, width), BF)
    return pl.pallas_call(
        functools.partial(weight_grads_kernel, sides, halves, outs, len(addends), len(waits)),
        grid_spec=pltpu.PrefetchScalarGridSpec(
            num_scalar_prefetch=1,
            grid=(width // tile,),
            in_specs=specs + [ANYWHERE] * len(waits),
            out_specs=out_specs,
            scratch_shapes=[pltpu.VMEM((2 * depth, halves * span), BF)],
        ),
        out_shape=out_shape,
        input_output_aliases=aliases,
        compiler_params=kernel_params(),
        cost_estimate=pl.CostEstimate(
            flops=4 * halves * span * width * depth,
            bytes_accessed=4 * halves * span * width + 8 * depth * width,
            transcendentals=0,
        ),
        name="expert_weight_grads",
    )(order, *operands, *waits)


def swap(values, bit):
    size = lax.axis_size(EXPERT)
    return lax.ppermute(values, EXPERT, [(i, i ^ bit) for i in range(size)])


def plus(left, right):
    return (left.astype(F32) + right.astype(F32)).astype(BF)


def relative_columns(values):
    here = lax.axis_index(EXPERT)
    size = lax.axis_size(EXPERT)
    span = values.shape[1] // size
    order = [*range(0, size, 2), *range(1, size, 2)]
    return jnp.concatenate(
        [lax.dynamic_slice_in_dim(values, (here ^ r) * span, span, 1) for r in order], axis=1
    )


def block_terms(values):
    rows = values.shape[0] // 4
    mine, to_two, to_four, across = (values[n * rows : (n + 1) * rows] for n in range(4))
    return (across[: rows // 2], across[rows // 2 :]), to_four, to_two, mine


def beside(terms, via):
    _, to_four, to_two, _ = terms
    middle = to_four.shape[0] // 2
    return (
        jnp.concatenate([plus(to_four[:middle], via[0]), to_four[middle:]], axis=0),
        jnp.concatenate([to_two[:middle], plus(to_two[middle:], via[1])], axis=0),
    )


def join(*values):
    return lax.optimization_barrier(values)


def scatter_tensor(values):
    return lax.psum_scatter(values, TENSOR, scatter_dimension=0, tiled=True)


HALVES = 2


def shards_near(
    tokens, cotangent, seq_lengths, expert_ids, slot_index, w_query, w_key, w_value, w_output,
    query_gain, key_gain, attn_gain, moe_gain, router, w_gate, w_up, w_down,
):
    rows, width = tokens.shape
    local = w_query.shape[1]
    groups = lax.axis_size(EXPERT)
    n_tensor = lax.axis_size(TENSOR)
    here = lax.axis_index(EXPERT)
    layer = lax.axis_index(TENSOR)
    experts_here, hid = w_gate.shape[0], w_gate.shape[2]
    experts_all = experts_here * groups
    own_rows = rows // n_tensor
    own = lambda array: lax.dynamic_slice_in_dim(array, layer * own_rows, own_rows, 0)
    view = lambda array: array.reshape(n_tensor, HALVES, own_rows // HALVES, array.shape[-1])
    half = range(HALVES)

    chips = groups // 2
    sides_of = [[2 * chip + core for chip in range(chips)] for core in (0, 1)]
    core = lax.rem(here, 2)

    core_rows = local // 2
    w_half = lax.dynamic_slice_in_dim(w_output, core * core_rows, core_rows, 0)
    w_mine = [swap_tensor(w_half, bits) for bits in (1, 2)]

    def pack(gate, up, down):
        return jnp.concatenate([down, gate.T, up.T], axis=0)

    def spread(value):
        return lax.all_gather(value, EXPERT, axis_index_groups=sides_of)

    depth = 3 * hid
    packed = [pack(w_gate[j], w_up[j], w_down[j]) for j in range(experts_here)]
    weights = [spread(packed[0])]
    number = jnp.arange(experts_all, dtype=jnp.int32)
    carried = (expert_ids[:, :, None] == number) & (slot_index >= 0)[:, :, None]
    carried = jnp.sum(carried.astype(BF), axis=1)
    segment, position = layout(seq_lengths, rows)
    cosine, sine = rope_angles(position, HEAD_DIM)
    cos_table = jnp.concatenate([cosine, cosine], axis=1)
    sin_table = jnp.concatenate([-sine, sine], axis=1)
    attn_in, inverse_in, query_raw, key_raw, values, totals = front_call(
        tokens, attn_gain[None], w_query, w_key, w_value, [*packed, cos_table, sin_table]
    )
    total = sum_small(totals.T.reshape(-1, LANES)).reshape(2, rows)
    total, w_mine[0], w_mine[1] = join(total, *w_mine)
    w_mine.append(swap_tensor(w_mine[1], 1))
    query_inverse = lax.rsqrt(total[0] / width + EPS)[:, None]
    key_inverse = lax.rsqrt(total[1] / width + EPS)[:, None]
    operands = [
        query_raw, key_raw, values, query_inverse, key_inverse, query_gain[None], key_gain[None],
        cos_table, sin_table, segment[:, None], segment[None],
    ]
    queries, keys, context, lse = attention_call(operands, rows, local)
    context_here = context
    far_context = swap_tensor(context, 2)
    near_context = swap_tensor(context, 1)
    w_mine[2], context = join(w_mine[2], context)
    near_context, far_context, *w_mine = join(near_context, far_context, *w_mine)
    contexts = [context, near_context, far_context, swap_tensor(far_context, 1)]
    w_mine = jnp.concatenate(w_mine, axis=0)
    w_other, packed[1], contexts[3] = join(swap(w_mine, 1), packed[1], contexts[3])
    w_all = [w_output, w_mine, w_other]
    weights.append(spread(packed[1]))
    carried_later, cotangent_later, contexts[0] = lax.optimization_barrier((carried, cotangent, contexts[0]))
    carried_sides = [view(carried), view(swap(carried_later, 1))]
    cotangent_sides = [view(cotangent), view(swap(cotangent_later, 1))]
    hidden_own, moe_low, inverse_own = hidden_call(
        jnp.stack([core, layer]).astype(jnp.int32), tokens, moe_gain[None], contexts, w_all
    )
    sides = [view(moe_low), view(swap(moe_low, 1))]
    router_wide = router.astype(F32)
    calls, kept, shares = [None, None], [{}, {}], [None, None]

    def run(h, j, *waits):
        before = None if calls[h] is None else calls[h][:4]
        calls[h] = rows_call(
            core[None], router, sides, cotangent_sides, carried_sides, h, weights[j], j, experts_here, before, waits
        )
        kept[h][j] = calls[h][4]
        shares[h] = calls[h][5]

    def send_back(h):
        terms = plus(calls[h][2], swap(calls[h][3], 1))
        return terms, scatter_tensor(terms)

    chip = here // 2

    def part(j, first, second, *rest, **more):
        order = jnp.stack([first, second]).astype(jnp.int32)
        return weight_grads_call(
            sides, cotangent_sides, [kept[h][j] for h in half], order, depth, *rest, **more
        )

    def send(terms, bits):
        return [swap(term, bit) for term, bit in zip(terms, bits)]

    run(0, 0)
    run(1, 0, calls[0][4])
    *far, mine_low, mine_high = part(0, chip ^ 3, chip)
    via = send(far, (2, 4))
    run(0, 1, *far)
    *calls[0], via[0], via[1] = join(*calls[0], *via)
    kept[0][1] = calls[0][4]
    terms, sums_first = send_back(0)
    run(1, 1, terms)
    *calls[1], sums_first = join(*calls[1], sums_first)
    kept[1][1] = calls[1][4]
    terms, sums_second = send_back(1)
    near = part(0, chip ^ 2, chip ^ 1, via, [terms])
    near_low = send(near[::2], (4, 2))
    second = part(1, 0 * chip, 0 * chip + 1, (), [near[0]], pair=0)
    sums_second, second, attn_in, *moe_terms = join(sums_second, second, attn_in, *calls[0][:2], *calls[1][:2])
    moe_terms = [plus(moe_terms[2 * h], swap(moe_terms[2 * h + 1], 1)) for h in half]
    moe_terms = jnp.stack([term.reshape(n_tensor, -1, width) for term in moe_terms], axis=1).reshape(rows, width)
    sums = jnp.concatenate([sums_first, sums_second], axis=0)
    dshares = sums[:, width : width + experts_all].astype(F32) * own(carried).astype(F32)
    share = jnp.concatenate(
        [lax.dynamic_slice_in_dim(item, layer * (own_rows // HALVES), own_rows // HALVES, 0) for item in shares], axis=0
    )
    moe_in = hidden_own * inverse_own * moe_gain
    dlogits = share * (dshares - jnp.sum(share * dshares, axis=-1, keepdims=True))
    router_back = jnp.einsum("te,de->td", dlogits, router_wide, precision=lax.Precision.HIGHEST)
    grad_norm_moe, grad_moe_gain = norm_back(
        hidden_own, inverse_own, moe_gain, sums[:, :width].astype(F32) + router_back
    )
    grad_hidden = own(cotangent).astype(F32) + grad_norm_moe
    grad_low = grad_hidden.astype(BF)

    by_head, by_mine, by_other = (mul(grad_low, weight, NT).astype(BF) for weight in w_all)
    core_columns = local // 2
    grad_context = jnp.zeros((rows, local), BF)
    for bits in range(n_tensor):
        if bits == 0:
            came = by_head
        else:
            columns = slice((bits - 1) * core_columns, bits * core_columns)
            mine, other = by_mine[:, columns], by_other[:, columns]
            lower = jnp.where(core == 0, mine, other)
            upper = jnp.where(core == 0, other, mine)
            came = swap_tensor(jnp.concatenate([lower, upper], axis=1), bits)
        grad_context = lax.dynamic_update_slice_in_dim(grad_context, came, (layer ^ bits) * own_rows, 0)
    heads_own = jnp.concatenate([own(item) for item in contexts], axis=1)
    output_grads = mul(relative_columns(grad_low), heads_own, TN).astype(BF)
    output_grads = [output_grads[: width // 2], output_grads[width // 2 :]]
    attn_relative = relative_columns(attn_in)
    router_part = jnp.einsum("td,te->de", moe_in, dlogits, precision=lax.Precision.HIGHEST)
    grad_context, moe_terms, attn_relative, router_part, *output_grads = join(
        grad_context, moe_terms, attn_relative, router_part, *output_grads
    )
    moe = scatter_tensor(moe_terms)
    came = swap(output_grads[1], 1)
    back = attention_back_call(
        operands + [queries, keys, context_here, lse, grad_context], rows, local, [output_grads[1]]
    )
    *back, came, near_low[0], near_low[1] = join(*back, came, *near_low)
    near_high = send(near[1::2], (4, 2))
    dq, dk, value_low, inner, grad_query_gain, grad_key_gain = back
    inner = jnp.sum(inner, axis=0).T
    inner = sum_small(inner.reshape(-1, LANES)).reshape(inner.shape)
    output_grads = block_terms(plus(output_grads[0], came))
    second = part(1, 0 * chip + 2, 0 * chip + 3, (), [inner], pair=1, into=second)
    across = output_grads[0]
    inner, moe, second, near_high[0], near_high[1], *across = join(inner, moe, second, *near_high, *across)
    output_via = send(across, (2, 4))
    grads_one = lax.psum_scatter(
        second.reshape(-1, width), EXPERT, scatter_dimension=0, axis_index_groups=sides_of, tiled=True
    )
    out_own = (hidden_own + moe.astype(F32)).astype(BF)
    came = exchange(out_own, out_own)

    def raw_grad(scaled, raw, inverse, total):
        return (inverse * scaled - raw * inverse * inverse * inverse * (total / width)[:, None]).astype(BF)

    query_low = raw_grad(dq, query_raw, query_inverse, inner[0])
    key_low = raw_grad(dk, key_raw, key_inverse, inner[1])
    lows = jnp.concatenate([query_low, key_low, value_low], axis=1)
    wide = jnp.concatenate([w_query, w_key, w_value], axis=1)
    terms_in = mul(lows, wide, NT).astype(BF)
    def expert_outputs(grads):
        return grads[hid : 2 * hid].T, grads[2 * hid :].T, grads[:hid]

    outputs_zero = jnp.concatenate([
        (mine.astype(F32) + near[0].astype(F32) + near[1].astype(F32)).astype(BF)
        for mine, near in ((mine_low, near_low), (mine_high, near_high))], axis=0)
    outputs_zero = list(expert_outputs(outputs_zero))
    grad_attn_gain = jnp.sum(terms_in.astype(F32) * tokens.astype(F32) * inverse_in, axis=0)
    *came, terms_in, lows, grad_attn_gain, output_via[0], output_via[1] = join(
        *came, terms_in, lows, grad_attn_gain, *output_via
    )
    output_near = send(beside(output_grads, output_via), (4, 2))
    out_above, out_below = [from_above(came)], [from_below(came)]
    chunk = lambda place: lax.dynamic_slice_in_dim(terms_in, jnp.clip(place, 0, n_tensor - 1) * own_rows, own_rows, 0)
    sum_above = sum_below = jnp.zeros((), BF)
    for step in range(1, n_tensor):
        came = exchange(
            jnp.where(
                layer >= n_tensor - step, plus(chunk(layer - n_tensor + step), sum_above), out_above[-1]
            ),
            jnp.where(layer < step, plus(chunk(layer + n_tensor - step), sum_below), out_below[-1]),
        )
        if step == 1:
            own_width, span = width // groups, local // groups
            spread_gain = lambda gain: jnp.pad(
                gain.reshape(groups, span), ((0, 0), (0, own_width - span))
            ).reshape(width, 1)
            small = jnp.concatenate([
                router_part, grad_moe_gain[:, None], grad_attn_gain[:, None],
                spread_gain(grad_query_gain), spread_gain(grad_key_gain)], axis=1).astype(BF)
            small = jnp.pad(small, ((0, 0), (0, LANES - small.shape[1])))
            blocks = jnp.concatenate([
                mul(attn_relative, lows, TN).astype(BF), relative_columns(small.T).T], axis=1)
            blocks = [blocks[: width // 2], blocks[width // 2 :]]
            *came, blocks[0], blocks[1] = join(*came, *blocks)
            blocks_came = swap(blocks[1], 1)
        elif step == 2:
            came[0], came[1], blocks_came, *outputs_zero = join(*came, blocks_came, *outputs_zero)
            blocks = block_terms(plus(blocks[0], blocks_came))
            via = send(blocks[0], (2, 4))
        else:
            *came, via[0], via[1] = join(*came, *via)
        above, below = from_above(came), from_below(came)
        sum_above = jnp.where(layer == n_tensor - 1, 0, above)
        sum_below = jnp.where(layer == 0, 0, below)
        if step < n_tensor - 1:
            out_above.append(above)
            out_below.append(below)
    grad_normed = own(terms_in).astype(F32) + sum_above.astype(F32) + sum_below.astype(F32)
    out = end_line(out_own, out_above, out_below)

    grad_norm_in, _ = norm_back(own(tokens).astype(F32), own(inverse_in), attn_gain, grad_normed)
    grad_input = (grad_hidden + grad_norm_in).astype(BF)
    input_above, input_below = [grad_input], [grad_input]
    for step in range(1, n_tensor):
        came = exchange(input_above[-1], input_below[-1])
        if step == 1:
            near = send(beside(blocks, via), (4, 2))
            *came, output_near[0], output_near[1] = join(*came, *output_near)
        if step == 2:
            *came, near[0], near[1], grads_one = join(*came, *near, grads_one)
        input_above.append(from_above(came))
        input_below.append(from_below(came))
    projections = sum((item.astype(F32) for item in near), blocks[3].astype(F32))
    small = projections[:, 3 * local :]
    projections = projections[:, : 3 * local].astype(BF)
    by_index = sum((item.astype(F32) for item in output_near), output_grads[3].astype(F32))
    grad_w_output, shared = by_index[:, :local], small
    for bits in range(1, n_tensor):
        terms = jnp.concatenate([by_index[:, bits * local : (bits + 1) * local], small], axis=1)
        came = swap_tensor(terms.astype(BF), bits).astype(F32)
        grad_w_output, shared = grad_w_output + came[:, :local], shared + came[:, local:]
    grad_w_output = grad_w_output.T
    grad_input = end_line(grad_input, input_above[1:], input_below[1:])

    gains = small[:span, experts_all + 2 : experts_all + 4].astype(BF)
    return (
        out, grad_input,
        projections[:, :local], projections[:, local : 2 * local], projections[:, 2 * local : 3 * local],
        grad_w_output.astype(BF),
        gains[:, 0], gains[:, 1], shared[:, experts_all + 1].astype(BF), shared[:, experts_all].astype(BF),
        shared[:, :experts_all].astype(BF),
        *(jnp.stack(pair) for pair in zip(outputs_zero, expert_outputs(grads_one))),
    )


def swap_tensor(values, bit):
    size = lax.axis_size(TENSOR)
    return lax.ppermute(values, TENSOR, [(i, i ^ bit) for i in range(size)])


def scatter_halving(values):
    place = lax.axis_index(TENSOR)
    rows = values.shape[0] // lax.axis_size(TENSOR)
    cut = lambda bits: lax.dynamic_slice_in_dim(values, (place ^ bits) * rows, rows, 0)
    passed = swap_tensor(plus(cut(2), swap_tensor(cut(3), 1)), 2)
    return cut(0).astype(F32) + swap_tensor(cut(1), 1).astype(F32) + passed.astype(F32), passed


def scatter_direct(values):
    place = lax.axis_index(TENSOR)
    size = lax.axis_size(TENSOR)
    rows = values.shape[0] // size
    cut = lambda bits: lax.dynamic_slice_in_dim(values, (place ^ bits) * rows, rows, 0)
    return sum((swap_tensor(cut(bits), bits).astype(F32) for bits in range(1, size)), cut(0).astype(F32))


def exchange(to_below, to_above):
    place = lax.axis_index(TENSOR)
    even = lax.rem(place, 2) == 0
    outer = lax.ppermute(jnp.where(even, to_above, to_below), TENSOR, [(0, 1), (1, 0), (2, 3), (3, 2)])
    inner = lax.ppermute(jnp.where(even, to_below, to_above), TENSOR, [(1, 2), (2, 1), (0, 0), (3, 3)])
    return [outer, inner]


def from_above(came):
    return jnp.where(lax.rem(lax.axis_index(TENSOR), 2) == 0, came[0], came[1])


def from_below(came):
    return jnp.where(lax.rem(lax.axis_index(TENSOR), 2) == 0, came[1], came[0])


def end_line(values, above, below):
    place = lax.axis_index(TENSOR)
    size = lax.axis_size(TENSOR)
    rows = values.shape[0]
    everything = jnp.zeros((rows * size,) + values.shape[1:], values.dtype)
    everything = lax.dynamic_update_slice_in_dim(everything, values, place * rows, 0)
    for ahead in range(1, size):
        whole_line = size - ahead - 1 == size - 2
        after_end = below[0] if whole_line else below[size - ahead - 1]
        before_end = above[0] if ahead == size - 1 else above[ahead - 1]
        piece = jnp.where(place + ahead < size, before_end, after_end)
        everything = lax.dynamic_update_slice_in_dim(everything, piece, lax.rem(place + ahead, size) * rows, 0)
    first, last = place == 0, place == size - 1
    piece = jnp.where(first, above[-1], jnp.where(last, below[-1], values))
    position = jnp.where(first, size - 1, jnp.where(last, 0, place))
    return lax.dynamic_update_slice_in_dim(everything, piece, position * rows, 0)


def exchange_doubling(values):
    far = swap_tensor(values, 2)
    return [swap_tensor(values, 1), far, swap_tensor(far, 1)]


def start_gather(values):
    return [swap_tensor(values, bits) for bits in range(1, lax.axis_size(TENSOR))]


def end_gather(values, came):
    place = lax.axis_index(TENSOR)
    rows = values.shape[0]
    everything = jnp.zeros((rows * (1 + len(came)),) + values.shape[1:], values.dtype)
    for bits, piece in enumerate((values, *came)):
        everything = lax.dynamic_update_slice_in_dim(everything, piece, (place ^ bits) * rows, 0)
    return everything


def gather_doubling(values):
    place = lax.axis_index(TENSOR)
    rows = values.shape[0]
    far = swap_tensor(values, 2)
    pieces = {0: values, 1: swap_tensor(values, 1), 2: far, 3: swap_tensor(far, 1)}
    everything = jnp.zeros((rows * lax.axis_size(TENSOR),) + values.shape[1:], values.dtype)
    for bits, piece in pieces.items():
        everything = lax.dynamic_update_slice_in_dim(everything, piece, (place ^ bits) * rows, 0)
    return everything


def mix_halves(values):
    size = lax.axis_size(TENSOR)
    view = values.reshape(HALVES, size, -1, values.shape[-1])
    return jnp.swapaxes(view, 0, 1).reshape(values.shape)


def unmix_halves(values):
    size = lax.axis_size(TENSOR)
    view = values.reshape(size, HALVES, -1, values.shape[-1])
    return jnp.swapaxes(view, 0, 1).reshape(values.shape)


def rotations():
    size = lax.axis_size(TENSOR)
    return [[(i, (i + d) % size) for i in range(size)] for d in range(1, size)]


def sum_small(values):
    total = values
    for pairs in rotations():
        total = total + lax.ppermute(values, TENSOR, pairs)
    return total


def gather_small(values):
    rows = values.shape[0]
    size = lax.axis_size(TENSOR)
    place = lax.axis_index(TENSOR)
    whole_rows = jnp.zeros((rows * size,) + values.shape[1:], values.dtype)
    whole_rows = lax.dynamic_update_slice_in_dim(whole_rows, values, place * rows, 0)
    for d, pairs in enumerate(rotations(), 1):
        came = lax.ppermute(values, TENSOR, pairs)
        whole_rows = lax.dynamic_update_slice_in_dim(whole_rows, came, lax.rem(place + size - d, size) * rows, 0)
    return whole_rows


def scatter_small(values):
    size = lax.axis_size(TENSOR)
    place = lax.axis_index(TENSOR)
    rows = values.shape[0] // size
    cut = lambda index: lax.dynamic_slice_in_dim(values, index * rows, rows, 0)
    total = cut(place)
    for d, pairs in enumerate(rotations(), 1):
        total = total + lax.ppermute(cut(lax.rem(place + d, size)), TENSOR, pairs)
    return total


NEAR_GROUPS = 8


def solution(mesh):
    placed = (
        P(EXPERT, None),
        P(EXPERT, None),
        P(EXPERT),
        P(EXPERT, None),
        P(EXPERT, None),
        P(None, TENSOR),
        P(None, TENSOR),
        P(None, TENSOR),
        P(TENSOR, None),
        P(TENSOR),
        P(TENSOR),
        P(),
        P(),
        P(),
        P(EXPERT, None, TENSOR),
        P(EXPERT, None, TENSOR),
        P(EXPERT, TENSOR, None),
    )
    return jax.shard_map(
        shards_near if mesh.shape[EXPERT] == NEAR_GROUPS else shards,
        mesh=mesh,
        in_specs=placed,
        out_specs=(
            P(EXPERT, None),
            P(EXPERT, None),
            P(EXPERT, TENSOR),
            P(EXPERT, TENSOR),
            P(EXPERT, TENSOR),
            P(TENSOR, EXPERT),
            P((TENSOR, EXPERT)),
            P((TENSOR, EXPERT)),
            P(EXPERT),
            P(EXPERT),
            P(EXPERT, None),
            P(EXPERT, None, TENSOR),
            P(EXPERT, None, TENSOR),
            P(EXPERT, TENSOR, None),
        ),
        check_vma=False,
    )
```
